512 devices in a mesh: section: 4 (over x_lo, core), seq: 32 (over z, x_hi), tp: 4 (over y).
Axes of the slice: x: 4 (x_hi: 2, x_lo: 2; x = x_hi * 2 + x_lo), y: 4, z: 16, core: 2. Of those that a mesh axis runs over, the one named last changes fastest.
Arguments:
- first_stream: bfloat16 [4, 4096, 4096], P('section', 'seq', 'tp'), may hold values from -6 to 6
- gate_stream: bfloat16 [4, 4096, 4096], P('section', 'seq', 'tp'), may hold values from -6 to 6
- value_stream: bfloat16 [4, 4096, 4096], P('section', 'seq', 'tp'), may hold values from -6 to 6
- short_taps: float32 [4, 3, 3, 4096], P('section', None, None, 'tp'), may hold values from -3 to 3
- long_filter: float32 [4, 4, 32, 32, 4096], P('section', 'tp', 'seq'), may hold values from -2 to 2, as said below
- skip_gain: float32 [4, 4096], P('section', 'tp'), may hold values from -4 to 4
- queries: bfloat16 [4, 4096, 2048], P('section', 'seq', 'tp'), may hold values from -5 to 5
- attn_keys: bfloat16 [4, 4096, 2048], P('section', 'seq', 'tp'), may hold values from -5 to 5
- attn_values: bfloat16 [4, 4096, 2048], P('section', 'seq', 'tp'), may hold values from -6 to 6
- out_weight: bfloat16 [4, 2048, 4, 1024], P('section', 'tp', None, 'seq'), may hold values from -0.125 to 0.125
Outputs:
- handed: bfloat16 [4, 4096, 4096], P('section', 'seq', 'tp')
- attended: bfloat16 [4, 4096, 4096], P('section', 'seq', 'tp')
The draws below stay inside these ranges and needn't reach their ends.
Inputs may be any that keep to these rules, and one draw needn't show every extreme that they name: `long_filter`: a causal filter for each channel over lags 0 to 4095.
All inputs are finite; a program needn't handle non-finite values.
Results may differ from the reference program's by a relative error of at most 0.015.
Values may be sent and summed in bfloat16 or wider, within the bound.
No kernel may reach another device: no remote copies, remote signals or barrier semaphores. Data moves between devices by JAX's collectives and lax.ppermute only.
A program may use at most 64 MiB of HBM per device.

```python
import math
import jax
import jax.numpy as jnp
from jax import lax

D = 4096
HD = 128
HEADS = 16
L = 4096
CH = 32
N_SECTION = 4
N_SEQ = 32
N_TP = 4


def draw_queries(key, part):
    key = jax.random.fold_in(key, 5)
    values_drawn = jnp.clip(jax.random.normal(key, (N_SECTION, L, HEADS, HD), jnp.float32), -4.0, 4.0)
    return values_drawn.reshape(N_SECTION, L, HEADS * HD).astype(jnp.bfloat16)


def draw_attn_keys(key, part):
    key = jax.random.fold_in(key, 7)
    values_drawn = jnp.clip(jax.random.normal(key, (N_SECTION, L, HEADS, HD), jnp.float32), -4.0, 4.0)
    return values_drawn.reshape(N_SECTION, L, HEADS * HD).astype(jnp.bfloat16)


def draw_long_filter(key, part):
    key = jax.random.fold_in(key, 11)
    rate_key, jitter_key = jax.random.split(key)
    full_shape = (N_SECTION, N_TP, N_SEQ, CH, L)
    lowest, highest = (0.1 / L, 1.0 / 30.0)
    decay_rates = jnp.exp(jax.random.uniform(rate_key, (N_SECTION, N_TP, N_SEQ, CH, 1), jnp.float32, math.log(lowest), math.log(highest)))
    lag_ids = lax.broadcasted_iota(jnp.float32, (1, 1, 1, 1, L), 4)
    jitter = jnp.clip(jax.random.normal(jitter_key, full_shape, jnp.float32), -5.0, 5.0)
    return jitter * jnp.exp(-decay_rates * lag_ids) * jnp.sqrt(1.0 - jnp.exp(-2.0 * decay_rates))


def block_scale(key, dims, cuts, low, largest):
    def one(position, blocks):
        heights = jax.random.uniform(jax.random.fold_in(jax.random.fold_in(key, 6), position), (blocks,), jnp.float32, low / len(cuts), largest / len(cuts))
        return jnp.repeat(jnp.exp(heights), dims[position] // blocks).reshape((-1,) + (1,) * (len(dims) - position - 1))

    gain = one(*cuts[0])
    for cut in cuts[1:]:
        gain = gain * one(*cut)
    return gain


def gaussian(stream_key, dims, spread, bound, pieces=(), dtype=jnp.bfloat16):
    result = jax.random.normal(stream_key, dims, jnp.float32) * spread
    if len(pieces) > 0:
        result = block_scale(stream_key, dims, pieces, -0.22, 0.18) * result
    return jnp.clip(result, min=-bound, max=bound).astype(dtype)


def setup_inputs(seed: int = 0) -> dict:
    key_of = jax.random.split(jax.random.key(seed), 11)
    first_stream = gaussian(key_of[0], (N_SECTION, L, D), 1.0, 6.0, ((0, 4), (1, 32), (2, 4)))
    gate_stream = gaussian(key_of[1], (N_SECTION, L, D), 1.0, 6.0, ((0, 4), (1, 32), (2, 4)))
    value_stream = gaussian(key_of[2], (N_SECTION, L, D), 1.0, 6.0, ((0, 4), (1, 32), (2, 4)))
    short_taps = gaussian(key_of[3], (N_SECTION, 3, 3, D), 0.6, 3.0, ((0, 4), (3, 4)), jnp.float32)
    long_filter = draw_long_filter(jax.random.fold_in(key_of[10], 71), 0)
    skip_gain = gaussian(key_of[5], (N_SECTION, D), 1.0, 4.0, ((0, 4), (1, 4)), jnp.float32)
    queries = draw_queries(jax.random.fold_in(key_of[10], 71), 0)
    attn_keys = draw_attn_keys(jax.random.fold_in(key_of[10], 71), 0)
    attn_values = gaussian(key_of[8], (N_SECTION, L, HEADS * HD), 1.0, 6.0, ((0, 4), (1, 32), (2, 4)))
    out_weight = gaussian(key_of[9], (N_SECTION, HEADS * HD, N_TP, D // N_TP), (HEADS * HD) ** -0.5, 0.125, ((0, 4), (1, 4), (3, 32)))
    return {"first_stream": first_stream, "gate_stream": gate_stream, "value_stream": value_stream, "short_taps": short_taps, "long_filter": long_filter, "skip_gain": skip_gain, "queries": queries, "attn_keys": attn_keys, "attn_values": attn_values, "out_weight": out_weight}


def lagged_rows(signal, amount):
    return jnp.pad(signal[:signal.shape[0] - amount], ((amount, 0), (0, 0)))

def short_filter(stream, weights):
    signal = stream.astype(jnp.float32)
    return weights[0] * signal + weights[1] * lagged_rows(signal, 1) + weights[2] * lagged_rows(signal, 2)

def hyena_mixer(first_stream, gate_stream, value_stream, short_taps, long_filter, skip_gain):
    first_short = short_filter(first_stream, short_taps[0])
    gate_short = short_filter(gate_stream, short_taps[1])
    value_short = short_filter(value_stream, short_taps[2])
    product = (first_short * value_short).astype(jnp.bfloat16)
    signal = product.astype(jnp.float32)
    kernel = long_filter.reshape(D, L).T
    length = 2 * L
    spectrum = jnp.fft.rfft(signal, n=length, axis=0) * jnp.fft.rfft(kernel, n=length, axis=0)
    convolved = jnp.fft.irfft(spectrum, n=length, axis=0)[:L]
    long_out = (convolved + skip_gain * signal).astype(jnp.bfloat16)
    return (gate_short * long_out.astype(jnp.float32)).astype(jnp.bfloat16)

def causal_head(operands):
    head_query, head_key, head_value = operands
    scores = jnp.dot(head_query, head_key.T, preferred_element_type=jnp.float32) * (1.0 / math.sqrt(HD))
    row_ids = lax.broadcasted_iota(jnp.int32, scores.shape, 0)
    col_ids = lax.broadcasted_iota(jnp.int32, scores.shape, 1)
    allowed = col_ids <= row_ids
    masked = jnp.where(allowed, scores, -1e+30)
    highest = lax.optimization_barrier(jnp.max(masked, axis=1, keepdims=True))
    probs = jnp.where(allowed, jnp.exp(masked - highest), 0.0)
    totals = lax.optimization_barrier(jnp.sum(probs, axis=1, keepdims=True))
    weighted = jnp.dot(probs.astype(jnp.bfloat16), head_value, preferred_element_type=jnp.float32) / totals
    return weighted.astype(jnp.bfloat16)

def split_heads(columns):
    return columns.reshape(L, HEADS, HD).transpose(1, 0, 2)

def attention(queries, attn_keys, attn_values):
    per_head = lax.map(causal_head, (split_heads(queries), split_heads(attn_keys), split_heads(attn_values)))
    return per_head.transpose(1, 0, 2).reshape(L, HEADS * HD)

def reference(first_stream, gate_stream, value_stream, short_taps, long_filter, skip_gain, queries, attn_keys, attn_values, out_weight):
    hyena_list = []
    attended_list = []
    for section_at in range(N_SECTION):
        hyena_list.append(hyena_mixer(first_stream[section_at], gate_stream[section_at], value_stream[section_at], short_taps[section_at], long_filter[section_at], skip_gain[section_at]))
        heads_out = attention(queries[section_at], attn_keys[section_at], attn_values[section_at])
        weight_flat = out_weight[section_at].reshape(HEADS * HD, D)
        attended_list.append(jnp.dot(heads_out, weight_flat, preferred_element_type=jnp.float32).astype(jnp.bfloat16))
    handed = jnp.stack([hyena_list[(section_at - 1) % N_SECTION] for section_at in range(N_SECTION)])
    return (handed, jnp.stack(attended_list))
```

```python
import math

import jax
import jax.numpy as jnp
import numpy as np
from jax import lax
from jax.sharding import Mesh, PartitionSpec as P

HD = 128
BF16 = jnp.bfloat16
F32 = jnp.float32
HIGH = lax.Precision.HIGH


def dot(left, right, contract, precision=None):
    return lax.dot_general(
        left, right, (contract, ((), ())), precision=precision, preferred_element_type=F32
    )


def transform_tables(depth, breadth):
    full = 2 * depth
    half = depth + 1
    k = np.arange(half)
    a = np.arange(depth)
    b = np.arange(breadth)
    one = -2.0 * np.pi * np.outer(k, a) / full
    first = np.stack([np.cos(one), np.sin(one)])
    mid = -2.0 * np.pi * np.outer(k, b) / (full * breadth)
    two = -2.0 * np.pi * (np.outer(b, b) % breadth) / breadth
    cos_two, sin_two = np.cos(two), np.sin(two)
    forward = np.block([[cos_two, sin_two], [-sin_two, cos_two]])
    backward = np.block([[cos_two, -sin_two], [sin_two, cos_two]])
    weight = np.where((k == 0) | (k == depth), 1.0, 2.0) / (full * breadth)
    last = np.concatenate([np.cos(one).T * weight, np.sin(one).T * weight], axis=1)
    as32 = lambda x: np.asarray(x, np.float32)
    return as32(first), as32(np.cos(mid)), as32(np.sin(mid)), as32(forward), as32(backward), as32(last)


def forward_transform(blocks, tables):
    first, cos_mid, sin_mid, forward, _, _ = tables
    depth, channels, breadth = blocks.shape
    flat = blocks.reshape(depth, channels * breadth)
    real = dot(first[0], flat, ((1,), (0,)), HIGH).reshape(-1, channels, breadth)
    imag = dot(first[1], flat, ((1,), (0,)), HIGH).reshape(-1, channels, breadth)
    cos_mid, sin_mid = cos_mid[:, None], sin_mid[:, None]
    turned = jnp.concatenate(
        [real * cos_mid - imag * sin_mid, real * sin_mid + imag * cos_mid], axis=2
    )
    return dot(turned, forward, ((2,), (0,)), HIGH)


def inverse_transform(spectrum, tables):
    _, cos_mid, sin_mid, _, backward, last = tables
    half, channels, twice = spectrum.shape
    breadth = twice // 2
    mid = dot(spectrum, backward, ((2,), (0,)), HIGH)
    real, imag = mid[:, :, :breadth], mid[:, :, breadth:]
    cos_mid, sin_mid = cos_mid[:, None], sin_mid[:, None]
    turned = jnp.concatenate(
        [real * cos_mid + imag * sin_mid, imag * cos_mid - real * sin_mid], axis=0
    )
    out = dot(last, turned.reshape(2 * half, channels * breadth), ((1,), (0,)), HIGH)
    return out.reshape(-1, channels, breadth)


def short_by_token(stream, before, taps):
    rows = stream.shape[0]
    whole = jnp.concatenate([before, stream], axis=0).astype(F32)
    return taps[0] * whole[2:] + taps[1] * whole[1 : rows + 1] + taps[2] * whole[:rows]


def body(
    first_stream,
    gate_stream,
    value_stream,
    short_taps,
    long_filter,
    skip_gain,
    queries,
    attn_keys,
    attn_values,
    out_weight,
):
    n_z, n_x, n_tp = lax.axis_size("z"), lax.axis_size("xh"), lax.axis_size("tp")
    n_seq = n_z * n_x
    n_plane = n_x * n_tp
    seq_at = lax.axis_index(("z", "xh"))
    tp_at = lax.axis_index("tp")
    x_at = lax.axis_index("xh")
    rows = queries.shape[1]
    wide = queries.shape[2]
    channels = long_filter.shape[3]
    heads = wide // HD
    quarter = rows // n_tp
    eighth = quarter // n_x

    streams = jnp.stack([first_stream[0], gate_stream[0], value_stream[0]])
    tails = lax.ppermute(
        streams[:, -2:], ("z", "xh"), [(i, i + 1) for i in range(n_seq - 1)]
    )

    weight = out_weight[0].transpose(1, 2, 0)
    packed = jnp.concatenate(
        [
            queries[0].reshape(n_tp, quarter, wide),
            attn_keys[0].reshape(n_tp, quarter, wide),
            attn_values[0].reshape(n_tp, quarter, wide),
            weight,
        ],
        axis=1,
    )
    packed = lax.all_to_all(packed, "tp", 0, 0)
    weight = packed[:, 3 * quarter :].transpose(1, 0, 2).reshape(channels, n_tp * wide)
    weight = lax.all_gather(weight, "z", axis=0, tiled=True)

    taps = short_taps[0]
    first_short = short_by_token(first_stream[0], tails[0], taps[0])
    value_short = short_by_token(value_stream[0], tails[2], taps[2])
    product = (first_short * value_short).astype(BF16)
    product = product.T.reshape(n_seq, channels, rows)
    attn_in = packed[:, : 3 * quarter].reshape(n_tp, 3, n_x, eighth, heads, HD)
    attn_in = attn_in.transpose(0, 4, 2, 1, 3, 5).reshape(n_seq, 3 * eighth, HD)
    mixed = lax.all_to_all(jnp.concatenate([attn_in, product], axis=1), ("z", "xh"), 0, 0)

    tables = transform_tables(n_seq, rows)
    kernel = long_filter[0, 0, 0].reshape(channels, n_seq, rows).transpose(1, 0, 2)
    kernel_spec = forward_transform(kernel, tables)

    own = mixed[:, : 3 * eighth].reshape(n_seq, 3, eighth, HD).transpose(1, 0, 2, 3)
    query = own[0].reshape(n_seq * eighth, HD)
    pairs = lax.all_to_all(
        jnp.broadcast_to(own[None, 1:], (n_plane, 2, n_seq, eighth, HD)), ("xh", "tp"), 0, 0
    )

    product = mixed[:, 3 * eighth :].astype(F32)
    spec = forward_transform(product, tables)
    real, imag = spec[:, :, :rows], spec[:, :, rows:]
    kernel_real, kernel_imag = kernel_spec[:, :, :rows], kernel_spec[:, :, rows:]
    joined = jnp.concatenate(
        [real * kernel_real - imag * kernel_imag, real * kernel_imag + imag * kernel_real], axis=2
    )
    convolved = inverse_transform(joined, tables)
    gain = lax.dynamic_slice_in_dim(skip_gain[0], seq_at * channels, channels, 0)
    long_out = (convolved + gain[None, :, None] * product).astype(BF16)

    keys = pairs[:, 0].reshape(-1, HD)
    values = pairs[:, 1].reshape(-1, HD)
    scores = dot(query, keys, ((1,), (1,))) * (1.0 / math.sqrt(HD))
    q_ids = lax.broadcasted_iota(jnp.int32, (n_seq * eighth, 1), 0)
    q_pos = q_ids // eighth * rows + q_ids % eighth + tp_at * quarter + x_at * eighth
    k_ids = lax.broadcasted_iota(jnp.int32, (1, n_seq * rows), 1)
    k_from = k_ids // (n_seq * eighth)
    k_in = k_ids % (n_seq * eighth)
    k_pos = (
        k_in // eighth * rows + k_in % eighth + k_from % n_tp * quarter + k_from // n_tp * eighth
    )
    allowed = k_pos <= q_pos
    masked = jnp.where(allowed, scores, -1e30)
    highest = jnp.max(masked, axis=1, keepdims=True)
    probs = jnp.exp(masked - highest)
    totals = jnp.sum(probs, axis=1, keepdims=True)
    heads_out = (dot(probs.astype(BF16), values, ((1,), (0,))) / totals).astype(BF16)

    back = lax.all_to_all(
        jnp.concatenate([heads_out.reshape(n_seq, eighth, HD), long_out], axis=1),
        ("z", "xh"),
        0,
        0,
    )
    heads_rows = back[:, :eighth].reshape(n_z, n_x, eighth, HD).transpose(1, 2, 0, 3)
    heads_rows = heads_rows.reshape(quarter, n_z * HD)
    plane_rows = lax.all_to_all(
        jnp.broadcast_to(heads_rows[None], (n_plane, quarter, n_z * HD)), ("xh", "tp"), 0, 0
    ).reshape(n_x * rows, n_z * HD)

    gate_short = short_by_token(gate_stream[0], tails[1], taps[1])
    long_rows = back[:, eighth:].reshape(n_seq * channels, rows).T
    hyena = (gate_short * long_rows.astype(F32)).astype(BF16)
    n_sec = lax.axis_size("section")
    handed = lax.ppermute(hyena, "section", [(i, (i + 1) % n_sec) for i in range(n_sec)])

    out = dot(plane_rows, weight, ((1,), (1,))).astype(BF16)
    out = lax.all_to_all(out.reshape(n_x, rows, n_z * channels), "xh", 0, 0)
    attended = out.reshape(n_x, rows, n_z, channels).transpose(1, 2, 0, 3).reshape(rows, -1)
    return (handed[None], attended[None])


def solution(mesh):
    n_sec, n_seq, n_tp = (mesh.shape[name] for name in ("section", "seq", "tp"))
    finer = Mesh(mesh.devices.reshape(n_sec, n_seq // 2, 2, n_tp), ("section", "z", "xh", "tp"))
    seq = ("z", "xh")
    placed = (
        P("section", seq, "tp"),
        P("section", seq, "tp"),
        P("section", seq, "tp"),
        P("section", None, None, "tp"),
        P("section", "tp", seq, None, None),
        P("section", "tp"),
        P("section", seq, "tp"),
        P("section", seq, "tp"),
        P("section", seq, "tp"),
        P("section", "tp", None, seq),
    )
    return jax.shard_map(
        body,
        mesh=finer,
        in_specs=placed,
        out_specs=(P("section", seq, "tp"), P("section", seq, "tp")),
        check_vma=False,
    )
```

```python
import math

import jax
import jax.numpy as jnp
import numpy as np
from jax import lax
from jax.sharding import Mesh, PartitionSpec as P

HD = 128
BF16 = jnp.bfloat16
F32 = jnp.float32
HIGH = lax.Precision.HIGH


def dot(left, right, contract, precision=None):
    return lax.dot_general(
        left, right, (contract, ((), ())), precision=precision, preferred_element_type=F32
    )


def transform_tables(depth, breadth):
    full = 2 * depth
    half = depth + 1
    k = np.arange(half)
    a = np.arange(depth)
    b = np.arange(breadth)
    one = -2.0 * np.pi * np.outer(k, a) / full
    first = np.stack([np.cos(one), np.sin(one)])
    mid = -2.0 * np.pi * np.outer(k, b) / (full * breadth)
    two = -2.0 * np.pi * (np.outer(b, b) % breadth) / breadth
    cos_two, sin_two = np.cos(two), np.sin(two)
    forward = np.block([[cos_two, sin_two], [-sin_two, cos_two]])
    backward = np.block([[cos_two, -sin_two], [sin_two, cos_two]])
    weight = np.where((k == 0) | (k == depth), 1.0, 2.0) / (full * breadth)
    last = np.concatenate([np.cos(one).T * weight, np.sin(one).T * weight], axis=1)
    as32 = lambda x: np.asarray(x, np.float32)
    return as32(first), as32(np.cos(mid)), as32(np.sin(mid)), as32(forward), as32(backward), as32(last)


def forward_transform(blocks, tables):
    first, cos_mid, sin_mid, forward, _, _ = tables
    depth, channels, breadth = blocks.shape
    flat = blocks.reshape(depth, channels * breadth)
    real = dot(first[0], flat, ((1,), (0,)), HIGH).reshape(-1, channels, breadth)
    imag = dot(first[1], flat, ((1,), (0,)), HIGH).reshape(-1, channels, breadth)
    cos_mid, sin_mid = cos_mid[:, None], sin_mid[:, None]
    turned = jnp.concatenate(
        [real * cos_mid - imag * sin_mid, real * sin_mid + imag * cos_mid], axis=2
    )
    return dot(turned, forward, ((2,), (0,)), HIGH)


def inverse_transform(spectrum, tables):
    _, cos_mid, sin_mid, _, backward, last = tables
    half, channels, twice = spectrum.shape
    breadth = twice // 2
    mid = dot(spectrum, backward, ((2,), (0,)), HIGH)
    real, imag = mid[:, :, :breadth], mid[:, :, breadth:]
    cos_mid, sin_mid = cos_mid[:, None], sin_mid[:, None]
    turned = jnp.concatenate(
        [real * cos_mid + imag * sin_mid, imag * cos_mid - real * sin_mid], axis=0
    )
    out = dot(last, turned.reshape(2 * half, channels * breadth), ((1,), (0,)), HIGH)
    return out.reshape(-1, channels, breadth)


def short_by_token(stream, before, taps):
    rows = stream.shape[0]
    whole = jnp.concatenate([before, stream], axis=0).astype(F32)
    return taps[0] * whole[2:] + taps[1] * whole[1 : rows + 1] + taps[2] * whole[:rows]


def body(
    first_stream,
    gate_stream,
    value_stream,
    short_taps,
    long_filter,
    skip_gain,
    queries,
    attn_keys,
    attn_values,
    out_weight,
):
    n_z, n_x, n_tp = lax.axis_size("z"), lax.axis_size("xh"), lax.axis_size("tp")
    n_seq = n_z * n_x
    n_plane = n_x * n_tp
    seq_at = lax.axis_index(("z", "xh"))
    tp_at = lax.axis_index("tp")
    x_at = lax.axis_index("xh")
    rows = queries.shape[1]
    wide = queries.shape[2]
    channels = long_filter.shape[3]
    heads = wide // HD
    quarter = rows // n_tp
    eighth = quarter // n_x

    streams = jnp.stack([first_stream[0], gate_stream[0], value_stream[0]])
    tails = lax.ppermute(
        streams[:, -2:], ("z", "xh"), [(i, i + 1) for i in range(n_seq - 1)]
    )

    weight = out_weight[0].transpose(1, 2, 0)
    early, late = weight[: n_tp // 2], weight[n_tp // 2 :]
    early = lax.all_gather(early.reshape(-1, wide), "z")
    packed = jnp.concatenate(
        [
            queries[0].reshape(n_tp, quarter, wide),
            attn_keys[0].reshape(n_tp, quarter, wide),
            attn_values[0].reshape(n_tp, quarter, wide),
        ],
        axis=1,
    )
    packed = lax.all_to_all(packed, "tp", 0, 0)

    taps = short_taps[0]
    first_short = short_by_token(first_stream[0], tails[0], taps[0])
    value_short = short_by_token(value_stream[0], tails[2], taps[2])
    product = (first_short * value_short).astype(BF16)
    product = product.T.reshape(n_seq, channels, rows)
    attn_in = packed.reshape(n_tp, 3, n_x, eighth, heads, HD)
    attn_in = attn_in.transpose(0, 4, 2, 1, 3, 5).reshape(n_seq, 3 * eighth, HD)
    mixed = lax.all_to_all(jnp.concatenate([attn_in, product], axis=1), ("z", "xh"), 0, 0)
    mixed, late = lax.optimization_barrier((mixed, late))
    late = lax.all_gather(late.reshape(-1, wide), "z")

    tables = transform_tables(n_seq, rows)
    kernel = long_filter[0, 0, 0].reshape(channels, n_seq, rows).transpose(1, 0, 2)
    kernel_spec = forward_transform(kernel, tables)

    own = mixed[:, : 3 * eighth].reshape(n_seq, 3, eighth, HD).transpose(1, 0, 2, 3)
    query = own[0].reshape(n_seq * eighth, HD)
    pairs = lax.all_to_all(
        jnp.broadcast_to(own[None, 1:], (n_plane, 2, n_seq, eighth, HD)), ("xh", "tp"), 0, 0
    )

    product = mixed[:, 3 * eighth :].astype(F32)
    spec = forward_transform(product, tables)
    real, imag = spec[:, :, :rows], spec[:, :, rows:]
    kernel_real, kernel_imag = kernel_spec[:, :, :rows], kernel_spec[:, :, rows:]
    joined = jnp.concatenate(
        [real * kernel_real - imag * kernel_imag, real * kernel_imag + imag * kernel_real], axis=2
    )
    convolved = inverse_transform(joined, tables)
    gain = lax.dynamic_slice_in_dim(skip_gain[0], seq_at * channels, channels, 0)
    long_out = (convolved + gain[None, :, None] * product).astype(BF16)

    keys = pairs[:, 0].reshape(-1, HD)
    values = pairs[:, 1].reshape(-1, HD)
    scores = dot(query, keys, ((1,), (1,))) * (1.0 / math.sqrt(HD))
    q_ids = lax.broadcasted_iota(jnp.int32, (n_seq * eighth, 1), 0)
    q_pos = q_ids // eighth * rows + q_ids % eighth + tp_at * quarter + x_at * eighth
    k_ids = lax.broadcasted_iota(jnp.int32, (1, n_seq * rows), 1)
    k_from = k_ids // (n_seq * eighth)
    k_in = k_ids % (n_seq * eighth)
    k_pos = (
        k_in // eighth * rows + k_in % eighth + k_from % n_tp * quarter + k_from // n_tp * eighth
    )
    allowed = k_pos <= q_pos
    masked = jnp.where(allowed, scores, -1e30)
    highest = jnp.max(masked, axis=1, keepdims=True)
    probs = jnp.exp(masked - highest)
    totals = jnp.sum(probs, axis=1, keepdims=True)
    heads_out = (dot(probs.astype(BF16), values, ((1,), (0,))) / totals).astype(BF16)

    back = lax.all_to_all(
        jnp.concatenate([heads_out.reshape(n_seq, eighth, HD), long_out], axis=1),
        ("z", "xh"),
        0,
        0,
    )
    heads_rows = back[:, :eighth].reshape(n_tp, heads, n_x, eighth, HD).transpose(0, 2, 3, 1, 4)
    heads_rows = jnp.broadcast_to(
        heads_rows.reshape(1, n_tp, quarter, wide), (n_x, n_tp, quarter, wide)
    )
    plane_rows = lax.all_to_all(
        heads_rows.reshape(n_plane, quarter, wide), ("xh", "tp"), 0, 0
    ).reshape(n_x * rows, wide)

    gate_short = short_by_token(gate_stream[0], tails[1], taps[1])
    long_rows = back[:, eighth:].reshape(n_seq * channels, rows).T
    hyena = (gate_short * long_rows.astype(F32)).astype(BF16)
    n_sec = lax.axis_size("section")
    handed = lax.ppermute(hyena, "section", [(i, (i + 1) % n_sec) for i in range(n_sec)])

    partials = []
    for weight in (early, late):
        weight = weight.reshape(n_z, n_tp // 2, channels, wide)
        for at in range(n_tp // 2):
            part = weight[:, at].reshape(n_z * channels, wide)
            part = dot(plane_rows, part, ((1,), (1,))).astype(BF16)
            partials.append(part.reshape(n_x, rows, n_z * channels))
    partials = jnp.stack(partials, axis=1).reshape(n_plane, rows, n_z * channels)
    partials = lax.all_to_all(partials, ("xh", "tp"), 0, 0)
    out = jnp.sum(partials.reshape(n_x, n_tp, rows, n_z * channels).astype(F32), axis=1).astype(BF16)
    attended = out.reshape(n_x, rows, n_z, channels).transpose(1, 2, 0, 3).reshape(rows, -1)
    return (handed[None], attended[None])


def solution(mesh):
    n_sec, n_seq, n_tp = (mesh.shape[name] for name in ("section", "seq", "tp"))
    finer = Mesh(mesh.devices.reshape(n_sec, n_seq // 2, 2, n_tp), ("section", "z", "xh", "tp"))
    seq = ("z", "xh")
    placed = (
        P("section", seq, "tp"),
        P("section", seq, "tp"),
        P("section", seq, "tp"),
        P("section", None, None, "tp"),
        P("section", "tp", seq, None, None),
        P("section", "tp"),
        P("section", seq, "tp"),
        P("section", seq, "tp"),
        P("section", seq, "tp"),
        P("section", "tp", None, seq),
    )
    return jax.shard_map(
        body,
        mesh=finer,
        in_specs=placed,
        out_specs=(P("section", seq, "tp"), P("section", seq, "tp")),
        check_vma=False,
    )
```

```python
import math

import jax
import jax.numpy as jnp
import numpy as np
from jax import lax
from jax.sharding import Mesh, PartitionSpec as P

HD = 128
BF16 = jnp.bfloat16
F32 = jnp.float32
HIGH = lax.Precision.HIGH


def dot(left, right, contract, precision=None):
    return lax.dot_general(
        left, right, (contract, ((), ())), precision=precision, preferred_element_type=F32
    )


def transform_tables(depth, breadth):
    full = 2 * depth
    half = depth + 1
    k = np.arange(half)
    a = np.arange(depth)
    b = np.arange(breadth)
    one = -2.0 * np.pi * np.outer(k, a) / full
    first = np.stack([np.cos(one), np.sin(one)])
    mid = -2.0 * np.pi * np.outer(k, b) / (full * breadth)
    two = -2.0 * np.pi * (np.outer(b, b) % breadth) / breadth
    cos_two, sin_two = np.cos(two), np.sin(two)
    forward = np.block([[cos_two, sin_two], [-sin_two, cos_two]])
    backward = np.block([[cos_two, -sin_two], [sin_two, cos_two]])
    weight = np.where((k == 0) | (k == depth), 1.0, 2.0) / (full * breadth)
    last = np.concatenate([np.cos(one).T * weight, np.sin(one).T * weight], axis=1)
    as32 = lambda x: np.asarray(x, np.float32)
    return as32(first), as32(np.cos(mid)), as32(np.sin(mid)), as32(forward), as32(backward), as32(last)


def forward_transform(blocks, tables):
    first, cos_mid, sin_mid, forward, _, _ = tables
    depth, channels, breadth = blocks.shape
    flat = blocks.reshape(depth, channels * breadth)
    real = dot(first[0], flat, ((1,), (0,)), HIGH).reshape(-1, channels, breadth)
    imag = dot(first[1], flat, ((1,), (0,)), HIGH).reshape(-1, channels, breadth)
    cos_mid, sin_mid = cos_mid[:, None], sin_mid[:, None]
    turned = jnp.concatenate(
        [real * cos_mid - imag * sin_mid, real * sin_mid + imag * cos_mid], axis=2
    )
    return dot(turned, forward, ((2,), (0,)), HIGH)


def inverse_transform(spectrum, tables):
    _, cos_mid, sin_mid, _, backward, last = tables
    half, channels, twice = spectrum.shape
    breadth = twice // 2
    mid = dot(spectrum, backward, ((2,), (0,)), HIGH)
    real, imag = mid[:, :, :breadth], mid[:, :, breadth:]
    cos_mid, sin_mid = cos_mid[:, None], sin_mid[:, None]
    turned = jnp.concatenate(
        [real * cos_mid + imag * sin_mid, imag * cos_mid - real * sin_mid], axis=0
    )
    out = dot(last, turned.reshape(2 * half, channels * breadth), ((1,), (0,)), HIGH)
    return out.reshape(-1, channels, breadth)


def short_by_token(stream, before, taps):
    rows = stream.shape[0]
    whole = jnp.concatenate([before, stream], axis=0).astype(F32)
    return taps[0] * whole[2:] + taps[1] * whole[1 : rows + 1] + taps[2] * whole[:rows]


def edge_short(edges, taps):
    edges = edges.astype(F32)
    before = jnp.pad(edges[:-1, 2:], ((1, 0), (0, 0), (0, 0)))
    zero = taps[0] * edges[:, 0] + taps[1] * before[:, 1] + taps[2] * before[:, 0]
    one = taps[0] * edges[:, 1] + taps[1] * edges[:, 0] + taps[2] * before[:, 1]
    return zero, one


def part_of_attention(query, keys, values, q_pos, k_pos):
    scores = dot(query, keys, ((1,), (1,))) * (1.0 / math.sqrt(HD))
    allowed = k_pos <= q_pos
    masked = jnp.where(allowed, scores, -1e30)
    highest = jnp.max(masked, axis=1, keepdims=True)
    probs = jnp.where(allowed, jnp.exp(masked - highest), 0.0)
    totals = jnp.sum(probs, axis=1, keepdims=True)
    out = dot(probs.astype(BF16), values, ((1,), (0,))) / jnp.maximum(totals, 1e-30)
    return out, jnp.where(totals > 0.0, highest + jnp.log(jnp.maximum(totals, 1e-30)), -1e30)


def in_three(x):
    first = x.astype(BF16)
    rest = x - first.astype(F32)
    second = rest.astype(BF16)
    return [first, second, (rest - second.astype(F32)).astype(BF16)]


def body(
    first_stream,
    gate_stream,
    value_stream,
    short_taps,
    long_filter,
    skip_gain,
    queries,
    attn_keys,
    attn_values,
    out_weight,
):
    seq = ("zi", "zp", "zq", "xh")
    n_seq, n_x, n_tp = lax.axis_size(seq), lax.axis_size("xh"), lax.axis_size("tp")
    n_pair = lax.axis_size("zq") * n_x
    n_z = n_seq // n_x
    n_plane = n_x * n_tp
    seq_at = lax.axis_index(seq)
    half_at = lax.axis_index("zp")
    pair_at = lax.axis_index(("zq", "xh"))
    rows = queries.shape[1]
    wide = queries.shape[2]
    channels = long_filter.shape[3]
    heads = wide // HD
    chunks = n_seq // heads
    few = rows // chunks
    own_rows = n_seq * few
    taps = short_taps[0]

    weight = out_weight[0].transpose(1, 2, 0).reshape(-1, wide)
    weight = lax.all_gather(weight, ("zi", "zp", "zq"))

    nothing = jnp.zeros_like(first_stream[0, :2])
    first_short = short_by_token(first_stream[0], nothing, taps[0])
    value_short = short_by_token(value_stream[0], nothing, taps[2])
    product = (first_short * value_short).astype(BF16)
    product = product.T.reshape(n_seq, channels, rows)
    edges = jnp.concatenate(
        [x[0, at : at + 2] for x in (first_stream, value_stream) for at in (0, rows - 2)]
    )
    edges = edges.reshape(8, n_seq, channels).transpose(1, 0, 2).reshape(n_seq, -1, rows)
    attn_in = jnp.stack([queries[0], attn_keys[0], attn_values[0]])
    attn_in = attn_in.reshape(3, chunks, few, heads, HD).transpose(3, 1, 0, 2, 4)
    attn_in = attn_in.reshape(n_seq, 3 * few, HD)
    mixed = lax.all_to_all(jnp.concatenate([attn_in, product, edges], axis=1), seq, 0, 0)

    tail = lax.ppermute(gate_stream[0, -2:], seq, [(i, i + 1) for i in range(n_seq - 1)])
    tables = transform_tables(n_seq, rows)
    kernel = long_filter[0, 0, 0].reshape(channels, n_seq, rows).transpose(1, 0, 2)
    kernel_spec = forward_transform(kernel, tables)

    own = mixed[:, : 3 * few].reshape(n_seq, 3, few, HD).transpose(1, 0, 2, 3)
    query = own[0].reshape(own_rows, HD)
    swap = [(0, 1), (1, 0)]
    other_query = lax.ppermute(query, "zp", swap)
    pairs = lax.all_to_all(
        jnp.broadcast_to(own[None, 1:], (n_pair, 2, n_seq, few, HD)), ("zq", "xh"), 0, 0
    )

    local_taps = lax.dynamic_slice_in_dim(taps, seq_at * channels, channels, 2)
    edges = mixed[:, 3 * few + channels :].reshape(n_seq, 8, channels)
    first_zero, first_one = edge_short(edges[:, :4], local_taps[0])
    value_zero, value_one = edge_short(edges[:, 4:], local_taps[2])
    token = lax.broadcasted_iota(jnp.int32, (1, 1, rows), 2)
    product = mixed[:, 3 * few : 3 * few + channels]
    product = jnp.where(token == 0, (first_zero * value_zero).astype(BF16)[:, :, None], product)
    product = jnp.where(token == 1, (first_one * value_one).astype(BF16)[:, :, None], product)
    product = product.astype(F32)
    spec = forward_transform(product, tables)
    real, imag = spec[:, :, :rows], spec[:, :, rows:]
    kernel_real, kernel_imag = kernel_spec[:, :, :rows], kernel_spec[:, :, rows:]
    joined = jnp.concatenate(
        [real * kernel_real - imag * kernel_imag, real * kernel_imag + imag * kernel_real], axis=2
    )
    convolved = inverse_transform(joined, tables)
    gain = lax.dynamic_slice_in_dim(skip_gain[0], seq_at * channels, channels, 0)
    long_out = (convolved + gain[None, :, None] * product).astype(BF16)

    keys = pairs[:, 0].reshape(-1, HD)
    values = pairs[:, 1].reshape(-1, HD)
    q_ids = lax.broadcasted_iota(jnp.int32, (own_rows, 1), 0)
    q_base = q_ids // few * rows + q_ids % few + pair_at * few
    k_ids = lax.broadcasted_iota(jnp.int32, (1, n_pair * own_rows), 1)
    k_in = k_ids % own_rows
    k_pos = k_in // few * rows + k_in % few + (half_at * n_pair + k_ids // own_rows) * few
    other_out, other_log = part_of_attention(
        other_query, keys, values, q_base + (1 - half_at) * (n_pair * few), k_pos
    )
    sent = jnp.concatenate(
        [other_out.astype(BF16), jnp.concatenate(in_three(other_log.reshape(-1, HD)))]
    )
    got = lax.ppermute(sent, "zp", swap)
    own_out, own_log = part_of_attention(
        query, keys, values, q_base + half_at * (n_pair * few), k_pos
    )
    got_log = got[own_rows:].astype(F32).reshape(3, -1, HD)
    got_log = (got_log[0] + got_log[1] + got_log[2]).reshape(own_rows, 1)
    highest = jnp.maximum(own_log, got_log)
    own_share, got_share = jnp.exp(own_log - highest), jnp.exp(got_log - highest)
    heads_out = own_out * own_share + got[:own_rows].astype(F32) * got_share
    heads_out = (heads_out / (own_share + got_share)).astype(BF16)

    back = lax.all_to_all(
        jnp.concatenate([heads_out.reshape(n_seq, few, HD), long_out], axis=1), seq, 0, 0
    )
    natural = back[:, :few].reshape(heads, chunks, few, HD).transpose(1, 2, 0, 3)
    plane_rows = lax.all_to_all(
        jnp.broadcast_to(natural.reshape(1, rows, wide), (n_x, rows, wide)), "xh", 0, 0
    ).reshape(n_x * rows, wide)

    gate_short = short_by_token(gate_stream[0], tail, taps[1])
    long_rows = back[:, few:].reshape(n_seq * channels, rows).T
    hyena = (gate_short * long_rows.astype(F32)).astype(BF16)
    plane_rows, hyena = lax.optimization_barrier((plane_rows, hyena))
    n_sec = lax.axis_size("section")
    handed = lax.ppermute(hyena, "section", [(i, (i + 1) % n_sec) for i in range(n_sec)])

    partials = []
    weight = weight.reshape(n_z, n_tp, channels, wide)
    for at in range(n_tp):
        part = weight[:, at].reshape(n_z * channels, wide)
        part = dot(plane_rows, part, ((1,), (1,))).astype(BF16)
        partials.append(part.reshape(n_x, rows, n_z * channels))
    partials = jnp.stack(partials, axis=1).reshape(n_plane, rows, n_z * channels)
    partials = lax.all_to_all(partials, ("xh", "tp"), 0, 0)
    out = jnp.sum(partials.reshape(n_x, n_tp, rows, n_z * channels).astype(F32), axis=1).astype(BF16)
    attended = out.reshape(n_x, rows, n_z, channels).transpose(1, 2, 0, 3).reshape(rows, -1)
    return (handed[None], attended[None])


def solution(mesh):
    n_sec, n_seq, n_tp = (mesh.shape[name] for name in ("section", "seq", "tp"))
    finer = Mesh(
        mesh.devices.reshape(n_sec, n_seq // 8, 2, 2, 2, n_tp),
        ("section", "zi", "zp", "zq", "xh", "tp"),
    )
    seq = ("zi", "zp", "zq", "xh")
    placed = (
        P("section", seq, "tp"),
        P("section", seq, "tp"),
        P("section", seq, "tp"),
        P("section", None, None, "tp"),
        P("section", "tp", seq, None, None),
        P("section", "tp"),
        P("section", seq, "tp"),
        P("section", seq, "tp"),
        P("section", seq, "tp"),
        P("section", "tp", None, seq),
    )
    return jax.shard_map(
        body,
        mesh=finer,
        in_specs=placed,
        out_specs=(P("section", seq, "tp"), P("section", seq, "tp")),
        check_vma=False,
    )
```

```python
import functools
import math

import jax
import jax.numpy as jnp
import numpy as np
from jax import lax
from jax.experimental import pallas as pl
from jax.experimental.pallas import tpu as pltpu
from jax.sharding import Mesh, PartitionSpec as P

HD = 128
BF16 = jnp.bfloat16
F32 = jnp.float32
HIGH = lax.Precision.HIGH


def dot(left, right, contract, precision=None):
    return lax.dot_general(
        left, right, (contract, ((), ())), precision=precision, preferred_element_type=F32
    )


def transform_tables(depth, breadth):
    full = 2 * depth
    half = depth + 1
    k = np.arange(half)
    a = np.arange(depth)
    b = np.arange(breadth)
    one = -2.0 * np.pi * np.outer(k, a) / full
    first = np.stack([np.cos(one), np.sin(one)])
    mid = -2.0 * np.pi * np.outer(k, b) / (full * breadth)
    two = -2.0 * np.pi * (np.outer(b, b) % breadth) / breadth
    cos_two, sin_two = np.cos(two), np.sin(two)
    forward = np.block([[cos_two, sin_two], [-sin_two, cos_two]])
    backward = np.block([[cos_two, -sin_two], [sin_two, cos_two]])
    weight = np.where((k == 0) | (k == depth), 1.0, 2.0) / (full * breadth)
    last = np.concatenate([np.cos(one).T * weight, np.sin(one).T * weight], axis=1)
    as32 = lambda x: np.asarray(x, np.float32)
    return as32(first), as32(np.cos(mid)), as32(np.sin(mid)), as32(forward), as32(backward), as32(last)


def forward_transform(blocks, tables):
    first, cos_mid, sin_mid, forward, _, _ = tables
    depth, channels, breadth = blocks.shape
    flat = blocks.reshape(depth, channels * breadth)
    real = dot(first[0], flat, ((1,), (0,)), HIGH).reshape(-1, channels, breadth)
    imag = dot(first[1], flat, ((1,), (0,)), HIGH).reshape(-1, channels, breadth)
    cos_mid, sin_mid = cos_mid[:, None], sin_mid[:, None]
    turned = jnp.concatenate(
        [real * cos_mid - imag * sin_mid, real * sin_mid + imag * cos_mid], axis=2
    )
    return dot(turned, forward, ((2,), (0,)), HIGH)


def inverse_transform(spectrum, tables):
    _, cos_mid, sin_mid, _, backward, last = tables
    half, channels, twice = spectrum.shape
    breadth = twice // 2
    mid = dot(spectrum, backward, ((2,), (0,)), HIGH)
    real, imag = mid[:, :, :breadth], mid[:, :, breadth:]
    cos_mid, sin_mid = cos_mid[:, None], sin_mid[:, None]
    turned = jnp.concatenate(
        [real * cos_mid + imag * sin_mid, imag * cos_mid - real * sin_mid], axis=0
    )
    out = dot(last, turned.reshape(2 * half, channels * breadth), ((1,), (0,)), HIGH)
    return out.reshape(-1, channels, breadth)


def edge_short(edges, taps):
    edges = edges.astype(F32)
    before = jnp.pad(edges[:-1, 2:], ((1, 0), (0, 0), (0, 0)))
    zero = taps[0] * edges[:, 0] + taps[1] * before[:, 1] + taps[2] * before[:, 0]
    one = taps[0] * edges[:, 1] + taps[1] * edges[:, 0] + taps[2] * before[:, 1]
    return zero, one


def kernel_call(kernel, out_shape, scalars, arrays, scratch=(), flops=0):
    in_specs = [pl.BlockSpec(memory_space=pltpu.SMEM)] * len(scalars)
    in_specs += [pl.BlockSpec(memory_space=pltpu.VMEM)] * len(arrays)
    outs = out_shape if isinstance(out_shape, tuple) else (out_shape,)
    moved = sum(x.size * x.dtype.itemsize for x in (*arrays, *outs))
    return pl.pallas_call(
        kernel,
        out_shape=out_shape,
        in_specs=in_specs,
        out_specs=jax.tree.map(lambda _: pl.BlockSpec(memory_space=pltpu.VMEM), out_shape),
        scratch_shapes=list(scratch),
        compiler_params=pltpu.CompilerParams(vmem_limit_bytes=32 * 1024 * 1024),
        cost_estimate=pl.CostEstimate(flops=flops, bytes_accessed=moved, transcendentals=0),
    )(*scalars, *arrays)


def pack_kernel(first_ref, value_ref, taps_ref, query_ref, key_ref, value_head_ref, out_ref):
    n_seq, _, lanes = out_ref.shape
    rows, wide = query_ref.shape
    heads = wide // HD
    chunks = n_seq // heads
    few = rows // chunks
    per = n_seq * lanes // first_ref.shape[1]
    channels = lanes // per
    for at, ref in enumerate((query_ref, key_ref, value_head_ref)):
        for head in range(heads):
            block = ref[:, head * HD : (head + 1) * HD].reshape(chunks, few, HD)
            out_ref[head * chunks : (head + 1) * chunks, at * few : (at + 1) * few, :] = block
    for group in range(n_seq // per):
        span = slice(group * lanes, (group + 1) * lanes)
        shorts, edges = [], []
        for ref, which in ((first_ref, 0), (value_ref, 2)):
            x = ref[:, span].astype(F32)
            shorts.append(
                taps_ref[which, 0:1, span] * x
                + taps_ref[which, 1:2, span] * pltpu.roll(x, 1, 0)
                + taps_ref[which, 2:3, span] * pltpu.roll(x, 2, 0)
            )
            edges += [x[:2], x[rows - 2 :]]
        turned = (shorts[0] * shorts[1]).T.astype(BF16).reshape(per, channels, rows)
        out_ref[group * per : (group + 1) * per, 3 * few : 3 * few + channels, :] = turned
        edges = jnp.concatenate(edges, axis=0)
        for at in range(per):
            edge = pltpu.roll(edges, lanes - at * channels, 1) if at else edges
            out_ref[group * per + at, 3 * few + channels :, :] = edge.astype(BF16)


def attend(delta, query_ref, pairs_ref, tile, few, rows):
    size = 128
    query = query_ref[tile * size : (tile + 1) * size, :]
    row = lax.broadcasted_iota(jnp.int32, (size, size), 0)
    column = lax.broadcasted_iota(jnp.int32, (size, size), 1)
    q_pos = row // few * rows + row % few
    k_pos = column // few * rows + column % few
    parts = []
    for at in range(pairs_ref.shape[0]):
        allowed = k_pos + (at * few + delta) <= q_pos
        for start, stop in ((0, tile * size), (tile * size, (tile + 1) * size)):
            if start == stop:
                continue
            keys = pairs_ref[at, 0, start:stop, :]
            scores = dot(query, keys, ((1,), (1,))) * (1.0 / math.sqrt(HD))
            if start == tile * size:
                parts.append((jnp.where(allowed, scores, -1e30), allowed, at, start, stop))
            else:
                parts.append((scores, None, at, start, stop))
    highest = parts[0][0].max(axis=1, keepdims=True)
    for part in parts[1:]:
        highest = jnp.maximum(highest, part[0].max(axis=1, keepdims=True))
    totals = jnp.zeros((size, 1), F32)
    weighted = jnp.zeros((size, HD), F32)
    for scores, allowed, at, start, stop in parts:
        probs = jnp.exp(scores - highest)
        if allowed is not None:
            probs = jnp.where(allowed, probs, 0.0)
        totals = totals + probs.sum(axis=1, keepdims=True)
        values = pairs_ref[at, 1, start:stop, :]
        weighted = weighted + dot(probs.astype(BF16), values, ((1,), (0,)))
    some = totals > 0.0
    totals = jnp.maximum(totals, 1e-30)
    return weighted / totals, jnp.where(some, highest + jnp.log(totals), -1e30)


def other_kernel(rows, few, delta_ref, query_ref, pairs_ref, out_ref, log_ref):
    own_rows = query_ref.shape[0]
    log_ref[...] = jnp.zeros_like(log_ref)
    for tile in range(own_rows // 128):
        out, log = attend(delta_ref[0], query_ref, pairs_ref, tile, few, rows)
        out_ref[tile * 128 : (tile + 1) * 128, :] = out.astype(BF16)
        line = jnp.broadcast_to(log, (128, 128)).T[:8]
        first = line.astype(BF16).astype(F32)
        second = (line - first).astype(BF16).astype(F32)
        third = line - first - second
        for at, term in enumerate((first, second, third)):
            log_ref[at * 8 + tile : at * 8 + tile + 1, :] = term[:1]
    out_ref[own_rows:, :] = log_ref[...].astype(BF16)


def own_kernel(rows, few, delta_ref, query_ref, pairs_ref, out_ref, log_ref):
    for tile in range(query_ref.shape[0] // 128):
        span = slice(tile * 128, (tile + 1) * 128)
        out, log = attend(delta_ref[0], query_ref, pairs_ref, tile, few, rows)
        out_ref[span, :] = out
        log_ref[span, :] = jnp.broadcast_to(log, (128, 128))


def merge_kernel(few, own_ref, log_ref, got_ref, long_ref, out_ref):
    own_rows = own_ref.shape[0]
    per = 128 // (2 * few)
    logs = got_ref[own_rows:, :].astype(F32)
    for tile in range(own_rows // 128):
        span = slice(tile * 128, (tile + 1) * 128)
        log = log_ref[span, :]
        line = logs[tile : tile + 1] + logs[8 + tile : 9 + tile] + logs[16 + tile : 17 + tile]
        got_log = jnp.broadcast_to(line, (128, 128)).T
        highest = jnp.maximum(log, got_log)
        own_share, got_share = jnp.exp(log - highest), jnp.exp(got_log - highest)
        merged = own_ref[span, :] * own_share + got_ref[span, :].astype(F32) * got_share
        merged = (merged / (own_share + got_share)).astype(BF16).reshape(per, 2 * few, HD)
        for x_at in range(2):
            out_ref[tile * per : (tile + 1) * per, x_at, : 2 * few, :] = merged
    out_ref[:, :, 2 * few :, :] = long_ref[...]


def project_kernel(heads, few, back_ref, weight_ref, out_ref):
    n_seq = back_ref.shape[0]
    chunks = n_seq // heads
    n_z, n_tp, channels, wide = weight_ref.shape
    blocks = []
    for x_at in range(2):
        columns = [
            back_ref[head * chunks : (head + 1) * chunks, x_at * few : (x_at + 1) * few, :].reshape(
                chunks * few, HD
            )
            for head in range(heads)
        ]
        blocks.append(jnp.concatenate(columns, axis=1))
    whole = jnp.concatenate(blocks, axis=0)
    for at in range(n_tp):
        part = weight_ref[:, at].reshape(n_z * channels, wide)
        out = dot(whole, part, ((1,), (1,))).astype(BF16)
        for x_at in range(2):
            out_ref[x_at, at] = out[x_at * chunks * few : (x_at + 1) * chunks * few]


def split_kernel(few, mixed_ref, pairs_ref, query_ref):
    n_seq = mixed_ref.shape[0]
    query_ref[...] = mixed_ref[:, :few, :].reshape(n_seq * few, HD)
    for at in range(2):
        block = mixed_ref[:, (at + 1) * few : (at + 2) * few, :].reshape(n_seq * few, HD)
        for to in range(pairs_ref.shape[0]):
            pairs_ref[to, at] = block


def gate_kernel(start, back_ref, gate_ref, tail_ref, taps_ref, out_ref):
    rows = gate_ref.shape[0]
    lanes = 128
    per = lanes // (back_ref.shape[1] - start)
    row = lax.broadcasted_iota(jnp.int32, (rows, lanes), 0)
    for group in range(gate_ref.shape[1] // lanes):
        span = slice(group * lanes, (group + 1) * lanes)
        x = gate_ref[:, span].astype(F32)
        tail = tail_ref[:, span].astype(F32)
        one = jnp.where(row == 0, tail[1:2], pltpu.roll(x, 1, 0))
        two = jnp.where(row == 0, tail[0:1], jnp.where(row == 1, tail[1:2], pltpu.roll(x, 2, 0)))
        short = (
            taps_ref[1, 0:1, span] * x + taps_ref[1, 1:2, span] * one + taps_ref[1, 2:3, span] * two
        )
        rows_long = back_ref[group * per : (group + 1) * per, start:, :].astype(F32)
        out_ref[:, span] = (short * rows_long.reshape(lanes, rows).T).astype(BF16)


def unite_kernel(channels, parts_ref, out_ref):
    n_tp = parts_ref.shape[0] // 2
    rows, lanes = parts_ref.shape[1], 128
    sums = []
    for x_at in range(2):
        total = parts_ref[x_at * n_tp].astype(F32)
        for at in range(1, n_tp):
            total = total + parts_ref[x_at * n_tp + at].astype(F32)
        sums.append(total)
    lane = lax.broadcasted_iota(jnp.int32, (rows, lanes), 1)
    for group in range(out_ref.shape[1] // lanes):
        span = slice(group // 2 * lanes, (group // 2 + 1) * lanes)
        start = group % 2 * 2 * channels
        even, odd = sums[0][:, span], sums[1][:, span]

        def moved(x, by):
            by = by % lanes
            return pltpu.roll(x, by, 1) if by else x

        low = jnp.where(lane < channels, moved(even, -start), moved(odd, channels - start))
        high = jnp.where(
            lane < 3 * channels, moved(even, channels - start), moved(odd, 2 * channels - start)
        )
        out_ref[:, group * lanes : (group + 1) * lanes] = jnp.where(
            lane < 2 * channels, low, high
        ).astype(BF16)


def body(
    first_stream,
    gate_stream,
    value_stream,
    short_taps,
    long_filter,
    skip_gain,
    queries,
    attn_keys,
    attn_values,
    out_weight,
):
    seq = ("zi", "zp", "zq", "xh")
    n_seq, n_x, n_tp = lax.axis_size(seq), lax.axis_size("xh"), lax.axis_size("tp")
    n_pair = lax.axis_size("zq") * n_x
    n_z = n_seq // n_x
    n_plane = n_x * n_tp
    seq_at = lax.axis_index(seq)
    half_at = lax.axis_index("zp")
    pair_at = lax.axis_index(("zq", "xh"))
    rows = queries.shape[1]
    wide = queries.shape[2]
    channels = long_filter.shape[3]
    heads = wide // HD
    chunks = n_seq // heads
    few = rows // chunks
    own_rows = n_seq * few
    taps = short_taps[0]

    weight = out_weight[0].transpose(1, 2, 0).reshape(-1, wide)
    weight = lax.all_gather(weight, ("zi", "zp", "zq"))

    packed = kernel_call(
        pack_kernel,
        jax.ShapeDtypeStruct((n_seq, 3 * few + channels + 8, rows), BF16),
        (),
        (first_stream[0], value_stream[0], taps, queries[0], attn_keys[0], attn_values[0]),
    )
    mixed = lax.all_to_all(packed, seq, 0, 0)

    tail = lax.ppermute(gate_stream[0, -2:], seq, [(i, i + 1) for i in range(n_seq - 1)])
    mixed, tail = lax.optimization_barrier((mixed, tail))
    tables = transform_tables(n_seq, rows)
    kernel = long_filter[0, 0, 0].reshape(channels, n_seq, rows).transpose(1, 0, 2)
    kernel_spec = forward_transform(kernel, tables)

    sent_pairs, query = kernel_call(
        functools.partial(split_kernel, few),
        (
            jax.ShapeDtypeStruct((n_pair, 2, own_rows, HD), BF16),
            jax.ShapeDtypeStruct((own_rows, HD), BF16),
        ),
        (),
        (mixed,),
    )
    swap = [(0, 1), (1, 0)]
    other_query = lax.ppermute(query, "zp", swap)
    pairs = lax.all_to_all(sent_pairs, ("zq", "xh"), 0, 0)

    local_taps = lax.dynamic_slice_in_dim(taps, seq_at * channels, channels, 2)
    edges = mixed[:, 3 * few + channels :, :channels]
    first_zero, first_one = edge_short(edges[:, :4], local_taps[0])
    value_zero, value_one = edge_short(edges[:, 4:], local_taps[2])
    token = lax.broadcasted_iota(jnp.int32, (1, 1, rows), 2)
    product = mixed[:, 3 * few : 3 * few + channels]
    product = jnp.where(token == 0, (first_zero * value_zero).astype(BF16)[:, :, None], product)
    product = jnp.where(token == 1, (first_one * value_one).astype(BF16)[:, :, None], product)
    product = product.astype(F32)
    spec = forward_transform(product, tables)
    real, imag = spec[:, :, :rows], spec[:, :, rows:]
    kernel_real, kernel_imag = kernel_spec[:, :, :rows], kernel_spec[:, :, rows:]
    joined = jnp.concatenate(
        [real * kernel_real - imag * kernel_imag, real * kernel_imag + imag * kernel_real], axis=2
    )
    convolved = inverse_transform(joined, tables)
    gain = lax.dynamic_slice_in_dim(skip_gain[0], seq_at * channels, channels, 0)
    long_out = (convolved + gain[None, :, None] * product).astype(BF16)

    work = 2 * own_rows * n_pair * own_rows * HD
    own_delta = -pair_at * few
    other_delta = (2 * half_at - 1) * (n_pair * few) + own_delta
    sent = kernel_call(
        functools.partial(other_kernel, rows, few),
        jax.ShapeDtypeStruct((own_rows + 32, HD), BF16),
        (other_delta.astype(jnp.int32).reshape(1),),
        (other_query, pairs),
        (pltpu.VMEM((32, HD), F32),),
        work,
    )
    got = lax.ppermute(sent, "zp", swap)
    query, sent = lax.optimization_barrier((query, sent))
    own_out, own_log = kernel_call(
        functools.partial(own_kernel, rows, few),
        (jax.ShapeDtypeStruct((own_rows, HD), F32),) * 2,
        (own_delta.astype(jnp.int32).reshape(1),),
        (query, pairs),
        (),
        work,
    )
    returned = kernel_call(
        functools.partial(merge_kernel, few),
        jax.ShapeDtypeStruct((n_z, n_x, n_x * few + channels, HD), BF16),
        (),
        (own_out, own_log, got, long_out.reshape(n_z, n_x, channels, rows)),
    )
    back = lax.all_to_all(returned.reshape(n_seq, -1, HD), seq, 0, 0)

    hyena = kernel_call(
        functools.partial(gate_kernel, n_x * few),
        jax.ShapeDtypeStruct(gate_stream.shape[1:], BF16),
        (),
        (back, gate_stream[0], tail, taps),
    )
    n_sec = lax.axis_size("section")
    handed = lax.ppermute(hyena, "section", [(i, (i + 1) % n_sec) for i in range(n_sec)])

    partials = kernel_call(
        functools.partial(project_kernel, heads, few),
        jax.ShapeDtypeStruct((n_x, n_tp, rows, n_z * channels), BF16),
        (),
        (back, weight.reshape(n_z, n_tp, channels, wide)),
        (),
        2 * n_x * rows * wide * n_seq * channels * n_tp // n_x,
    ).reshape(n_plane, rows, n_z * channels)
    partials = lax.all_to_all(partials, ("xh", "tp"), 0, 0)
    attended = kernel_call(
        functools.partial(unite_kernel, channels),
        jax.ShapeDtypeStruct(handed.shape, BF16),
        (),
        (partials,),
    )
    return (handed[None], attended[None])


def solution(mesh):
    n_sec, n_seq, n_tp = (mesh.shape[name] for name in ("section", "seq", "tp"))
    finer = Mesh(
        mesh.devices.reshape(n_sec, n_seq // 8, 2, 2, 2, n_tp),
        ("section", "zi", "zp", "zq", "xh", "tp"),
    )
    seq = ("zi", "zp", "zq", "xh")
    placed = (
        P("section", seq, "tp"),
        P("section", seq, "tp"),
        P("section", seq, "tp"),
        P("section", None, None, "tp"),
        P("section", "tp", seq, None, None),
        P("section", "tp"),
        P("section", seq, "tp"),
        P("section", seq, "tp"),
        P("section", seq, "tp"),
        P("section", "tp", None, seq),
    )
    return jax.shard_map(
        body,
        mesh=finer,
        in_specs=placed,
        out_specs=(P("section", seq, "tp"), P("section", seq, "tp")),
        check_vma=False,
    )
```

```python
import functools
import math

import jax
import jax.numpy as jnp
import numpy as np
from jax import lax
from jax.experimental import pallas as pl
from jax.experimental.pallas import tpu as pltpu
from jax.sharding import Mesh, PartitionSpec as P

HD = 128
BF16 = jnp.bfloat16
F32 = jnp.float32
HIGH = lax.Precision.HIGH


def dot(left, right, contract, precision=None):
    return lax.dot_general(
        left, right, (contract, ((), ())), precision=precision, preferred_element_type=F32
    )


def transform_tables(depth, breadth):
    full = 2 * depth
    half = depth + 1
    k = np.arange(half)
    a = np.arange(depth)
    b = np.arange(breadth)
    one = -2.0 * np.pi * np.outer(k, a) / full
    first = np.stack([np.cos(one), np.sin(one)])
    mid = -2.0 * np.pi * np.outer(k, b) / (full * breadth)
    two = -2.0 * np.pi * (np.outer(b, b) % breadth) / breadth
    cos_two, sin_two = np.cos(two), np.sin(two)
    forward = np.block([[cos_two, sin_two], [-sin_two, cos_two]])
    backward = np.block([[cos_two, -sin_two], [sin_two, cos_two]])
    weight = np.where((k == 0) | (k == depth), 1.0, 2.0) / (full * breadth)
    last = np.concatenate([np.cos(one).T * weight, np.sin(one).T * weight], axis=1)
    as32 = lambda x: np.asarray(x, np.float32)
    return as32(first), as32(np.cos(mid)), as32(np.sin(mid)), as32(forward), as32(backward), as32(last)


def forward_transform(blocks, tables):
    first, cos_mid, sin_mid, forward, _, _ = tables
    depth, channels, breadth = blocks.shape
    flat = blocks.reshape(depth, channels * breadth)
    real = dot(first[0], flat, ((1,), (0,)), HIGH).reshape(-1, channels, breadth)
    imag = dot(first[1], flat, ((1,), (0,)), HIGH).reshape(-1, channels, breadth)
    cos_mid, sin_mid = cos_mid[:, None], sin_mid[:, None]
    turned = jnp.concatenate(
        [real * cos_mid - imag * sin_mid, real * sin_mid + imag * cos_mid], axis=2
    )
    return dot(turned, forward, ((2,), (0,)), HIGH)


def inverse_transform(spectrum, tables):
    _, cos_mid, sin_mid, _, backward, last = tables
    half, channels, twice = spectrum.shape
    breadth = twice // 2
    mid = dot(spectrum, backward, ((2,), (0,)), HIGH)
    real, imag = mid[:, :, :breadth], mid[:, :, breadth:]
    cos_mid, sin_mid = cos_mid[:, None], sin_mid[:, None]
    turned = jnp.concatenate(
        [real * cos_mid + imag * sin_mid, imag * cos_mid - real * sin_mid], axis=0
    )
    out = dot(last, turned.reshape(2 * half, channels * breadth), ((1,), (0,)), HIGH)
    return out.reshape(-1, channels, breadth)


def kernel_call(kernel, out_shape, scalars, arrays, scratch=(), flops=0, grant=32):
    in_specs = [pl.BlockSpec(memory_space=pltpu.SMEM)] * len(scalars)
    in_specs += [pl.BlockSpec(memory_space=pltpu.VMEM)] * len(arrays)
    outs = out_shape if isinstance(out_shape, tuple) else (out_shape,)
    moved = sum(x.size * x.dtype.itemsize for x in (*arrays, *outs))
    return pl.pallas_call(
        kernel,
        out_shape=out_shape,
        in_specs=in_specs,
        out_specs=jax.tree.map(lambda _: pl.BlockSpec(memory_space=pltpu.VMEM), out_shape),
        scratch_shapes=list(scratch),
        compiler_params=pltpu.CompilerParams(vmem_limit_bytes=grant * 1024 * 1024),
        cost_estimate=pl.CostEstimate(flops=flops, bytes_accessed=moved, transcendentals=0),
    )(*scalars, *arrays)


def pack_kernel(first_ref, value_ref, taps_ref, query_ref, key_ref, value_head_ref, out_ref):
    n_seq, _, lanes = out_ref.shape
    rows, wide = query_ref.shape
    heads = wide // HD
    chunks = n_seq // heads
    few = rows // chunks
    per = n_seq * lanes // first_ref.shape[1]
    channels = lanes // per
    for at, ref in enumerate((query_ref, key_ref, value_head_ref)):
        for head in range(heads):
            block = ref[:, head * HD : (head + 1) * HD].reshape(chunks, few, HD)
            out_ref[head * chunks : (head + 1) * chunks, at * few : (at + 1) * few, :] = block
    for group in range(n_seq // per):
        span = slice(group * lanes, (group + 1) * lanes)
        shorts, edges = [], []
        for ref, which in ((first_ref, 0), (value_ref, 2)):
            x = ref[:, span].astype(F32)
            shorts.append(
                taps_ref[0, which, 0:1, span] * x
                + taps_ref[0, which, 1:2, span] * pltpu.roll(x, 1, 0)
                + taps_ref[0, which, 2:3, span] * pltpu.roll(x, 2, 0)
            )
            edges += [x[:2], x[rows - 2 :]]
        turned = (shorts[0] * shorts[1]).T.astype(BF16).reshape(per, channels, rows)
        out_ref[group * per : (group + 1) * per, 3 * few : 3 * few + channels, :] = turned
        edges = jnp.concatenate(edges, axis=0)
        for at in range(per):
            edge = pltpu.roll(edges, lanes - at * channels, 1) if at else edges
            out_ref[group * per + at, 3 * few + channels :, :] = edge.astype(BF16)


def attend(delta, query_ref, pairs_ref, tile, few, rows):
    size = 128
    query = query_ref[tile * size : (tile + 1) * size, :]
    row = lax.broadcasted_iota(jnp.int32, (size, size), 0)
    column = lax.broadcasted_iota(jnp.int32, (size, size), 1)
    q_pos = row // few * rows + row % few
    k_pos = column // few * rows + column % few
    parts = []
    for at in range(pairs_ref.shape[0]):
        allowed = k_pos + (at * few + delta) <= q_pos
        for start, stop in ((0, tile * size), (tile * size, (tile + 1) * size)):
            if start == stop:
                continue
            keys = pairs_ref[at, 0, start:stop, :]
            scores = dot(query, keys, ((1,), (1,))) * (1.0 / math.sqrt(HD))
            if start == tile * size:
                parts.append((jnp.where(allowed, scores, -1e30), allowed, at, start, stop))
            else:
                parts.append((scores, None, at, start, stop))
    highest = parts[0][0].max(axis=1, keepdims=True)
    for part in parts[1:]:
        highest = jnp.maximum(highest, part[0].max(axis=1, keepdims=True))
    totals = jnp.zeros((size, 1), F32)
    weighted = jnp.zeros((size, HD), F32)
    for scores, allowed, at, start, stop in parts:
        probs = jnp.exp(scores - highest)
        if allowed is not None:
            probs = jnp.where(allowed, probs, 0.0)
        totals = totals + probs.sum(axis=1, keepdims=True)
        values = pairs_ref[at, 1, start:stop, :]
        weighted = weighted + dot(probs.astype(BF16), values, ((1,), (0,)))
    some = totals > 0.0
    totals = jnp.maximum(totals, 1e-30)
    return weighted / totals, jnp.where(some, highest + jnp.log(totals), -1e30)


def other_kernel(rows, few, delta_ref, query_ref, pairs_ref, out_ref, log_ref):
    own_rows = query_ref.shape[0]
    log_ref[...] = jnp.zeros_like(log_ref)
    for tile in range(own_rows // 128):
        out, log = attend(delta_ref[0], query_ref, pairs_ref, tile, few, rows)
        out_ref[tile * 128 : (tile + 1) * 128, :] = out.astype(BF16)
        line = jnp.broadcast_to(log, (128, 128)).T[:8]
        first = line.astype(BF16).astype(F32)
        second = (line - first).astype(BF16).astype(F32)
        third = line - first - second
        for at, term in enumerate((first, second, third)):
            log_ref[at * 8 + tile : at * 8 + tile + 1, :] = term[:1]
    out_ref[own_rows:, :] = log_ref[...].astype(BF16)


def own_kernel(rows, few, delta_ref, query_ref, pairs_ref, out_ref, log_ref):
    for tile in range(query_ref.shape[0] // 128):
        span = slice(tile * 128, (tile + 1) * 128)
        out, log = attend(delta_ref[0], query_ref, pairs_ref, tile, few, rows)
        out_ref[span, :] = out
        log_ref[span, :] = jnp.broadcast_to(log, (128, 128))


def merge_kernel(few, own_ref, log_ref, got_ref, long_ref, out_ref):
    own_rows = own_ref.shape[0]
    per = 128 // (2 * few)
    logs = got_ref[own_rows:, :].astype(F32)
    for tile in range(own_rows // 128):
        span = slice(tile * 128, (tile + 1) * 128)
        log = log_ref[span, :]
        line = logs[tile : tile + 1] + logs[8 + tile : 9 + tile] + logs[16 + tile : 17 + tile]
        got_log = jnp.broadcast_to(line, (128, 128)).T
        highest = jnp.maximum(log, got_log)
        own_share, got_share = jnp.exp(log - highest), jnp.exp(got_log - highest)
        merged = own_ref[span, :] * own_share + got_ref[span, :].astype(F32) * got_share
        merged = (merged / (own_share + got_share)).astype(BF16).reshape(per, 2 * few, HD)
        for x_at in range(2):
            out_ref[tile * per : (tile + 1) * per, x_at, : 2 * few, :] = merged
    out_ref[:, :, 2 * few :, :] = long_ref[...]


def project_kernel(heads, few, back_ref, weight_ref, out_ref):
    n_seq = back_ref.shape[0]
    chunks = n_seq // heads
    n_z, n_tp, channels, wide = weight_ref.shape
    blocks = []
    for x_at in range(2):
        columns = [
            back_ref[head * chunks : (head + 1) * chunks, x_at * few : (x_at + 1) * few, :].reshape(
                chunks * few, HD
            )
            for head in range(heads)
        ]
        blocks.append(jnp.concatenate(columns, axis=1))
    whole = jnp.concatenate(blocks, axis=0)
    for at in range(n_tp):
        part = weight_ref[:, at].reshape(n_z * channels, wide)
        out = dot(whole, part, ((1,), (1,))).astype(BF16)
        for x_at in range(2):
            out_ref[x_at, at] = out[x_at * chunks * few : (x_at + 1) * chunks * few]


def split_kernel(few, mixed_ref, pairs_ref, query_ref):
    n_seq = mixed_ref.shape[0]
    query_ref[...] = mixed_ref[:, :few, :].reshape(n_seq * few, HD)
    for at in range(2):
        block = mixed_ref[:, (at + 1) * few : (at + 2) * few, :].reshape(n_seq * few, HD)
        for to in range(pairs_ref.shape[0]):
            pairs_ref[to, at] = block


def product_kernel(start, mixed_ref, taps_ref, out_ref):
    n_seq, channels, rows = out_ref.shape
    count = n_seq * 8
    edges = mixed_ref[:, start + channels :, :].astype(F32).reshape(count, rows).T[:channels]
    lane = lax.broadcasted_iota(jnp.int32, (channels, count), 1)
    kind = lane % 8
    before = jnp.where(lane >= 8, 1.0, 0.0)
    ahead = jnp.where(kind % 4 == 0, pltpu.roll(edges, 5, 1) * before, pltpu.roll(edges, 1, 1))
    further = pltpu.roll(edges, 6, 1) * before
    tap = [jnp.where(kind < 4, taps_ref[:, i : i + 1], taps_ref[:, 6 + i : 7 + i]) for i in range(3)]
    short = tap[0] * edges + tap[1] * ahead + tap[2] * further
    made = (short * pltpu.roll(short, count - 4, 1)).astype(BF16).astype(F32)
    column = lax.broadcasted_iota(jnp.int32, (channels, rows), 1)
    for at in range(n_seq):
        turned = pltpu.roll(made, count - 8 * at, 1) if at else made
        block = mixed_ref[at, start : start + channels, :].astype(F32)
        out_ref[at] = jnp.where(column < 2, turned[:, :rows], block)


def gate_kernel(start, back_ref, gate_ref, tail_ref, taps_ref, out_ref):
    rows = gate_ref.shape[0]
    lanes = 128
    per = lanes // (back_ref.shape[1] - start)
    row = lax.broadcasted_iota(jnp.int32, (rows, lanes), 0)
    for group in range(gate_ref.shape[1] // lanes):
        span = slice(group * lanes, (group + 1) * lanes)
        x = gate_ref[:, span].astype(F32)
        tail = tail_ref[:, span].astype(F32)
        one = jnp.where(row == 0, tail[1:2], pltpu.roll(x, 1, 0))
        two = jnp.where(row == 0, tail[0:1], jnp.where(row == 1, tail[1:2], pltpu.roll(x, 2, 0)))
        short = (
            taps_ref[0:1, span] * x + taps_ref[1:2, span] * one + taps_ref[2:3, span] * two
        )
        rows_long = back_ref[group * per : (group + 1) * per, start:, :].astype(F32)
        out_ref[:, span] = (short * rows_long.reshape(lanes, rows).T).astype(BF16)


def unite_kernel(channels, parts_ref, out_ref):
    n_tp = parts_ref.shape[0] // 2
    rows, lanes = parts_ref.shape[1], 128
    sums = []
    for x_at in range(2):
        total = parts_ref[x_at * n_tp].astype(F32)
        for at in range(1, n_tp):
            total = total + parts_ref[x_at * n_tp + at].astype(F32)
        sums.append(total)
    lane = lax.broadcasted_iota(jnp.int32, (rows, lanes), 1)
    for group in range(out_ref.shape[1] // lanes):
        span = slice(group // 2 * lanes, (group // 2 + 1) * lanes)
        start = group % 2 * 2 * channels
        even, odd = sums[0][:, span], sums[1][:, span]

        def moved(x, by):
            by = by % lanes
            return pltpu.roll(x, by, 1) if by else x

        low = jnp.where(lane < channels, moved(even, -start), moved(odd, channels - start))
        high = jnp.where(
            lane < 3 * channels, moved(even, channels - start), moved(odd, 2 * channels - start)
        )
        out_ref[:, group * lanes : (group + 1) * lanes] = jnp.where(
            lane < 2 * channels, low, high
        ).astype(BF16)


def body(
    first_stream,
    gate_stream,
    value_stream,
    short_taps,
    long_filter,
    skip_gain,
    queries,
    attn_keys,
    attn_values,
    out_weight,
):
    seq = ("zi", "zp", "zq", "xh")
    n_seq, n_x, n_tp = lax.axis_size(seq), lax.axis_size("xh"), lax.axis_size("tp")
    n_pair = lax.axis_size("zq") * n_x
    n_z = n_seq // n_x
    n_plane = n_x * n_tp
    seq_at = lax.axis_index(seq)
    half_at = lax.axis_index("zp")
    pair_at = lax.axis_index(("zq", "xh"))
    rows = queries.shape[1]
    wide = queries.shape[2]
    channels = long_filter.shape[3]
    heads = wide // HD
    chunks = n_seq // heads
    few = rows // chunks
    own_rows = n_seq * few
    taps = short_taps[0]

    weight = out_weight[0].transpose(1, 2, 0).reshape(-1, wide)
    weight = lax.all_gather(weight, ("zi", "zp", "zq"))

    packed = kernel_call(
        pack_kernel,
        jax.ShapeDtypeStruct((n_seq, 3 * few + channels + 8, rows), BF16),
        (),
        (first_stream[0], value_stream[0], short_taps, queries[0], attn_keys[0], attn_values[0]),
        grant=56,
    )
    mixed = lax.all_to_all(packed, seq, 0, 0)

    n_sec = lax.axis_size("section")
    onward = [(i, (i + 1) % n_sec) for i in range(n_sec)]
    gate = lax.ppermute(gate_stream[0], "section", onward)
    gate_taps = lax.ppermute(taps[1], "section", onward)
    tail = lax.ppermute(
        gate_stream[0, -2:],
        ("section",) + seq,
        [(s * n_seq + i, t * n_seq + i + 1) for s, t in onward for i in range(n_seq - 1)],
    )
    local_taps = lax.dynamic_slice_in_dim(taps, seq_at * channels, channels, 2)
    local_taps = local_taps.reshape(9, channels).T
    mixed, gate, gate_taps, tail = lax.optimization_barrier((mixed, gate, gate_taps, tail))
    tables = transform_tables(n_seq, rows)
    kernel = long_filter[0, 0, 0].reshape(channels, n_seq, rows).transpose(1, 0, 2)
    kernel_spec = forward_transform(kernel, tables)

    sent_pairs, query = kernel_call(
        functools.partial(split_kernel, few),
        (
            jax.ShapeDtypeStruct((n_pair, 2, own_rows, HD), BF16),
            jax.ShapeDtypeStruct((own_rows, HD), BF16),
        ),
        (),
        (mixed,),
    )
    swap = [(0, 1), (1, 0)]
    other_query = lax.ppermute(query, "zp", swap)
    pairs = lax.all_to_all(sent_pairs, ("zq", "xh"), 0, 0)

    product = kernel_call(
        functools.partial(product_kernel, 3 * few),
        jax.ShapeDtypeStruct((n_seq, channels, rows), F32),
        (),
        (mixed, local_taps),
    )
    spec = forward_transform(product, tables)
    spec, other_query = lax.optimization_barrier((spec, other_query))
    real, imag = spec[:, :, :rows], spec[:, :, rows:]
    kernel_real, kernel_imag = kernel_spec[:, :, :rows], kernel_spec[:, :, rows:]
    joined = jnp.concatenate(
        [real * kernel_real - imag * kernel_imag, real * kernel_imag + imag * kernel_real], axis=2
    )
    convolved = inverse_transform(joined, tables)
    gain = lax.dynamic_slice_in_dim(skip_gain[0], seq_at * channels, channels, 0)
    long_out = (convolved + gain[None, :, None] * product).astype(BF16)
    long_out = lax.ppermute(long_out, "section", onward)

    work = 2 * own_rows * n_pair * own_rows * HD
    own_delta = -pair_at * few
    other_delta = (2 * half_at - 1) * (n_pair * few) + own_delta
    sent = kernel_call(
        functools.partial(other_kernel, rows, few),
        jax.ShapeDtypeStruct((own_rows + 32, HD), BF16),
        (other_delta.astype(jnp.int32).reshape(1),),
        (other_query, pairs),
        (pltpu.VMEM((32, HD), F32),),
        work,
    )
    got = lax.ppermute(sent, "zp", swap)
    query, sent = lax.optimization_barrier((query, sent))
    own_out, own_log = kernel_call(
        functools.partial(own_kernel, rows, few),
        (jax.ShapeDtypeStruct((own_rows, HD), F32),) * 2,
        (own_delta.astype(jnp.int32).reshape(1),),
        (query, pairs),
        (),
        work,
    )
    returned = kernel_call(
        functools.partial(merge_kernel, few),
        jax.ShapeDtypeStruct((n_z, n_x, n_x * few + channels, HD), BF16),
        (),
        (own_out, own_log, got, long_out.reshape(n_z, n_x, channels, rows)),
    )
    back = lax.all_to_all(returned.reshape(n_seq, -1, HD), seq, 0, 0)

    handed = kernel_call(
        functools.partial(gate_kernel, n_x * few),
        jax.ShapeDtypeStruct(gate_stream.shape[1:], BF16),
        (),
        (back, gate, tail, gate_taps),
    )

    partials = kernel_call(
        functools.partial(project_kernel, heads, few),
        jax.ShapeDtypeStruct((n_x, n_tp, rows, n_z * channels), BF16),
        (),
        (back, weight.reshape(n_z, n_tp, channels, wide)),
        (),
        2 * n_x * rows * wide * n_seq * channels * n_tp // n_x,
        56,
    ).reshape(n_plane, rows, n_z * channels)
    partials = lax.all_to_all(partials, ("xh", "tp"), 0, 0)
    attended = kernel_call(
        functools.partial(unite_kernel, channels),
        jax.ShapeDtypeStruct(handed.shape, BF16),
        (),
        (partials,),
    )
    return (handed[None], attended[None])


def solution(mesh):
    n_sec, n_seq, n_tp = (mesh.shape[name] for name in ("section", "seq", "tp"))
    finer = Mesh(
        mesh.devices.reshape(n_sec, n_seq // 8, 2, 2, 2, n_tp),
        ("section", "zi", "zp", "zq", "xh", "tp"),
    )
    seq = ("zi", "zp", "zq", "xh")
    placed = (
        P("section", seq, "tp"),
        P("section", seq, "tp"),
        P("section", seq, "tp"),
        P("section", None, None, "tp"),
        P("section", "tp", seq, None, None),
        P("section", "tp"),
        P("section", seq, "tp"),
        P("section", seq, "tp"),
        P("section", seq, "tp"),
        P("section", "tp", None, seq),
    )
    return jax.shard_map(
        body,
        mesh=finer,
        in_specs=placed,
        out_specs=(P("section", seq, "tp"), P("section", seq, "tp")),
        check_vma=False,
    )
```

```python
import functools
import math

import jax
import jax.numpy as jnp
import numpy as np
from jax import lax
from jax.experimental import pallas as pl
from jax.experimental.pallas import tpu as pltpu
from jax.sharding import Mesh, PartitionSpec as P

HD = 128
BF16 = jnp.bfloat16
F32 = jnp.float32
HIGH = lax.Precision.HIGH


def dot(left, right, contract, precision=None):
    return lax.dot_general(
        left, right, (contract, ((), ())), precision=precision, preferred_element_type=F32
    )


def transform_tables(depth, breadth):
    full = 2 * depth
    half = depth + 1
    k = np.arange(half)
    a = np.arange(depth)
    b = np.arange(breadth)
    one = -2.0 * np.pi * np.outer(k, a) / full
    first = np.stack([np.cos(one), np.sin(one)])
    mid = -2.0 * np.pi * np.outer(k, b) / (full * breadth)
    two = -2.0 * np.pi * (np.outer(b, b) % breadth) / breadth
    cos_two, sin_two = np.cos(two), np.sin(two)
    forward = np.block([[cos_two, sin_two], [-sin_two, cos_two]])
    backward = np.block([[cos_two, -sin_two], [sin_two, cos_two]])
    weight = np.where((k == 0) | (k == depth), 1.0, 2.0) / (full * breadth)
    last = np.concatenate([np.cos(one).T * weight, np.sin(one).T * weight], axis=1)
    as32 = lambda x: np.asarray(x, np.float32)
    return as32(first), as32(np.cos(mid)), as32(np.sin(mid)), as32(forward), as32(backward), as32(last)


def forward_transform(blocks, tables):
    first, cos_mid, sin_mid, forward, _, _ = tables
    depth, channels, breadth = blocks.shape
    flat = blocks.reshape(depth, channels * breadth)
    real = dot(first[0], flat, ((1,), (0,)), HIGH).reshape(-1, channels, breadth)
    imag = dot(first[1], flat, ((1,), (0,)), HIGH).reshape(-1, channels, breadth)
    cos_mid, sin_mid = cos_mid[:, None], sin_mid[:, None]
    turned = jnp.concatenate(
        [real * cos_mid - imag * sin_mid, real * sin_mid + imag * cos_mid], axis=2
    )
    return dot(turned, forward, ((2,), (0,)), HIGH)


def inverse_transform(spectrum, tables):
    _, cos_mid, sin_mid, _, backward, last = tables
    half, channels, twice = spectrum.shape
    breadth = twice // 2
    mid = dot(spectrum, backward, ((2,), (0,)), HIGH)
    real, imag = mid[:, :, :breadth], mid[:, :, breadth:]
    cos_mid, sin_mid = cos_mid[:, None], sin_mid[:, None]
    turned = jnp.concatenate(
        [real * cos_mid + imag * sin_mid, imag * cos_mid - real * sin_mid], axis=0
    )
    out = dot(last, turned.reshape(2 * half, channels * breadth), ((1,), (0,)), HIGH)
    return out.reshape(-1, channels, breadth)


def kernel_call(kernel, out_shape, scalars, arrays, scratch=(), flops=0, grant=32):
    in_specs = [pl.BlockSpec(memory_space=pltpu.SMEM)] * len(scalars)
    in_specs += [pl.BlockSpec(memory_space=pltpu.VMEM)] * len(arrays)
    outs = out_shape if isinstance(out_shape, tuple) else (out_shape,)
    moved = sum(x.size * x.dtype.itemsize for x in (*arrays, *outs))
    return pl.pallas_call(
        kernel,
        out_shape=out_shape,
        in_specs=in_specs,
        out_specs=jax.tree.map(lambda _: pl.BlockSpec(memory_space=pltpu.VMEM), out_shape),
        scratch_shapes=list(scratch),
        compiler_params=pltpu.CompilerParams(vmem_limit_bytes=grant * 1024 * 1024),
        cost_estimate=pl.CostEstimate(flops=flops, bytes_accessed=moved, transcendentals=0),
    )(*scalars, *arrays)


def pack_kernel(x_ref, first_ref, value_ref, taps_ref, query_ref, key_ref, value_head_ref, weight_ref, rows_ref, own_ref, other_ref):
    n_tp = rows_ref.shape[0]
    rows = query_ref.shape[0]
    part = rows // n_tp
    for at, ref in enumerate((query_ref, key_ref, value_head_ref)):
        rows_ref[:, at * part : (at + 1) * part, :] = ref[...].reshape(n_tp, part, -1)
    rows_ref[:, 3 * part :, :] = weight_ref[...]
    n_z, _, lanes = own_ref.shape
    per = 2 * n_z * lanes // first_ref.shape[1]
    channels = lanes // per
    low = x_ref[0] == 0
    for group in range(2 * n_z // per):
        span = slice(group * lanes, (group + 1) * lanes)
        shorts, edges = [], []
        for ref, which in ((first_ref, 0), (value_ref, 2)):
            x = ref[:, span].astype(F32)
            shorts.append(
                taps_ref[0, which, 0:1, span] * x
                + taps_ref[0, which, 1:2, span] * pltpu.roll(x, 1, 0)
                + taps_ref[0, which, 2:3, span] * pltpu.roll(x, 2, 0)
            )
            edges += [x[:2], x[rows - 2 :]]
        turned = (shorts[0] * shorts[1]).T
        edges = jnp.concatenate(edges, axis=0)
        for at in range(per // 2):
            z_at = group * per // 2 + at
            blocks = []
            for x_at in range(2):
                j = 2 * at + x_at
                edge = pltpu.roll(edges, lanes - j * channels, 1) if j else edges
                blocks.append(jnp.concatenate([turned[j * channels : (j + 1) * channels], edge], axis=0))
            own_ref[z_at] = jnp.where(low, blocks[0], blocks[1]).astype(BF16)
            other_ref[z_at] = jnp.where(low, blocks[1], blocks[0]).astype(BF16)


def repack_kernel(x_ref, rows_ref, own_ref, got_ref, out_ref, weight_ref):
    n_tp, height, wide = rows_ref.shape
    channels = weight_ref.shape[1]
    size = height - channels
    heads = wide // HD
    for at in range(n_tp):
        for head in range(heads):
            block = rows_ref[at, :size, head * HD : (head + 1) * HD]
            out_ref[at * heads + head, :size, :] = block
    weight_ref[...] = rows_ref[:, size:, :]
    low = x_ref[0] == 0
    own, got = own_ref[...].astype(F32), got_ref[...].astype(F32)
    even = jnp.where(low, own, got).astype(BF16)
    odd = jnp.where(low, got, own).astype(BF16)
    out_ref[:, size : size + channels, :] = even[:, :channels]
    out_ref[:, size + channels : size + 2 * channels, :] = odd[:, :channels]
    out_ref[:, size + 2 * channels : size + 2 * channels + 8, :] = even[:, channels:]
    out_ref[:, size + 2 * channels + 8 :, :] = odd[:, channels:]


def split_kernel(part, mixed_ref, pairs_ref, query_ref):
    n_z = mixed_ref.shape[0]
    query_ref[...] = mixed_ref[:, :part, :].reshape(n_z * part, HD)
    for at in range(2):
        block = mixed_ref[:, (at + 1) * part : (at + 2) * part, :].reshape(n_z * part, HD)
        for to in range(pairs_ref.shape[0]):
            pairs_ref[to, at] = block


def product_kernel(start, mixed_ref, taps_ref, out_ref):
    n_seq, channels, rows = out_ref.shape
    count = n_seq * 8
    edges = mixed_ref[:, start + 2 * channels :, :].astype(F32).reshape(count, rows).T[:channels]
    lane = lax.broadcasted_iota(jnp.int32, (channels, count), 1)
    kind = lane % 8
    before = jnp.where(lane >= 8, 1.0, 0.0)
    ahead = jnp.where(kind % 4 == 0, pltpu.roll(edges, 5, 1) * before, pltpu.roll(edges, 1, 1))
    further = pltpu.roll(edges, 6, 1) * before
    tap = [jnp.where(kind < 4, taps_ref[:, i : i + 1], taps_ref[:, 6 + i : 7 + i]) for i in range(3)]
    short = tap[0] * edges + tap[1] * ahead + tap[2] * further
    made = (short * pltpu.roll(short, count - 4, 1)).astype(BF16).astype(F32)
    column = lax.broadcasted_iota(jnp.int32, (channels, rows), 1)
    for at in range(n_seq):
        turned = pltpu.roll(made, count - 8 * at, 1) if at else made
        begin = start + at % 2 * channels
        block = mixed_ref[at // 2, begin : begin + channels, :].astype(F32)
        out_ref[at] = jnp.where(column < 2, turned[:, :rows], block)


def attend_kernel(rows, delta_ref, query_ref, pairs_ref, long_ref, out_ref):
    size = 128
    n_z, height, _ = out_ref.shape
    own_rows = query_ref.shape[0]
    part = own_rows // n_z
    per = size // part
    row = lax.broadcasted_iota(jnp.int32, (size, size), 0)
    column = lax.broadcasted_iota(jnp.int32, (size, size), 1)
    q_pos = row // part * (2 * rows) + row % part
    k_pos = column // part * (2 * rows) + column % part + delta_ref[0]
    out_ref[:, part:, :] = long_ref[...]
    for tile in range(own_rows // size):
        query = query_ref[tile * size : (tile + 1) * size, :]
        parts = []
        for at in range(pairs_ref.shape[0]):
            n_tp = pairs_ref.shape[0] // 2
            allowed = k_pos + (at // n_tp * rows + at % n_tp * part) <= q_pos
            for start, stop in ((0, tile * size), (tile * size, (tile + 1) * size)):
                if start == stop:
                    continue
                keys = pairs_ref[at, 0, start:stop, :]
                scores = dot(query, keys, ((1,), (1,))) * (1.0 / math.sqrt(HD))
                if start == tile * size:
                    parts.append((jnp.where(allowed, scores, -1e30), allowed, at, start, stop))
                else:
                    parts.append((scores, None, at, start, stop))
        highest = parts[0][0].max(axis=1, keepdims=True)
        for piece in parts[1:]:
            highest = jnp.maximum(highest, piece[0].max(axis=1, keepdims=True))
        totals = jnp.zeros((size, 1), F32)
        weighted = jnp.zeros((size, HD), F32)
        for scores, allowed, at, start, stop in parts:
            probs = jnp.exp(scores - highest)
            if allowed is not None:
                probs = jnp.where(allowed, probs, 0.0)
            totals = totals + probs.sum(axis=1, keepdims=True)
            values = pairs_ref[at, 1, start:stop, :]
            weighted = weighted + dot(probs.astype(BF16), values, ((1,), (0,)))
        out = (weighted / totals).astype(BF16).reshape(per, part, HD)
        out_ref[tile * per : (tile + 1) * per, :part, :] = out


def rows_kernel(x_ref, back_ref, rows_ref, own_ref, other_ref):
    part = rows_ref.shape[1]
    channels = own_ref.shape[1]
    for head in range(back_ref.shape[0]):
        block = back_ref[head, :part, :]
        for to in range(rows_ref.shape[0]):
            rows_ref[to, :, head * HD : (head + 1) * HD] = block
    low = x_ref[0] == 0
    even = back_ref[:, part : part + channels, :].astype(F32)
    odd = back_ref[:, part + channels :, :].astype(F32)
    own_ref[...] = jnp.where(low, even, odd).astype(BF16)
    other_ref[...] = jnp.where(low, odd, even).astype(BF16)


def gate_kernel(x_ref, own_ref, got_ref, gate_ref, tail_ref, taps_ref, out_ref):
    rows = gate_ref.shape[0]
    lanes = 128
    channels = own_ref.shape[1]
    per = lanes // channels
    row = lax.broadcasted_iota(jnp.int32, (rows, lanes), 0)
    low = x_ref[0] == 0
    for group in range(gate_ref.shape[1] // lanes):
        span = slice(group * lanes, (group + 1) * lanes)
        x = gate_ref[:, span].astype(F32)
        tail = tail_ref[:, span].astype(F32)
        one = jnp.where(row == 0, tail[1:2], pltpu.roll(x, 1, 0))
        two = jnp.where(row == 0, tail[0:1], jnp.where(row == 1, tail[1:2], pltpu.roll(x, 2, 0)))
        short = taps_ref[0:1, span] * x + taps_ref[1:2, span] * one + taps_ref[2:3, span] * two
        blocks = []
        for at in range(per // 2):
            own = own_ref[group * per // 2 + at].astype(F32)
            got = got_ref[group * per // 2 + at].astype(F32)
            blocks += [jnp.where(low, own, got), jnp.where(low, got, own)]
        out_ref[:, span] = (short * jnp.concatenate(blocks, axis=0).T).astype(BF16)


def project_kernel(x_ref, rows_ref, weight_ref, own_ref, other_ref):
    half = own_ref.shape[0]
    n_z, n_tp, channels, wide = weight_ref.shape
    part = rows_ref.shape[1]
    whole = rows_ref[...].reshape(2 * half, n_tp * wide)
    out = jnp.zeros((2 * half, n_z * channels), F32)
    for at in range(n_tp):
        block = weight_ref[:, at].reshape(n_z * channels, wide)
        out = out + dot(whole[:, at * wide : (at + 1) * wide], block, ((1,), (1,)))
    low = x_ref[0] == 0
    own_ref[...] = jnp.where(low, out[:half], out[half:]).astype(BF16)
    other_ref[...] = jnp.where(low, out[half:], out[:half]).astype(BF16)


def unite_kernel(channels, x_ref, own_ref, got_ref, out_ref):
    rows, lanes = own_ref.shape[0], 128
    low = x_ref[0] == 0
    lane = lax.broadcasted_iota(jnp.int32, (rows, lanes), 1)
    for group in range(out_ref.shape[1] // lanes):
        span = slice(group // 2 * lanes, (group // 2 + 1) * lanes)
        start = group % 2 * 2 * channels
        own, got = own_ref[:, span].astype(F32), got_ref[:, span].astype(F32)
        even, odd = jnp.where(low, own, got), jnp.where(low, got, own)

        def moved(x, by):
            by = by % lanes
            return pltpu.roll(x, by, 1) if by else x

        left = jnp.where(lane < channels, moved(even, -start), moved(odd, channels - start))
        right = jnp.where(
            lane < 3 * channels, moved(even, channels - start), moved(odd, 2 * channels - start)
        )
        out_ref[:, group * lanes : (group + 1) * lanes] = jnp.where(
            lane < 2 * channels, left, right
        ).astype(BF16)


def body(
    first_stream,
    gate_stream,
    value_stream,
    short_taps,
    long_filter,
    skip_gain,
    queries,
    attn_keys,
    attn_values,
    out_weight,
):
    seq = ("z", "xh")
    n_z, n_x, n_tp = lax.axis_size("z"), lax.axis_size("xh"), lax.axis_size("tp")
    n_seq, n_plane = n_z * n_x, n_x * n_tp
    seq_at = lax.axis_index(seq)
    x_at = lax.axis_index("xh")
    x_scalar = x_at.astype(jnp.int32).reshape(1)
    rows = queries.shape[1]
    wide = queries.shape[2]
    channels = long_filter.shape[3]
    part = rows // n_tp
    own_rows = n_z * part
    taps = short_taps[0]
    swap = [(0, 1), (1, 0)]
    shape = jax.ShapeDtypeStruct

    sent_rows, own, other = kernel_call(
        pack_kernel,
        (
            shape((n_tp, 3 * part + channels, wide), BF16),
            shape((n_z, channels + 8, rows), BF16),
            shape((n_z, channels + 8, rows), BF16),
        ),
        (x_scalar,),
        (
            first_stream[0],
            value_stream[0],
            short_taps,
            queries[0],
            attn_keys[0],
            attn_values[0],
            out_weight[0].transpose(1, 2, 0),
        ),
        grant=56,
    )
    got = lax.ppermute(other, "xh", swap)
    got_rows = lax.all_to_all(sent_rows, "tp", 0, 0)
    packed, weight = kernel_call(
        repack_kernel,
        (
            shape((n_z, 3 * part + 2 * channels + 16, HD), BF16),
            shape((n_tp, channels, wide), BF16),
        ),
        (x_scalar,),
        (got_rows, own, got),
    )
    mixed = lax.all_to_all(packed, "z", 0, 0)
    weight = lax.all_gather(weight, "z")

    n_sec = lax.axis_size("section")
    onward = [(i, (i + 1) % n_sec) for i in range(n_sec)]
    gate = lax.ppermute(gate_stream[0], "section", onward)
    gate_taps = lax.ppermute(taps[1], "section", onward)
    tail = lax.ppermute(
        gate_stream[0, -2:],
        ("section",) + seq,
        [(s * n_seq + i, t * n_seq + i + 1) for s, t in onward for i in range(n_seq - 1)],
    )
    local_taps = lax.dynamic_slice_in_dim(taps, seq_at * channels, channels, 2)
    local_taps = local_taps.reshape(9, channels).T
    tables = transform_tables(n_seq, rows)
    kernel = long_filter[0, 0, 0].reshape(channels, n_seq, rows).transpose(1, 0, 2)
    kernel_spec = forward_transform(kernel, tables)
    mixed, gate, gate_taps, tail, local_taps, kernel_spec = lax.optimization_barrier(
        (mixed, gate, gate_taps, tail, local_taps, kernel_spec)
    )

    sent_pairs, query = kernel_call(
        functools.partial(split_kernel, part),
        (shape((n_plane, 2, own_rows, HD), BF16), shape((own_rows, HD), BF16)),
        (),
        (mixed,),
    )
    pairs = lax.all_to_all(sent_pairs, ("xh", "tp"), 0, 0)

    product = kernel_call(
        functools.partial(product_kernel, 3 * part),
        shape((n_seq, channels, rows), F32),
        (),
        (mixed, local_taps),
    )
    spec = forward_transform(product, tables)
    real, imag = spec[:, :, :rows], spec[:, :, rows:]
    kernel_real, kernel_imag = kernel_spec[:, :, :rows], kernel_spec[:, :, rows:]
    joined = jnp.concatenate(
        [real * kernel_real - imag * kernel_imag, real * kernel_imag + imag * kernel_real], axis=2
    )
    convolved = inverse_transform(joined, tables)
    gain = lax.dynamic_slice_in_dim(skip_gain[0], seq_at * channels, channels, 0)
    long_out = (convolved + gain[None, :, None] * product).astype(BF16)

    delta = -(x_at * rows + lax.axis_index("tp") * part)
    returned = kernel_call(
        functools.partial(attend_kernel, rows),
        shape((n_z, part + n_x * channels, HD), BF16),
        (delta.astype(jnp.int32).reshape(1),),
        (query, pairs, long_out.reshape(n_z, n_x * channels, rows)),
        (),
        4 * own_rows * n_plane * own_rows * HD,
    )
    back = lax.all_to_all(returned, "z", 0, 0)
    back, weight = lax.optimization_barrier((back, weight))

    plane_rows, own_long, other_long = kernel_call(
        rows_kernel,
        (
            shape((n_plane, part, n_z * HD), BF16),
            shape((n_z, channels, rows), BF16),
            shape((n_z, channels, rows), BF16),
        ),
        (x_scalar,),
        (back,),
    )
    plane_rows = lax.all_to_all(plane_rows, ("xh", "tp"), 0, 0)
    own_long = lax.ppermute(own_long, "section", onward)
    got_long = lax.ppermute(
        other_long, ("section", "xh"), [(2 * s + x, 2 * t + 1 - x) for s, t in onward for x in range(2)]
    )
    handed = kernel_call(
        gate_kernel,
        shape(gate_stream.shape[1:], BF16),
        (x_scalar,),
        (own_long, got_long, gate, tail, gate_taps),
    )
    own_out, other_out = kernel_call(
        project_kernel,
        (shape((rows, n_z * channels), BF16),) * 2,
        (x_scalar,),
        (plane_rows, weight),
        (),
        4 * rows * n_tp * wide * n_z * channels,
    )
    got_out = lax.ppermute(other_out, "xh", swap)
    attended = kernel_call(
        functools.partial(unite_kernel, channels),
        shape(handed.shape, BF16),
        (x_scalar,),
        (own_out, got_out),
    )
    return (handed[None], attended[None])


def solution(mesh):
    n_sec, n_seq, n_tp = (mesh.shape[name] for name in ("section", "seq", "tp"))
    finer = Mesh(mesh.devices.reshape(n_sec, n_seq // 2, 2, n_tp), ("section", "z", "xh", "tp"))
    seq = ("z", "xh")
    placed = (
        P("section", seq, "tp"),
        P("section", seq, "tp"),
        P("section", seq, "tp"),
        P("section", None, None, "tp"),
        P("section", "tp", seq, None, None),
        P("section", "tp"),
        P("section", seq, "tp"),
        P("section", seq, "tp"),
        P("section", seq, "tp"),
        P("section", "tp", None, seq),
    )
    return jax.shard_map(
        body,
        mesh=finer,
        in_specs=placed,
        out_specs=(P("section", seq, "tp"), P("section", seq, "tp")),
        check_vma=False,
    )
```

```python
import functools
import math

import jax
import jax.numpy as jnp
import numpy as np
from jax import lax
from jax.experimental import pallas as pl
from jax.experimental.pallas import tpu as pltpu
from jax.sharding import Mesh, PartitionSpec as P

HD = 128
BF16 = jnp.bfloat16
F32 = jnp.float32


def dot(left, right, contract):
    return lax.dot_general(left, right, (contract, ((), ())), preferred_element_type=F32)


def transform_tables(depth, breadth):
    full = 2 * depth
    half = -(-(depth + 1) // 8) * 8
    k = np.arange(depth + 1)
    b = np.arange(breadth)
    one = -2.0 * np.pi * np.outer(k, np.arange(depth)) / full
    first = np.zeros((2 * half, depth))
    first[: depth + 1], first[half : half + depth + 1] = np.cos(one), np.sin(one)
    angle = -2.0 * np.pi * np.outer(k, b) / (full * breadth)
    mid = np.zeros((2, half, breadth))
    mid[0, : depth + 1], mid[1, : depth + 1] = np.cos(angle), np.sin(angle)
    two = -2.0 * np.pi * (np.outer(b, b) % breadth) / breadth
    cos_two, sin_two = np.cos(two), np.sin(two)
    weight = np.where((k == 0) | (k == depth), 1.0, 2.0) / (full * breadth)
    last = np.zeros((depth, 2 * half))
    last[:, : depth + 1] = np.cos(one).T * weight
    last[:, half : half + depth + 1] = np.sin(one).T * weight

    def halves(x):
        high = x.astype(BF16)
        return high, (x - high.astype(np.float64)).astype(BF16)

    first_high, first_low = halves(first)
    last_high, last_low = halves(last)
    return {
        "first_two": np.concatenate([first_high, first_low], axis=1),
        "first_three": np.concatenate([first_high, first_high, first_low], axis=1),
        "mid": mid.astype(np.float32),
        "forward": np.stack(halves(np.block([[cos_two, sin_two], [-sin_two, cos_two]]))),
        "backward": np.stack(halves(np.block([[cos_two, -sin_two], [sin_two, cos_two]]))),
        "last": np.concatenate([last_high, last_high, last_low], axis=1),
    }


def kernel_call(
    kernel, out_shape, scalars, arrays, scratch=(), flops=0, grant=32, hbm_in=(), hbm_out=()
):
    single = not isinstance(out_shape, tuple)
    outs = (out_shape,) if single else out_shape

    def spec(at, hbm):
        return pl.BlockSpec(memory_space=pltpu.HBM if at in hbm else pltpu.VMEM)

    arrays = [
        pltpu.with_memory_space_constraint(x, pltpu.HBM) if at in hbm_in else x
        for at, x in enumerate(arrays)
    ]
    in_specs = [pl.BlockSpec(memory_space=pltpu.SMEM)] * len(scalars)
    in_specs += [spec(at, hbm_in) for at in range(len(arrays))]
    out_specs = tuple(spec(at, hbm_out) for at in range(len(outs)))
    moved = sum(x.size * x.dtype.itemsize for x in (*arrays, *outs))
    placed = tuple(
        pltpu.HBM(x.shape, x.dtype) if at in hbm_out else x for at, x in enumerate(outs)
    )
    return pl.pallas_call(
        kernel,
        out_shape=placed[0] if single else placed,
        in_specs=in_specs,
        out_specs=out_specs[0] if single else out_specs,
        scratch_shapes=list(scratch),
        compiler_params=pltpu.CompilerParams(vmem_limit_bytes=grant * 1024 * 1024),
        cost_estimate=pl.CostEstimate(flops=flops, bytes_accessed=moved, transcendentals=0),
    )(*scalars, *arrays)


def pack_kernel(x_ref, first_ref, value_ref, taps_ref, query_ref, key_ref, value_head_ref, weight_ref, rows_ref, own_ref, other_ref):
    n_tp = rows_ref.shape[0]
    rows = query_ref.shape[0]
    part = rows // n_tp
    for at, ref in enumerate((query_ref, key_ref, value_head_ref)):
        rows_ref[:, at * part : (at + 1) * part, :] = ref[...].reshape(n_tp, part, -1)
    rows_ref[:, 3 * part :, :] = weight_ref[...]
    n_z, _, lanes = own_ref.shape
    per = 2 * n_z * lanes // first_ref.shape[1]
    channels = lanes // per
    low = x_ref[0] == 0
    for group in range(2 * n_z // per):
        span = slice(group * lanes, (group + 1) * lanes)
        shorts, edges = [], []
        for ref, which in ((first_ref, 0), (value_ref, 2)):
            x = ref[:, span].astype(F32)
            shorts.append(
                taps_ref[3 * which, :, span] * x
                + taps_ref[3 * which + 1, :, span] * pltpu.roll(x, 1, 0)
                + taps_ref[3 * which + 2, :, span] * pltpu.roll(x, 2, 0)
            )
            edges += [x[:2], x[rows - 2 :]]
        turned = (shorts[0] * shorts[1]).T
        edges = jnp.concatenate(edges, axis=0)
        for at in range(per // 2):
            z_at = group * per // 2 + at
            blocks = []
            for x_at in range(2):
                j = 2 * at + x_at
                edge = pltpu.roll(edges, lanes - j * channels, 1) if j else edges
                blocks.append(jnp.concatenate([turned[j * channels : (j + 1) * channels], edge], axis=0))
            own_ref[z_at] = jnp.where(low, blocks[0], blocks[1]).astype(BF16)
            other_ref[z_at] = jnp.where(low, blocks[1], blocks[0]).astype(BF16)


def repack_kernel(
    x_ref, rows_ref, own_hbm, got_ref, out_hbm, weight_hbm, own_ref, out_ref, sems
):
    n_tp, height, wide = rows_ref.shape
    channels = weight_hbm.shape[1]
    size = height - channels
    heads = wide // HD
    fetch = pltpu.make_async_copy(own_hbm, own_ref, sems.at[0])
    fetch.start()
    pass_on = pltpu.make_async_copy(rows_ref.at[:, size:, :], weight_hbm, sems.at[1])
    pass_on.start()
    for at in range(n_tp):
        for head in range(heads):
            block = rows_ref[at, :size, head * HD : (head + 1) * HD]
            out_ref[at * heads + head, :size, :] = block
    low = x_ref[0] == 0
    fetch.wait()
    own, got = own_ref[...].astype(F32), got_ref[...].astype(F32)
    even = jnp.where(low, own, got).astype(BF16)
    odd = jnp.where(low, got, own).astype(BF16)
    out_ref[:, size : size + channels, :] = even[:, :channels]
    out_ref[:, size + channels : size + 2 * channels, :] = odd[:, :channels]
    out_ref[:, size + 2 * channels : size + 2 * channels + 8, :] = even[:, channels:]
    out_ref[:, size + 2 * channels + 8 :, :] = odd[:, channels:]
    store = pltpu.make_async_copy(out_ref, out_hbm, sems.at[2])
    store.start()
    store.wait()
    pass_on.wait()


def split_kernel(part, mixed_ref, pairs_hbm, query_ref, block_ref, sems):
    n_z = mixed_ref.shape[0]
    for at in range(2):
        block = mixed_ref[:, (at + 1) * part : (at + 2) * part, :]
        block_ref[at] = block.reshape(n_z * part, HD)
    stores = [
        pltpu.make_async_copy(block_ref, pairs_hbm.at[to], sems.at[to])
        for to in range(pairs_hbm.shape[0])
    ]
    for store in stores:
        store.start()
    query_ref[...] = mixed_ref[:, :part, :].reshape(n_z * part, HD)
    for store in stores:
        store.wait()


def split_two(x):
    high = x.astype(BF16)
    return high, (x - high.astype(F32)).astype(BF16)


def dot_three(x, high, low):
    x_high, x_low = split_two(x)
    rows = ((1,), (0,))
    return dot(x_high, high, rows) + (dot(x_low, high, rows) + dot(x_high, low, rows))


def turn(real, imag, cos_mid, sin_mid, turned_ref, span):
    breadth = cos_mid.shape[1]
    turned_ref[span, :breadth] = real * cos_mid - imag * sin_mid
    turned_ref[span, breadth:] = real * sin_mid + imag * cos_mid


def spectrum_kernel(filter_ref, first_ref, mid_ref, forward_ref, out_ref, turned_ref):
    channels = filter_ref.shape[0]
    half = mid_ref.shape[1]
    cos_mid, sin_mid = mid_ref[0], mid_ref[1]
    for at in range(channels):
        high, low = split_two(filter_ref[at])
        both = dot(first_ref[...], jnp.concatenate([high, low, high], axis=0), ((1,), (0,)))
        turn(both[:half], both[half:], cos_mid, sin_mid, turned_ref, slice(at * half, (at + 1) * half))
    step = 4 * half
    for at in range(channels // 4):
        span = slice(at * step, (at + 1) * step)
        out_ref[span, :] = dot_three(turned_ref[span, :], forward_ref[0], forward_ref[1])


def convolve_kernel(
    start,
    gain_ref,
    mixed_ref,
    taps_ref,
    spectrum_ref,
    first_ref,
    mid_ref,
    forward_ref,
    backward_ref,
    last_ref,
    out_ref,
    signal_ref,
    turned_ref,
):
    n_seq, channels, rows = out_ref.shape
    count = n_seq * 8
    edges = mixed_ref[:, start + 2 * channels :, :].astype(F32).reshape(count, rows).T[:channels]
    lane = lax.broadcasted_iota(jnp.int32, (channels, count), 1)
    kind = lane % 8
    before = jnp.where(lane >= 8, 1.0, 0.0)
    ahead = jnp.where(kind % 4 == 0, pltpu.roll(edges, 5, 1) * before, pltpu.roll(edges, 1, 1))
    further = pltpu.roll(edges, 6, 1) * before
    tap = [jnp.where(kind < 4, taps_ref[:, i : i + 1], taps_ref[:, 6 + i : 7 + i]) for i in range(3)]
    short = tap[0] * edges + tap[1] * ahead + tap[2] * further
    made = (short * pltpu.roll(short, count - 4, 1)).astype(BF16).astype(F32)
    column = lax.broadcasted_iota(jnp.int32, (channels, rows), 1)
    for at in range(n_seq):
        turned = pltpu.roll(made, count - 8 * at, 1) if at else made
        begin = start + at % 2 * channels
        block = mixed_ref[at // 2, begin : begin + channels, :].astype(F32)
        signal_ref[at * channels : (at + 1) * channels, :] = jnp.where(
            column < 2, turned[:, :rows], block
        )
    half = mid_ref.shape[1]
    cos_mid, sin_mid = mid_ref[0], mid_ref[1]
    for at in range(channels):
        signal = signal_ref[pl.ds(at, n_seq, stride=channels), :].astype(BF16)
        both = dot(first_ref[...], jnp.concatenate([signal, signal], axis=0), ((1,), (0,)))
        turn(both[:half], both[half:], cos_mid, sin_mid, turned_ref, slice(at * half, (at + 1) * half))
    step = 4 * half
    for group in range(channels // 4):
        span = slice(group * step, (group + 1) * step)
        mine = dot_three(turned_ref[span, :], forward_ref[0], forward_ref[1])
        real, imag = mine[:, :rows], mine[:, rows:]
        other_real, other_imag = spectrum_ref[span, :rows], spectrum_ref[span, rows:]
        joined = jnp.concatenate(
            [real * other_real - imag * other_imag, real * other_imag + imag * other_real], axis=1
        )
        mid = dot_three(joined, backward_ref[0], backward_ref[1])
        for at in range(4):
            real, imag = (mid[at * half : (at + 1) * half, c * rows : (c + 1) * rows] for c in (0, 1))
            back = jnp.concatenate(
                [real * cos_mid + imag * sin_mid, imag * cos_mid - real * sin_mid], axis=0
            )
            high, low = split_two(back)
            out = dot(last_ref[...], jnp.concatenate([high, low, high], axis=0), ((1,), (0,)))
            channel = group * 4 + at
            strided = pl.ds(channel, n_seq, stride=channels)
            signal_ref[strided, :] = out + gain_ref[channel] * signal_ref[strided, :]
    out_ref[...] = signal_ref[...].astype(BF16).reshape(n_seq, channels, rows)


def attend_kernel(rows, delta_ref, query_ref, pairs_ref, long_ref, out_ref):
    size = 128
    n_z, height, _ = out_ref.shape
    own_rows = query_ref.shape[0]
    part = own_rows // n_z
    per = size // part
    row = lax.broadcasted_iota(jnp.int32, (size, size), 0)
    column = lax.broadcasted_iota(jnp.int32, (size, size), 1)
    q_pos = row // part * (2 * rows) + row % part
    k_pos = column // part * (2 * rows) + column % part + delta_ref[0]
    out_ref[:, part:, :] = long_ref[...]
    for tile in range(own_rows // size):
        query = query_ref[tile * size : (tile + 1) * size, :]
        parts = []
        for at in range(pairs_ref.shape[0]):
            n_tp = pairs_ref.shape[0] // 2
            allowed = k_pos + (at // n_tp * rows + at % n_tp * part) <= q_pos
            for start, stop in ((0, tile * size), (tile * size, (tile + 1) * size)):
                if start == stop:
                    continue
                keys = pairs_ref[at, 0, start:stop, :]
                scores = dot(query, keys, ((1,), (1,))) * (1.0 / math.sqrt(HD))
                if start == tile * size:
                    parts.append((jnp.where(allowed, scores, -1e30), at, start, stop))
                else:
                    parts.append((scores, at, start, stop))
        highest = parts[0][0].max(axis=1, keepdims=True)
        for piece in parts[1:]:
            highest = jnp.maximum(highest, piece[0].max(axis=1, keepdims=True))
        totals = jnp.zeros((size, 1), F32)
        weighted = jnp.zeros((size, HD), F32)
        for scores, at, start, stop in parts:
            probs = jnp.exp(scores - highest)
            totals = totals + probs.sum(axis=1, keepdims=True)
            values = pairs_ref[at, 1, start:stop, :]
            weighted = weighted + dot(probs.astype(BF16), values, ((1,), (0,)))
        out = (weighted / totals).astype(BF16).reshape(per, part, HD)
        out_ref[tile * per : (tile + 1) * per, :part, :] = out


def rows_kernel(
    x_ref, back_ref, rows_hbm, own_hbm, other_hbm, rows_ref, own_ref, other_ref, sems
):
    part = rows_ref.shape[0]
    channels = own_ref.shape[1]
    count = rows_hbm.shape[0]
    for head in range(back_ref.shape[0]):
        rows_ref[:, head * HD : (head + 1) * HD] = back_ref[head, :part, :]
    stores = [pltpu.make_async_copy(rows_ref, rows_hbm.at[to], sems.at[to]) for to in range(count)]
    for store in stores:
        store.start()
    low = x_ref[0] == 0
    even = back_ref[:, part : part + channels, :].astype(F32)
    odd = back_ref[:, part + channels :, :].astype(F32)
    own_ref[...] = jnp.where(low, even, odd).astype(BF16)
    other_ref[...] = jnp.where(low, odd, even).astype(BF16)
    stores += [
        pltpu.make_async_copy(own_ref, own_hbm, sems.at[count]),
        pltpu.make_async_copy(other_ref, other_hbm, sems.at[count + 1]),
    ]
    for store in stores[count:]:
        store.start()
    for store in stores:
        store.wait()


def gate_kernel(x_ref, own_ref, got_ref, gate_ref, tail_ref, taps_ref, out_ref):
    rows = gate_ref.shape[0]
    lanes = 128
    channels = own_ref.shape[1]
    per = lanes // channels
    row = lax.broadcasted_iota(jnp.int32, (rows, lanes), 0)
    low = x_ref[0] == 0
    for group in range(gate_ref.shape[1] // lanes):
        span = slice(group * lanes, (group + 1) * lanes)
        x = gate_ref[:, span].astype(F32)
        tail = tail_ref[:, span].astype(F32)
        one = jnp.where(row == 0, tail[1:2], pltpu.roll(x, 1, 0))
        two = jnp.where(row == 0, tail[0:1], jnp.where(row == 1, tail[1:2], pltpu.roll(x, 2, 0)))
        short = taps_ref[0:1, span] * x + taps_ref[1:2, span] * one + taps_ref[2:3, span] * two
        blocks = []
        for at in range(per // 2):
            own = own_ref[group * per // 2 + at].astype(F32)
            got = got_ref[group * per // 2 + at].astype(F32)
            blocks += [jnp.where(low, own, got), jnp.where(low, got, own)]
        out_ref[:, span] = (short * jnp.concatenate(blocks, axis=0).T).astype(BF16)


def project_kernel(x_ref, rows_ref, weight_ref, own_ref, other_ref):
    half = own_ref.shape[0]
    n_z, n_tp, channels, wide = weight_ref.shape
    part = rows_ref.shape[1]
    whole = rows_ref[...].reshape(2 * half, n_tp * wide)
    out = jnp.zeros((2 * half, n_z * channels), F32)
    for at in range(n_tp):
        block = weight_ref[:, at].reshape(n_z * channels, wide)
        out = out + dot(whole[:, at * wide : (at + 1) * wide], block, ((1,), (1,)))
    low = x_ref[0] == 0
    own_ref[...] = jnp.where(low, out[:half], out[half:]).astype(BF16)
    other_ref[...] = jnp.where(low, out[half:], out[:half]).astype(BF16)


def unite_kernel(channels, x_ref, own_ref, got_ref, out_ref):
    rows, lanes = own_ref.shape[0], 128
    low = x_ref[0] == 0
    lane = lax.broadcasted_iota(jnp.int32, (rows, lanes), 1)
    for group in range(out_ref.shape[1] // lanes):
        span = slice(group // 2 * lanes, (group // 2 + 1) * lanes)
        start = group % 2 * 2 * channels
        own, got = own_ref[:, span].astype(F32), got_ref[:, span].astype(F32)
        even, odd = jnp.where(low, own, got), jnp.where(low, got, own)

        def moved(x, by):
            by = by % lanes
            return pltpu.roll(x, by, 1) if by else x

        left = jnp.where(lane < channels, moved(even, -start), moved(odd, channels - start))
        right = jnp.where(
            lane < 3 * channels, moved(even, channels - start), moved(odd, 2 * channels - start)
        )
        out_ref[:, group * lanes : (group + 1) * lanes] = jnp.where(
            lane < 2 * channels, left, right
        ).astype(BF16)


def body(
    first_stream,
    gate_stream,
    value_stream,
    short_taps,
    long_filter,
    skip_gain,
    queries,
    attn_keys,
    attn_values,
    out_weight,
):
    seq = ("z", "xh")
    n_z, n_x, n_tp = lax.axis_size("z"), lax.axis_size("xh"), lax.axis_size("tp")
    n_seq, n_plane = n_z * n_x, n_x * n_tp
    seq_at = lax.axis_index(seq)
    x_at = lax.axis_index("xh")
    x_scalar = x_at.astype(jnp.int32).reshape(1)
    rows = queries.shape[1]
    wide = queries.shape[2]
    channels = long_filter.shape[3]
    part = rows // n_tp
    own_rows = n_z * part
    taps = short_taps[0]
    swap = [(0, 1), (1, 0)]
    shape = jax.ShapeDtypeStruct

    sent_rows, own, other = kernel_call(
        pack_kernel,
        (
            shape((n_tp, 3 * part + channels, wide), BF16),
            shape((n_z, channels + 8, rows), BF16),
            shape((n_z, channels + 8, rows), BF16),
        ),
        (x_scalar,),
        (
            first_stream[0],
            value_stream[0],
            short_taps.reshape(9, 1, -1),
            queries[0],
            attn_keys[0],
            attn_values[0],
            out_weight[0].transpose(1, 2, 0),
        ),
        grant=56,
    )
    got = lax.ppermute(other, "xh", swap)
    got_rows = lax.all_to_all(sent_rows, "tp", 0, 0)
    packed, weight = kernel_call(
        repack_kernel,
        (
            shape((n_z, 3 * part + 2 * channels + 16, HD), BF16),
            shape((n_tp, channels, wide), BF16),
        ),
        (x_scalar,),
        (got_rows, own, got),
        (
            pltpu.VMEM((n_z, channels + 8, rows), BF16),
            pltpu.VMEM((n_z, 3 * part + 2 * channels + 16, HD), BF16),
            pltpu.SemaphoreType.DMA((3,)),
        ),
        hbm_in=(1,),
        hbm_out=(0, 1),
    )
    mixed = lax.all_to_all(packed, "z", 0, 0)
    weight = lax.all_gather(weight, "z")

    n_sec = lax.axis_size("section")
    onward = [(i, (i + 1) % n_sec) for i in range(n_sec)]
    gate = lax.ppermute(gate_stream[0], "section", onward)
    gate_taps = lax.ppermute(taps[1], "section", onward)
    tail = lax.ppermute(
        gate_stream[0, -2:],
        ("section",) + seq,
        [(s * n_seq + i, t * n_seq + i + 1) for s, t in onward for i in range(n_seq - 1)],
    )
    local_taps = lax.dynamic_slice_in_dim(taps, seq_at * channels, channels, 2)
    local_taps = local_taps.reshape(9, channels).T
    tables = transform_tables(n_seq, rows)
    half = tables["mid"].shape[1]
    kernel_spec = kernel_call(
        spectrum_kernel,
        shape((channels * half, 2 * rows), F32),
        (),
        (
            long_filter[0, 0, 0].reshape(channels, n_seq, rows),
            tables["first_three"],
            tables["mid"],
            tables["forward"],
        ),
        (pltpu.VMEM((channels * half, 2 * rows), F32),),
    )
    mixed, gate, gate_taps, tail, local_taps, kernel_spec = lax.optimization_barrier(
        (mixed, gate, gate_taps, tail, local_taps, kernel_spec)
    )

    sent_pairs, query = kernel_call(
        functools.partial(split_kernel, part),
        (shape((n_plane, 2, own_rows, HD), BF16), shape((own_rows, HD), BF16)),
        (),
        (mixed,),
        (pltpu.VMEM((2, own_rows, HD), BF16), pltpu.SemaphoreType.DMA((n_plane,))),
        hbm_out=(0,),
    )
    pairs = lax.all_to_all(sent_pairs, ("xh", "tp"), 0, 0)

    gain = lax.dynamic_slice_in_dim(skip_gain[0], seq_at * channels, channels, 0)
    long_out = kernel_call(
        functools.partial(convolve_kernel, 3 * part),
        shape((n_seq, channels, rows), BF16),
        (gain,),
        (
            mixed,
            local_taps,
            kernel_spec,
            tables["first_two"],
            tables["mid"],
            tables["forward"],
            tables["backward"],
            tables["last"],
        ),
        (
            pltpu.VMEM((n_seq * channels, rows), F32),
            pltpu.VMEM((channels * half, 2 * rows), F32),
        ),
    )

    delta = -(x_at * rows + lax.axis_index("tp") * part)
    returned = kernel_call(
        functools.partial(attend_kernel, rows),
        shape((n_z, part + n_x * channels, HD), BF16),
        (delta.astype(jnp.int32).reshape(1),),
        (query, pairs, long_out.reshape(n_z, n_x * channels, rows)),
        (),
        4 * own_rows * n_plane * own_rows * HD,
    )
    back = lax.all_to_all(returned, "z", 0, 0)
    back, weight = lax.optimization_barrier((back, weight))

    plane_rows, own_long, other_long = kernel_call(
        rows_kernel,
        (
            shape((n_plane, part, n_z * HD), BF16),
            shape((n_z, channels, rows), BF16),
            shape((n_z, channels, rows), BF16),
        ),
        (x_scalar,),
        (back,),
        (
            pltpu.VMEM((part, n_z * HD), BF16),
            pltpu.VMEM((n_z, channels, rows), BF16),
            pltpu.VMEM((n_z, channels, rows), BF16),
            pltpu.SemaphoreType.DMA((n_plane + 2,)),
        ),
        hbm_out=(0, 1, 2),
    )
    plane_rows = lax.all_to_all(plane_rows, ("xh", "tp"), 0, 0)
    own_long = lax.ppermute(own_long, "section", onward)
    got_long = lax.ppermute(
        other_long, ("section", "xh"), [(2 * s + x, 2 * t + 1 - x) for s, t in onward for x in range(2)]
    )
    handed = kernel_call(
        gate_kernel,
        shape(gate_stream.shape[1:], BF16),
        (x_scalar,),
        (own_long, got_long, gate, tail, gate_taps),
    )
    own_out, other_out = kernel_call(
        project_kernel,
        (shape((rows, n_z * channels), BF16),) * 2,
        (x_scalar,),
        (plane_rows, weight),
        (),
        4 * rows * n_tp * wide * n_z * channels,
    )
    got_out = lax.ppermute(other_out, "xh", swap)
    attended = kernel_call(
        functools.partial(unite_kernel, channels),
        shape(handed.shape, BF16),
        (x_scalar,),
        (own_out, got_out),
    )
    return (handed[None], attended[None])


def solution(mesh):
    n_sec, n_seq, n_tp = (mesh.shape[name] for name in ("section", "seq", "tp"))
    finer = Mesh(mesh.devices.reshape(n_sec, n_seq // 2, 2, n_tp), ("section", "z", "xh", "tp"))
    seq = ("z", "xh")
    placed = (
        P("section", seq, "tp"),
        P("section", seq, "tp"),
        P("section", seq, "tp"),
        P("section", None, None, "tp"),
        P("section", "tp", seq, None, None),
        P("section", "tp"),
        P("section", seq, "tp"),
        P("section", seq, "tp"),
        P("section", seq, "tp"),
        P("section", "tp", None, seq),
    )
    return jax.shard_map(
        body,
        mesh=finer,
        in_specs=placed,
        out_specs=(P("section", seq, "tp"), P("section", seq, "tp")),
        check_vma=False,
    )
```

```python
import functools
import math

import jax
import jax.numpy as jnp
import numpy as np
from jax import lax
from jax.experimental import pallas as pl
from jax.experimental.pallas import tpu as pltpu
from jax.sharding import Mesh, PartitionSpec as P

HD = 128
BF16 = jnp.bfloat16
F32 = jnp.float32


def dot(left, right, contract):
    return lax.dot_general(left, right, (contract, ((), ())), preferred_element_type=F32)


def transform_tables(depth, breadth):
    full = 2 * depth
    half = -(-(depth + 1) // 8) * 8
    k = np.arange(depth + 1)
    b = np.arange(breadth)
    one = -2.0 * np.pi * np.outer(k, np.arange(depth)) / full
    first = np.zeros((2 * half, depth))
    first[: depth + 1], first[half : half + depth + 1] = np.cos(one), np.sin(one)
    angle = -2.0 * np.pi * np.outer(k, b) / (full * breadth)
    mid = np.zeros((2, half, breadth))
    mid[0, : depth + 1], mid[1, : depth + 1] = np.cos(angle), np.sin(angle)
    two = -2.0 * np.pi * (np.outer(b, b) % breadth) / breadth
    cos_two, sin_two = np.cos(two), np.sin(two)
    weight = np.where((k == 0) | (k == depth), 1.0, 2.0) / (full * breadth)
    last = np.zeros((depth, 2 * half))
    last[:, : depth + 1] = np.cos(one).T * weight
    last[:, half : half + depth + 1] = np.sin(one).T * weight

    def halves(x):
        high = x.astype(BF16)
        return high, (x - high.astype(np.float64)).astype(BF16)

    first_high, first_low = halves(first)
    last_high, last_low = halves(last)
    return {
        "first_two": np.concatenate([first_high, first_low], axis=1),
        "first_three": np.concatenate([first_high, first_high, first_low], axis=1),
        "mid": mid.astype(np.float32),
        "forward": np.stack(halves(np.block([[cos_two, sin_two], [-sin_two, cos_two]]))),
        "backward": np.stack(halves(np.block([[cos_two, -sin_two], [sin_two, cos_two]]))),
        "last": np.concatenate([last_high, last_high, last_low], axis=1),
    }


def kernel_call(
    kernel, out_shape, scalars, arrays, scratch=(), flops=0, grant=16, hbm_in=(), hbm_out=()
):
    single = not isinstance(out_shape, tuple)
    outs = (out_shape,) if single else out_shape

    def spec(at, hbm):
        return pl.BlockSpec(memory_space=pltpu.HBM if at in hbm else pltpu.VMEM)

    arrays = [
        pltpu.with_memory_space_constraint(x, pltpu.HBM) if at in hbm_in else x
        for at, x in enumerate(arrays)
    ]
    in_specs = [pl.BlockSpec(memory_space=pltpu.SMEM)] * len(scalars)
    in_specs += [spec(at, hbm_in) for at in range(len(arrays))]
    out_specs = tuple(spec(at, hbm_out) for at in range(len(outs)))
    moved = sum(x.size * x.dtype.itemsize for x in (*arrays, *outs))
    placed = tuple(
        pltpu.HBM(x.shape, x.dtype) if at in hbm_out else x for at, x in enumerate(outs)
    )
    return pl.pallas_call(
        kernel,
        out_shape=placed[0] if single else placed,
        in_specs=in_specs,
        out_specs=out_specs[0] if single else out_specs,
        scratch_shapes=list(scratch),
        compiler_params=pltpu.CompilerParams(vmem_limit_bytes=grant * 1024 * 1024),
        cost_estimate=pl.CostEstimate(flops=flops, bytes_accessed=moved, transcendentals=0),
    )(*scalars, *arrays)


def pack_kernel(x_ref, first_ref, value_ref, taps_ref, query_ref, key_ref, value_head_ref, weight_ref, rows_ref, own_ref, other_ref):
    n_tp = rows_ref.shape[0]
    rows = query_ref.shape[0]
    part = rows // n_tp
    for at, ref in enumerate((query_ref, key_ref, value_head_ref)):
        rows_ref[:, at * part : (at + 1) * part, :] = ref[...].reshape(n_tp, part, -1)
    rows_ref[:, 3 * part :, :] = weight_ref[...]
    n_z, _, lanes = own_ref.shape
    per = 2 * n_z * lanes // first_ref.shape[1]
    channels = lanes // per
    low = x_ref[0] == 0
    for group in range(2 * n_z // per):
        span = slice(group * lanes, (group + 1) * lanes)
        shorts, edges = [], []
        for ref, which in ((first_ref, 0), (value_ref, 2)):
            x = ref[:, span].astype(F32)
            shorts.append(
                taps_ref[3 * which, :, span] * x
                + taps_ref[3 * which + 1, :, span] * pltpu.roll(x, 1, 0)
                + taps_ref[3 * which + 2, :, span] * pltpu.roll(x, 2, 0)
            )
            edges += [x[:2], x[rows - 2 :]]
        turned = (shorts[0] * shorts[1]).T
        edges = jnp.concatenate(edges, axis=0)
        for at in range(per // 2):
            z_at = group * per // 2 + at
            blocks = []
            for x_at in range(2):
                j = 2 * at + x_at
                edge = pltpu.roll(edges, lanes - j * channels, 1) if j else edges
                blocks.append(jnp.concatenate([turned[j * channels : (j + 1) * channels], edge], axis=0))
            own_ref[z_at] = jnp.where(low, blocks[0], blocks[1]).astype(BF16)
            other_ref[z_at] = jnp.where(low, blocks[1], blocks[0]).astype(BF16)


def repack_kernel(
    x_ref, rows_ref, own_hbm, got_ref, out_hbm, weight_hbm, own_ref, out_ref, sems
):
    n_tp, height, wide = rows_ref.shape
    channels = weight_hbm.shape[1]
    size = height - channels
    heads = wide // HD
    fetch = pltpu.make_async_copy(own_hbm, own_ref, sems.at[0])
    fetch.start()
    pass_on = pltpu.make_async_copy(rows_ref.at[:, size:, :], weight_hbm, sems.at[1])
    pass_on.start()
    for at in range(n_tp):
        for head in range(heads):
            block = rows_ref[at, :size, head * HD : (head + 1) * HD]
            out_ref[at * heads + head, :size, :] = block
    low = x_ref[0] == 0
    fetch.wait()
    own, got = own_ref[...].astype(F32), got_ref[...].astype(F32)
    even = jnp.where(low, own, got).astype(BF16)
    odd = jnp.where(low, got, own).astype(BF16)
    out_ref[:, size : size + channels, :] = even[:, :channels]
    out_ref[:, size + channels : size + 2 * channels, :] = odd[:, :channels]
    out_ref[:, size + 2 * channels : size + 2 * channels + 8, :] = even[:, channels:]
    out_ref[:, size + 2 * channels + 8 :, :] = odd[:, channels:]
    store = pltpu.make_async_copy(out_ref, out_hbm, sems.at[2])
    store.start()
    store.wait()
    pass_on.wait()


def split_kernel(part, mixed_ref, pairs_hbm, query_ref, block_ref, sems):
    n_z = mixed_ref.shape[0]
    for at in range(2):
        block = mixed_ref[:, (at + 1) * part : (at + 2) * part, :]
        block_ref[at] = block.reshape(n_z * part, HD)
    stores = [
        pltpu.make_async_copy(block_ref, pairs_hbm.at[to], sems.at[to])
        for to in range(pairs_hbm.shape[0])
    ]
    for store in stores:
        store.start()
    query_ref[...] = mixed_ref[:, :part, :].reshape(n_z * part, HD)
    for store in stores:
        store.wait()


def split_two(x):
    high = x.astype(BF16)
    return high, (x - high.astype(F32)).astype(BF16)


def dot_three(x, high, low):
    x_high, x_low = split_two(x)
    rows = ((1,), (0,))
    return dot(x_high, high, rows) + (dot(x_low, high, rows) + dot(x_high, low, rows))


def turn(real, imag, cos_mid, sin_mid, turned_ref, span):
    breadth = cos_mid.shape[1]
    turned_ref[span, :breadth] = real * cos_mid - imag * sin_mid
    turned_ref[span, breadth:] = real * sin_mid + imag * cos_mid


def spectrum_kernel(filter_ref, first_ref, mid_ref, forward_ref, out_ref, turned_ref):
    channels = filter_ref.shape[0]
    half = mid_ref.shape[1]
    cos_mid, sin_mid = mid_ref[0], mid_ref[1]
    for at in range(channels):
        high, low = split_two(filter_ref[at])
        both = dot(first_ref[...], jnp.concatenate([high, low, high], axis=0), ((1,), (0,)))
        turn(both[:half], both[half:], cos_mid, sin_mid, turned_ref, slice(at * half, (at + 1) * half))
    step = 4 * half
    for at in range(channels // 4):
        span = slice(at * step, (at + 1) * step)
        out_ref[span, :] = dot_three(turned_ref[span, :], forward_ref[0], forward_ref[1])


def convolve_kernel(
    start,
    gain_ref,
    mixed_ref,
    taps_ref,
    spectrum_ref,
    first_ref,
    mid_ref,
    forward_ref,
    backward_ref,
    last_ref,
    out_ref,
    signal_ref,
    turned_ref,
):
    n_seq, channels, rows = out_ref.shape
    count = n_seq * 8
    edges = mixed_ref[:, start + 2 * channels :, :].astype(F32).reshape(count, rows).T[:channels]
    lane = lax.broadcasted_iota(jnp.int32, (channels, count), 1)
    kind = lane % 8
    before = jnp.where(lane >= 8, 1.0, 0.0)
    ahead = jnp.where(kind % 4 == 0, pltpu.roll(edges, 5, 1) * before, pltpu.roll(edges, 1, 1))
    further = pltpu.roll(edges, 6, 1) * before
    tap = [jnp.where(kind < 4, taps_ref[:, i : i + 1], taps_ref[:, 6 + i : 7 + i]) for i in range(3)]
    short = tap[0] * edges + tap[1] * ahead + tap[2] * further
    made = (short * pltpu.roll(short, count - 4, 1)).astype(BF16).astype(F32)
    column = lax.broadcasted_iota(jnp.int32, (channels, rows), 1)
    for at in range(n_seq):
        turned = pltpu.roll(made, count - 8 * at, 1) if at else made
        begin = start + at % 2 * channels
        block = mixed_ref[at // 2, begin : begin + channels, :].astype(F32)
        signal_ref[at * channels : (at + 1) * channels, :] = jnp.where(
            column < 2, turned[:, :rows], block
        )
    half = mid_ref.shape[1]
    cos_mid, sin_mid = mid_ref[0], mid_ref[1]
    for at in range(channels):
        signal = signal_ref[pl.ds(at, n_seq, stride=channels), :].astype(BF16)
        both = dot(first_ref[...], jnp.concatenate([signal, signal], axis=0), ((1,), (0,)))
        turn(both[:half], both[half:], cos_mid, sin_mid, turned_ref, slice(at * half, (at + 1) * half))
    step = 4 * half
    for group in range(channels // 4):
        span = slice(group * step, (group + 1) * step)
        mine = dot_three(turned_ref[span, :], forward_ref[0], forward_ref[1])
        real, imag = mine[:, :rows], mine[:, rows:]
        other_real, other_imag = spectrum_ref[span, :rows], spectrum_ref[span, rows:]
        joined = jnp.concatenate(
            [real * other_real - imag * other_imag, real * other_imag + imag * other_real], axis=1
        )
        mid = dot_three(joined, backward_ref[0], backward_ref[1])
        for at in range(4):
            real, imag = (mid[at * half : (at + 1) * half, c * rows : (c + 1) * rows] for c in (0, 1))
            back = jnp.concatenate(
                [real * cos_mid + imag * sin_mid, imag * cos_mid - real * sin_mid], axis=0
            )
            high, low = split_two(back)
            out = dot(last_ref[...], jnp.concatenate([high, low, high], axis=0), ((1,), (0,)))
            channel = group * 4 + at
            strided = pl.ds(channel, n_seq, stride=channels)
            signal_ref[strided, :] = out + gain_ref[channel] * signal_ref[strided, :]
    out_ref[...] = signal_ref[...].astype(BF16).reshape(n_seq, channels, rows)


def attend(delta, query_ref, pairs_ref, tile, few, rows):
    size = 128
    query = query_ref[tile * size : (tile + 1) * size, :]
    row = lax.broadcasted_iota(jnp.int32, (size, size), 0)
    column = lax.broadcasted_iota(jnp.int32, (size, size), 1)
    q_pos = row // few * rows + row % few
    k_pos = column // few * rows + column % few
    parts = []
    for at in range(pairs_ref.shape[0]):
        allowed = k_pos + (at * few + delta) <= q_pos
        for start, stop in ((0, tile * size), (tile * size, (tile + 1) * size)):
            if start == stop:
                continue
            keys = pairs_ref[at, 0, start:stop, :]
            scores = dot(query, keys, ((1,), (1,))) * (1.0 / math.sqrt(HD))
            if start == tile * size:
                parts.append((jnp.where(allowed, scores, -1e30), allowed, at, start, stop))
            else:
                parts.append((scores, None, at, start, stop))
    highest = parts[0][0].max(axis=1, keepdims=True)
    for part in parts[1:]:
        highest = jnp.maximum(highest, part[0].max(axis=1, keepdims=True))
    totals = jnp.zeros((size, 1), F32)
    weighted = jnp.zeros((size, HD), F32)
    for scores, allowed, at, start, stop in parts:
        probs = jnp.exp(scores - highest)
        if allowed is not None:
            probs = jnp.where(allowed, probs, 0.0)
        totals = totals + probs.sum(axis=1, keepdims=True)
        values = pairs_ref[at, 1, start:stop, :]
        weighted = weighted + dot(probs.astype(BF16), values, ((1,), (0,)))
    some = totals > 0.0
    totals = jnp.maximum(totals, 1e-30)
    return weighted / totals, jnp.where(some, highest + jnp.log(totals), -1e30)


def other_kernel(rows, few, delta_ref, query_ref, pairs_ref, out_ref, log_ref):
    own_rows = query_ref.shape[0]
    log_ref[...] = jnp.zeros_like(log_ref)
    for tile in range(own_rows // 128):
        out, log = attend(delta_ref[0], query_ref, pairs_ref, tile, few, rows)
        out_ref[tile * 128 : (tile + 1) * 128, :] = out.astype(BF16)
        line = jnp.broadcast_to(log, (128, 128)).T[:8]
        first = line.astype(BF16).astype(F32)
        second = (line - first).astype(BF16).astype(F32)
        third = line - first - second
        for at, term in enumerate((first, second, third)):
            log_ref[at * 8 + tile : at * 8 + tile + 1, :] = term[:1]
    out_ref[own_rows:, :] = log_ref[...].astype(BF16)


def own_kernel(rows, few, delta_ref, query_ref, pairs_ref, out_ref, log_ref):
    for tile in range(query_ref.shape[0] // 128):
        span = slice(tile * 128, (tile + 1) * 128)
        out, log = attend(delta_ref[0], query_ref, pairs_ref, tile, few, rows)
        out_ref[span, :] = out
        log_ref[span, :] = jnp.broadcast_to(log, (128, 128))


def merge_kernel(own_ref, log_ref, got_ref, long_ref, out_ref):
    own_rows = own_ref.shape[0]
    few = own_rows // out_ref.shape[0]
    per = 128 // few
    logs = got_ref[own_rows:, :].astype(F32)
    for tile in range(own_rows // 128):
        span = slice(tile * 128, (tile + 1) * 128)
        log = log_ref[span, :]
        line = logs[tile : tile + 1] + logs[8 + tile : 9 + tile] + logs[16 + tile : 17 + tile]
        got_log = jnp.broadcast_to(line, (128, 128)).T
        highest = jnp.maximum(log, got_log)
        own_share, got_share = jnp.exp(log - highest), jnp.exp(got_log - highest)
        merged = own_ref[span, :] * own_share + got_ref[span, :].astype(F32) * got_share
        merged = (merged / (own_share + got_share)).astype(BF16).reshape(per, few, HD)
        out_ref[tile * per : (tile + 1) * per, :few, :] = merged
    out_ref[:, few:, :] = long_ref[...]


def rows_kernel(
    x_ref, back_ref, rows_hbm, own_hbm, other_hbm, rows_ref, own_ref, other_ref, sems
):
    part = rows_ref.shape[0]
    channels = own_ref.shape[1]
    count = rows_hbm.shape[0]
    for head in range(back_ref.shape[0]):
        rows_ref[:, head * HD : (head + 1) * HD] = back_ref[head, :part, :]
    stores = [pltpu.make_async_copy(rows_ref, rows_hbm.at[to], sems.at[to]) for to in range(count)]
    for store in stores:
        store.start()
    low = x_ref[0] == 0
    even = back_ref[:, part : part + channels, :].astype(F32)
    odd = back_ref[:, part + channels :, :].astype(F32)
    own_ref[...] = jnp.where(low, even, odd).astype(BF16)
    other_ref[...] = jnp.where(low, odd, even).astype(BF16)
    stores += [
        pltpu.make_async_copy(own_ref, own_hbm, sems.at[count]),
        pltpu.make_async_copy(other_ref, other_hbm, sems.at[count + 1]),
    ]
    for store in stores[count:]:
        store.start()
    for store in stores:
        store.wait()


def gate_kernel(x_ref, own_ref, got_ref, gate_ref, tail_ref, taps_ref, out_ref):
    rows = gate_ref.shape[0]
    lanes = 128
    channels = own_ref.shape[1]
    per = lanes // channels
    row = lax.broadcasted_iota(jnp.int32, (rows, lanes), 0)
    low = x_ref[0] == 0
    for group in range(gate_ref.shape[1] // lanes):
        span = slice(group * lanes, (group + 1) * lanes)
        x = gate_ref[:, span].astype(F32)
        tail = tail_ref[:, span].astype(F32)
        one = jnp.where(row == 0, tail[1:2], pltpu.roll(x, 1, 0))
        two = jnp.where(row == 0, tail[0:1], jnp.where(row == 1, tail[1:2], pltpu.roll(x, 2, 0)))
        short = taps_ref[0:1, span] * x + taps_ref[1:2, span] * one + taps_ref[2:3, span] * two
        blocks = []
        for at in range(per // 2):
            own = own_ref[group * per // 2 + at].astype(F32)
            got = got_ref[group * per // 2 + at].astype(F32)
            blocks += [jnp.where(low, own, got), jnp.where(low, got, own)]
        out_ref[:, span] = (short * jnp.concatenate(blocks, axis=0).T).astype(BF16)


def project_kernel(x_ref, rows_ref, weight_ref, own_ref, other_ref):
    half = own_ref.shape[0]
    n_z, n_tp, channels, wide = weight_ref.shape
    part = rows_ref.shape[1]
    whole = rows_ref[...].reshape(2 * half, n_tp * wide)
    out = jnp.zeros((2 * half, n_z * channels), F32)
    for at in range(n_tp):
        block = weight_ref[:, at].reshape(n_z * channels, wide)
        out = out + dot(whole[:, at * wide : (at + 1) * wide], block, ((1,), (1,)))
    low = x_ref[0] == 0
    own_ref[...] = jnp.where(low, out[:half], out[half:]).astype(BF16)
    other_ref[...] = jnp.where(low, out[half:], out[:half]).astype(BF16)


def unite_kernel(channels, x_ref, own_ref, got_ref, out_ref):
    rows, lanes = own_ref.shape[0], 128
    low = x_ref[0] == 0
    lane = lax.broadcasted_iota(jnp.int32, (rows, lanes), 1)
    for group in range(out_ref.shape[1] // lanes):
        span = slice(group // 2 * lanes, (group // 2 + 1) * lanes)
        start = group % 2 * 2 * channels
        own, got = own_ref[:, span].astype(F32), got_ref[:, span].astype(F32)
        even, odd = jnp.where(low, own, got), jnp.where(low, got, own)

        def moved(x, by):
            by = by % lanes
            return pltpu.roll(x, by, 1) if by else x

        left = jnp.where(lane < channels, moved(even, -start), moved(odd, channels - start))
        right = jnp.where(
            lane < 3 * channels, moved(even, channels - start), moved(odd, 2 * channels - start)
        )
        out_ref[:, group * lanes : (group + 1) * lanes] = jnp.where(
            lane < 2 * channels, left, right
        ).astype(BF16)


def body(
    first_stream,
    gate_stream,
    value_stream,
    short_taps,
    long_filter,
    skip_gain,
    queries,
    attn_keys,
    attn_values,
    out_weight,
):
    seq = ("z", "xh")
    n_z, n_x, n_tp = lax.axis_size("z"), lax.axis_size("xh"), lax.axis_size("tp")
    n_seq, n_plane = n_z * n_x, n_x * n_tp
    seq_at = lax.axis_index(seq)
    x_at = lax.axis_index("xh")
    x_scalar = x_at.astype(jnp.int32).reshape(1)
    rows = queries.shape[1]
    wide = queries.shape[2]
    channels = long_filter.shape[3]
    part = rows // n_tp
    own_rows = n_z * part
    taps = short_taps[0]
    swap = [(0, 1), (1, 0)]
    shape = jax.ShapeDtypeStruct

    sent_rows, own, other = kernel_call(
        pack_kernel,
        (
            shape((n_tp, 3 * part + channels, wide), BF16),
            shape((n_z, channels + 8, rows), BF16),
            shape((n_z, channels + 8, rows), BF16),
        ),
        (x_scalar,),
        (
            first_stream[0],
            value_stream[0],
            short_taps.reshape(9, 1, -1),
            queries[0],
            attn_keys[0],
            attn_values[0],
            out_weight[0].transpose(1, 2, 0),
        ),
        grant=56,
    )
    got = lax.ppermute(other, "xh", swap)
    got_rows = lax.all_to_all(sent_rows, "tp", 0, 0)
    packed, weight = kernel_call(
        repack_kernel,
        (
            shape((n_z, 3 * part + 2 * channels + 16, HD), BF16),
            shape((n_tp, channels, wide), BF16),
        ),
        (x_scalar,),
        (got_rows, own, got),
        (
            pltpu.VMEM((n_z, channels + 8, rows), BF16),
            pltpu.VMEM((n_z, 3 * part + 2 * channels + 16, HD), BF16),
            pltpu.SemaphoreType.DMA((3,)),
        ),
        hbm_in=(1,),
        hbm_out=(0, 1),
    )
    mixed = lax.all_to_all(packed, "z", 0, 0)
    weight = lax.all_gather(weight, "z")

    n_sec = lax.axis_size("section")
    onward = [(i, (i + 1) % n_sec) for i in range(n_sec)]
    gate = lax.ppermute(gate_stream[0], "section", onward)
    gate_taps = lax.ppermute(taps[1], "section", onward)
    tail = lax.ppermute(
        gate_stream[0, -2:],
        ("section",) + seq,
        [(s * n_seq + i, t * n_seq + i + 1) for s, t in onward for i in range(n_seq - 1)],
    )
    local_taps = lax.dynamic_slice_in_dim(taps, seq_at * channels, channels, 2)
    local_taps = local_taps.reshape(9, channels).T
    tables = transform_tables(n_seq, rows)
    half = tables["mid"].shape[1]
    kernel_spec = kernel_call(
        spectrum_kernel,
        shape((channels * half, 2 * rows), F32),
        (),
        (
            long_filter[0, 0, 0].reshape(channels, n_seq, rows),
            tables["first_three"],
            tables["mid"],
            tables["forward"],
        ),
        (pltpu.VMEM((channels * half, 2 * rows), F32),),
    )
    mixed, gate, gate_taps, tail, local_taps, kernel_spec = lax.optimization_barrier(
        (mixed, gate, gate_taps, tail, local_taps, kernel_spec)
    )

    sent_pairs, query = kernel_call(
        functools.partial(split_kernel, part),
        (shape((n_tp, 2, own_rows, HD), BF16), shape((own_rows, HD), BF16)),
        (),
        (mixed,),
        (pltpu.VMEM((2, own_rows, HD), BF16), pltpu.SemaphoreType.DMA((n_tp,))),
        hbm_out=(0,),
    )
    other_query = lax.ppermute(query, "xh", swap)
    pairs = lax.all_to_all(sent_pairs, "tp", 0, 0)

    gain = lax.dynamic_slice_in_dim(skip_gain[0], seq_at * channels, channels, 0)
    long_out = kernel_call(
        functools.partial(convolve_kernel, 3 * part),
        shape((n_seq, channels, rows), BF16),
        (gain,),
        (
            mixed,
            local_taps,
            kernel_spec,
            tables["first_two"],
            tables["mid"],
            tables["forward"],
            tables["backward"],
            tables["last"],
        ),
        (
            pltpu.VMEM((n_seq * channels, rows), F32),
            pltpu.VMEM((channels * half, 2 * rows), F32),
        ),
    )

    pairs, long_out = lax.optimization_barrier((pairs, long_out))
    work = 2 * own_rows * n_tp * own_rows * HD
    own_delta = -lax.axis_index("tp") * part
    other_delta = (2 * x_at - 1) * rows + own_delta
    sent = kernel_call(
        functools.partial(other_kernel, n_x * rows, part),
        shape((own_rows + 32, HD), BF16),
        (other_delta.astype(jnp.int32).reshape(1),),
        (other_query, pairs),
        (pltpu.VMEM((32, HD), F32),),
        work,
    )
    got = lax.ppermute(sent, "xh", swap)
    query, sent = lax.optimization_barrier((query, sent))
    own_out, own_log = kernel_call(
        functools.partial(own_kernel, n_x * rows, part),
        (shape((own_rows, HD), F32),) * 2,
        (own_delta.astype(jnp.int32).reshape(1),),
        (query, pairs),
        (),
        work,
    )
    returned = kernel_call(
        merge_kernel,
        shape((n_z, part + n_x * channels, HD), BF16),
        (),
        (own_out, own_log, got, long_out.reshape(n_z, n_x * channels, rows)),
    )
    back = lax.all_to_all(returned, "z", 0, 0)
    back, weight = lax.optimization_barrier((back, weight))

    plane_rows, own_long, other_long = kernel_call(
        rows_kernel,
        (
            shape((n_plane, part, n_z * HD), BF16),
            shape((n_z, channels, rows), BF16),
            shape((n_z, channels, rows), BF16),
        ),
        (x_scalar,),
        (back,),
        (
            pltpu.VMEM((part, n_z * HD), BF16),
            pltpu.VMEM((n_z, channels, rows), BF16),
            pltpu.VMEM((n_z, channels, rows), BF16),
            pltpu.SemaphoreType.DMA((n_plane + 2,)),
        ),
        hbm_out=(0, 1, 2),
    )
    plane_rows = lax.all_to_all(plane_rows, ("xh", "tp"), 0, 0)
    own_long = lax.ppermute(own_long, "section", onward)
    got_long = lax.ppermute(
        other_long, ("section", "xh"), [(2 * s + x, 2 * t + 1 - x) for s, t in onward for x in range(2)]
    )
    handed = kernel_call(
        gate_kernel,
        shape(gate_stream.shape[1:], BF16),
        (x_scalar,),
        (own_long, got_long, gate, tail, gate_taps),
    )
    own_out, other_out = kernel_call(
        project_kernel,
        (shape((rows, n_z * channels), BF16),) * 2,
        (x_scalar,),
        (plane_rows, weight),
        (),
        4 * rows * n_tp * wide * n_z * channels,
    )
    got_out = lax.ppermute(other_out, "xh", swap)
    attended = kernel_call(
        functools.partial(unite_kernel, channels),
        shape(handed.shape, BF16),
        (x_scalar,),
        (own_out, got_out),
    )
    return (handed[None], attended[None])


def solution(mesh):
    n_sec, n_seq, n_tp = (mesh.shape[name] for name in ("section", "seq", "tp"))
    finer = Mesh(mesh.devices.reshape(n_sec, n_seq // 2, 2, n_tp), ("section", "z", "xh", "tp"))
    seq = ("z", "xh")
    placed = (
        P("section", seq, "tp"),
        P("section", seq, "tp"),
        P("section", seq, "tp"),
        P("section", None, None, "tp"),
        P("section", "tp", seq, None, None),
        P("section", "tp"),
        P("section", seq, "tp"),
        P("section", seq, "tp"),
        P("section", seq, "tp"),
        P("section", "tp", None, seq),
    )
    return jax.shard_map(
        body,
        mesh=finer,
        in_specs=placed,
        out_specs=(P("section", seq, "tp"), P("section", seq, "tp")),
        check_vma=False,
    )
```

```python
import functools
import math

import jax
import jax.numpy as jnp
import numpy as np
from jax import lax
from jax.experimental import pallas as pl
from jax.experimental.pallas import tpu as pltpu
from jax.sharding import Mesh, PartitionSpec as P

HD = 128
BF16 = jnp.bfloat16
F32 = jnp.float32


def dot(left, right, contract):
    return lax.dot_general(left, right, (contract, ((), ())), preferred_element_type=F32)


def transform_tables(depth, breadth):
    full = 2 * depth
    half = -(-(depth + 1) // 8) * 8
    k = np.arange(depth + 1)
    b = np.arange(breadth)
    one = -2.0 * np.pi * np.outer(k, np.arange(depth)) / full
    first = np.zeros((2 * half, depth))
    first[: depth + 1], first[half : half + depth + 1] = np.cos(one), np.sin(one)
    angle = -2.0 * np.pi * np.outer(k, b) / (full * breadth)
    mid = np.zeros((2, half, breadth))
    mid[0, : depth + 1], mid[1, : depth + 1] = np.cos(angle), np.sin(angle)
    two = -2.0 * np.pi * (np.outer(b, b) % breadth) / breadth
    cos_two, sin_two = np.cos(two), np.sin(two)
    weight = np.where((k == 0) | (k == depth), 1.0, 2.0) / (full * breadth)
    last = np.zeros((depth, 2 * half))
    last[:, : depth + 1] = np.cos(one).T * weight
    last[:, half : half + depth + 1] = np.sin(one).T * weight

    def halves(x):
        high = x.astype(BF16)
        return high, (x - high.astype(np.float64)).astype(BF16)

    first_high, first_low = halves(first)
    last_high, last_low = halves(last)
    return {
        "first_two": np.concatenate([first_high, first_low], axis=1),
        "first_three": np.concatenate([first_high, first_high, first_low], axis=1),
        "mid": mid.astype(np.float32),
        "forward": np.stack(halves(np.block([[cos_two, sin_two], [-sin_two, cos_two]]))),
        "backward": np.stack(halves(np.block([[cos_two, -sin_two], [sin_two, cos_two]]))),
        "last": np.concatenate([last_high, last_high, last_low], axis=1),
    }


def kernel_call(
    kernel,
    out_shape,
    scalars,
    arrays,
    scratch=(),
    flops=0,
    grant=16,
    hbm_in=(),
    hbm_out=(),
    from_hbm=(),
):
    single = not isinstance(out_shape, tuple)
    outs = (out_shape,) if single else out_shape

    def spec(at, hbm):
        return pl.BlockSpec(memory_space=pltpu.HBM if at in hbm else pltpu.VMEM)

    arrays = [
        pltpu.with_memory_space_constraint(jnp.asarray(x), pltpu.HBM) if at in hbm_in + from_hbm else x
        for at, x in enumerate(arrays)
    ]
    in_specs = [pl.BlockSpec(memory_space=pltpu.SMEM)] * len(scalars)
    in_specs += [spec(at, hbm_in) for at in range(len(arrays))]
    out_specs = tuple(spec(at, hbm_out) for at in range(len(outs)))
    moved = sum(x.size * x.dtype.itemsize for x in (*arrays, *outs))
    placed = tuple(
        pltpu.HBM(x.shape, x.dtype) if at in hbm_out else x for at, x in enumerate(outs)
    )
    return pl.pallas_call(
        kernel,
        out_shape=placed[0] if single else placed,
        in_specs=in_specs,
        out_specs=out_specs[0] if single else out_specs,
        scratch_shapes=list(scratch),
        compiler_params=pltpu.CompilerParams(vmem_limit_bytes=grant * 1024 * 1024),
        cost_estimate=pl.CostEstimate(flops=flops, bytes_accessed=moved, transcendentals=0),
    )(*scalars, *arrays)


def pack_kernel(x_ref, first_ref, value_ref, taps_ref, query_ref, key_ref, value_head_ref, weight_ref, rows_ref, own_ref, other_ref):
    n_tp = rows_ref.shape[0]
    rows = query_ref.shape[0]
    part = rows // n_tp
    for at, ref in enumerate((query_ref, key_ref, value_head_ref)):
        rows_ref[:, at * part : (at + 1) * part, :] = ref[...].reshape(n_tp, part, -1)
    rows_ref[:, 3 * part :, :] = weight_ref[...]
    n_z, _, lanes = own_ref.shape
    per = 2 * n_z * lanes // first_ref.shape[1]
    channels = lanes // per
    low = x_ref[0] == 0
    for group in range(2 * n_z // per):
        span = slice(group * lanes, (group + 1) * lanes)
        shorts, edges = [], []
        for ref, which in ((first_ref, 0), (value_ref, 2)):
            x = ref[:, span].astype(F32)
            shorts.append(
                taps_ref[3 * which, :, span] * x
                + taps_ref[3 * which + 1, :, span] * pltpu.roll(x, 1, 0)
                + taps_ref[3 * which + 2, :, span] * pltpu.roll(x, 2, 0)
            )
            edges += [x[:2], x[rows - 2 :]]
        turned = (shorts[0] * shorts[1]).T
        edges = jnp.concatenate(edges, axis=0)
        for at in range(per // 2):
            z_at = group * per // 2 + at
            blocks = []
            for x_at in range(2):
                j = 2 * at + x_at
                edge = pltpu.roll(edges, lanes - j * channels, 1) if j else edges
                blocks.append(jnp.concatenate([turned[j * channels : (j + 1) * channels], edge], axis=0))
            own_ref[z_at] = jnp.where(low, blocks[0], blocks[1]).astype(BF16)
            other_ref[z_at] = jnp.where(low, blocks[1], blocks[0]).astype(BF16)


def repack_kernel(
    x_ref, rows_ref, own_hbm, got_ref, out_hbm, weight_hbm, own_ref, out_ref, sems
):
    n_tp, height, wide = rows_ref.shape
    channels = weight_hbm.shape[1]
    size = height - channels
    heads = wide // HD
    fetch = pltpu.make_async_copy(own_hbm, own_ref, sems.at[0])
    fetch.start()
    pass_on = pltpu.make_async_copy(rows_ref.at[:, size:, :], weight_hbm, sems.at[1])
    pass_on.start()
    for at in range(n_tp):
        for head in range(heads):
            block = rows_ref[at, :size, head * HD : (head + 1) * HD]
            out_ref[at * heads + head, :size, :] = block
    low = x_ref[0] == 0
    fetch.wait()
    own, got = own_ref[...].astype(F32), got_ref[...].astype(F32)
    even = jnp.where(low, own, got).astype(BF16)
    odd = jnp.where(low, got, own).astype(BF16)
    out_ref[:, size : size + channels, :] = even[:, :channels]
    out_ref[:, size + channels : size + 2 * channels, :] = odd[:, :channels]
    out_ref[:, size + 2 * channels : size + 2 * channels + 8, :] = even[:, channels:]
    out_ref[:, size + 2 * channels + 8 :, :] = odd[:, channels:]
    store = pltpu.make_async_copy(out_ref, out_hbm, sems.at[2])
    store.start()
    store.wait()
    pass_on.wait()


def split_kernel(part, mixed_ref, pairs_hbm, query_ref, block_ref, sems):
    n_z = mixed_ref.shape[0]
    for at in range(2):
        block = mixed_ref[:, (at + 1) * part : (at + 2) * part, :]
        block_ref[at] = block.reshape(n_z * part, HD)
    stores = [
        pltpu.make_async_copy(block_ref, pairs_hbm.at[to], sems.at[to])
        for to in range(pairs_hbm.shape[0])
    ]
    for store in stores:
        store.start()
    query_ref[...] = mixed_ref[:, :part, :].reshape(n_z * part, HD)
    for store in stores:
        store.wait()


def split_two(x):
    high = x.astype(BF16)
    return high, (x - high.astype(F32)).astype(BF16)


def dot_three(x, high, low):
    x_high, x_low = split_two(x)
    rows = ((1,), (0,))
    return dot(x_high, high, rows) + (dot(x_low, high, rows) + dot(x_high, low, rows))


def turn(real, imag, cos_mid, sin_mid, turned_ref, span):
    breadth = cos_mid.shape[1]
    turned_ref[span, :breadth] = real * cos_mid - imag * sin_mid
    turned_ref[span, breadth:] = real * sin_mid + imag * cos_mid


def spectrum_kernel(filter_ref, first_ref, mid_ref, forward_ref, out_ref, turned_ref):
    channels = filter_ref.shape[0]
    half = mid_ref.shape[1]
    cos_mid, sin_mid = mid_ref[0], mid_ref[1]
    for at in range(channels):
        high, low = split_two(filter_ref[at])
        both = dot(first_ref[...], jnp.concatenate([high, low, high], axis=0), ((1,), (0,)))
        turn(both[:half], both[half:], cos_mid, sin_mid, turned_ref, slice(at * half, (at + 1) * half))
    step = 4 * half
    for at in range(channels // 4):
        span = slice(at * step, (at + 1) * step)
        out_ref[span, :] = dot_three(turned_ref[span, :], forward_ref[0], forward_ref[1])


def signal_kernel(
    start,
    mixed_ref,
    taps_ref,
    spectrum_ref,
    first_ref,
    mid_ref,
    forward_ref,
    out_ref,
    signal_ref,
    done_ref,
    turned_ref,
):
    done_ref[...] = jnp.zeros_like(done_ref)
    rows, half = mid_ref.shape[2], mid_ref.shape[1]
    channels = out_ref.shape[0] // half
    n_seq = signal_ref.shape[0] // channels
    count = n_seq * 8
    edges = mixed_ref[:, start + 2 * channels :, :].astype(F32).reshape(count, rows).T[:channels]
    lane = lax.broadcasted_iota(jnp.int32, (channels, count), 1)
    kind = lane % 8
    before = jnp.where(lane >= 8, 1.0, 0.0)
    ahead = jnp.where(kind % 4 == 0, pltpu.roll(edges, 5, 1) * before, pltpu.roll(edges, 1, 1))
    further = pltpu.roll(edges, 6, 1) * before
    tap = [jnp.where(kind < 4, taps_ref[:, i : i + 1], taps_ref[:, 6 + i : 7 + i]) for i in range(3)]
    short = tap[0] * edges + tap[1] * ahead + tap[2] * further
    made = (short * pltpu.roll(short, count - 4, 1)).astype(BF16).astype(F32)
    column = lax.broadcasted_iota(jnp.int32, (channels, rows), 1)
    for at in range(n_seq):
        turned = pltpu.roll(made, count - 8 * at, 1) if at else made
        begin = start + at % 2 * channels
        block = mixed_ref[at // 2, begin : begin + channels, :].astype(F32)
        signal_ref[at * channels : (at + 1) * channels, :] = jnp.where(
            column < 2, turned[:, :rows], block
        )
    cos_mid, sin_mid = mid_ref[0], mid_ref[1]
    for at in range(channels):
        signal = signal_ref[pl.ds(at, n_seq, stride=channels), :].astype(BF16)
        both = dot(first_ref[...], jnp.concatenate([signal, signal], axis=0), ((1,), (0,)))
        turn(both[:half], both[half:], cos_mid, sin_mid, turned_ref, slice(at * half, (at + 1) * half))
    step = 4 * half
    for group in range(channels // 4):
        span = slice(group * step, (group + 1) * step)
        mine = dot_three(turned_ref[span, :], forward_ref[0], forward_ref[1])
        real, imag = mine[:, :rows], mine[:, rows:]
        other_real, other_imag = spectrum_ref[span, :rows], spectrum_ref[span, rows:]
        out_ref[span, :rows] = real * other_real - imag * other_imag
        out_ref[span, rows:] = real * other_imag + imag * other_real


def convolve_kernel(
    gain_ref, joined_ref, signal_ref, mid_ref, backward_ref, last_ref, out_ref, long_ref
):
    n_seq, channels, rows = out_ref.shape
    half = mid_ref.shape[1]
    cos_mid, sin_mid = mid_ref[0], mid_ref[1]
    step = 4 * half
    for group in range(channels // 4):
        span = slice(group * step, (group + 1) * step)
        mid = dot_three(joined_ref[span, :], backward_ref[0], backward_ref[1])
        for at in range(4):
            real, imag = (mid[at * half : (at + 1) * half, c * rows : (c + 1) * rows] for c in (0, 1))
            back = jnp.concatenate(
                [real * cos_mid + imag * sin_mid, imag * cos_mid - real * sin_mid], axis=0
            )
            high, low = split_two(back)
            out = dot(last_ref[...], jnp.concatenate([high, low, high], axis=0), ((1,), (0,)))
            channel = group * 4 + at
            strided = pl.ds(channel, n_seq, stride=channels)
            long_ref[strided, :] = out + gain_ref[channel] * signal_ref[strided, :]
    out_ref[...] = long_ref[...].astype(BF16).reshape(n_seq, channels, rows)


def attend(delta, query_ref, pairs_ref, tile, few, rows):
    size = 128
    query = query_ref[tile * size : (tile + 1) * size, :]
    row = lax.broadcasted_iota(jnp.int32, (size, size), 0)
    column = lax.broadcasted_iota(jnp.int32, (size, size), 1)
    q_pos = row // few * rows + row % few
    k_pos = column // few * rows + column % few
    parts = []
    for at in range(pairs_ref.shape[0]):
        allowed = k_pos + (at * few + delta) <= q_pos
        for start, stop in ((0, tile * size), (tile * size, (tile + 1) * size)):
            if start == stop:
                continue
            keys = pairs_ref[at, 0, start:stop, :]
            scores = dot(query, keys, ((1,), (1,))) * (1.0 / math.sqrt(HD))
            if start == tile * size:
                parts.append((jnp.where(allowed, scores, -1e30), allowed, at, start, stop))
            else:
                parts.append((scores, None, at, start, stop))
    highest = parts[0][0].max(axis=1, keepdims=True)
    for part in parts[1:]:
        highest = jnp.maximum(highest, part[0].max(axis=1, keepdims=True))
    totals = jnp.zeros((size, 1), F32)
    weighted = jnp.zeros((size, HD), F32)
    for scores, allowed, at, start, stop in parts:
        probs = jnp.exp(scores - highest)
        if allowed is not None:
            probs = jnp.where(allowed, probs, 0.0)
        totals = totals + probs.sum(axis=1, keepdims=True)
        values = pairs_ref[at, 1, start:stop, :]
        weighted = weighted + dot(probs.astype(BF16), values, ((1,), (0,)))
    some = totals > 0.0
    totals = jnp.maximum(totals, 1e-30)
    return weighted / totals, jnp.where(some, highest + jnp.log(totals), -1e30)


def other_kernel(rows, few, delta_ref, query_ref, pairs_ref, done_ref, out_ref, log_ref):
    own_rows = query_ref.shape[0]
    log_ref[...] = jnp.zeros_like(log_ref)
    for tile in range(own_rows // 128):
        out, log = attend(delta_ref[0], query_ref, pairs_ref, tile, few, rows)
        out_ref[tile * 128 : (tile + 1) * 128, :] = out.astype(BF16)
        line = jnp.broadcast_to(log, (128, 128)).T[:8]
        first = line.astype(BF16).astype(F32)
        second = (line - first).astype(BF16).astype(F32)
        third = line - first - second
        for at, term in enumerate((first, second, third)):
            log_ref[at * 8 + tile : at * 8 + tile + 1, :] = term[:1]
    out_ref[own_rows:, :] = log_ref[...].astype(BF16)


def own_kernel(rows, few, delta_ref, query_ref, pairs_ref, out_ref, log_ref):
    for tile in range(query_ref.shape[0] // 128):
        span = slice(tile * 128, (tile + 1) * 128)
        out, log = attend(delta_ref[0], query_ref, pairs_ref, tile, few, rows)
        out_ref[span, :] = out
        log_ref[span, :] = jnp.broadcast_to(log, (128, 128))


def merge_kernel(own_ref, log_ref, got_ref, long_ref, out_ref):
    own_rows = own_ref.shape[0]
    few = own_rows // out_ref.shape[0]
    per = 128 // few
    logs = got_ref[own_rows:, :].astype(F32)
    for tile in range(own_rows // 128):
        span = slice(tile * 128, (tile + 1) * 128)
        log = log_ref[span, :]
        line = logs[tile : tile + 1] + logs[8 + tile : 9 + tile] + logs[16 + tile : 17 + tile]
        got_log = jnp.broadcast_to(line, (128, 128)).T
        highest = jnp.maximum(log, got_log)
        own_share, got_share = jnp.exp(log - highest), jnp.exp(got_log - highest)
        merged = own_ref[span, :] * own_share + got_ref[span, :].astype(F32) * got_share
        merged = (merged / (own_share + got_share)).astype(BF16).reshape(per, few, HD)
        out_ref[tile * per : (tile + 1) * per, :few, :] = merged
    out_ref[:, few:, :] = long_ref[...]


def rows_kernel(
    x_ref, back_ref, rows_hbm, own_hbm, other_hbm, rows_ref, own_ref, other_ref, sems
):
    part = rows_ref.shape[0]
    channels = own_ref.shape[1]
    count = rows_hbm.shape[0]
    for head in range(back_ref.shape[0]):
        rows_ref[:, head * HD : (head + 1) * HD] = back_ref[head, :part, :]
    stores = [pltpu.make_async_copy(rows_ref, rows_hbm.at[to], sems.at[to]) for to in range(count)]
    for store in stores:
        store.start()
    low = x_ref[0] == 0
    even = back_ref[:, part : part + channels, :].astype(F32)
    odd = back_ref[:, part + channels :, :].astype(F32)
    own_ref[...] = jnp.where(low, even, odd).astype(BF16)
    other_ref[...] = jnp.where(low, odd, even).astype(BF16)
    stores += [
        pltpu.make_async_copy(own_ref, own_hbm, sems.at[count]),
        pltpu.make_async_copy(other_ref, other_hbm, sems.at[count + 1]),
    ]
    for store in stores[count:]:
        store.start()
    for store in stores:
        store.wait()


def gate_kernel(x_ref, own_ref, got_ref, gate_ref, tail_ref, taps_ref, out_ref):
    rows = gate_ref.shape[0]
    lanes = 128
    channels = own_ref.shape[1]
    per = lanes // channels
    row = lax.broadcasted_iota(jnp.int32, (rows, lanes), 0)
    low = x_ref[0] == 0
    for group in range(gate_ref.shape[1] // lanes):
        span = slice(group * lanes, (group + 1) * lanes)
        x = gate_ref[:, span].astype(F32)
        tail = tail_ref[:, span].astype(F32)
        one = jnp.where(row == 0, tail[1:2], pltpu.roll(x, 1, 0))
        two = jnp.where(row == 0, tail[0:1], jnp.where(row == 1, tail[1:2], pltpu.roll(x, 2, 0)))
        short = taps_ref[0:1, span] * x + taps_ref[1:2, span] * one + taps_ref[2:3, span] * two
        blocks = []
        for at in range(per // 2):
            own = own_ref[group * per // 2 + at].astype(F32)
            got = got_ref[group * per // 2 + at].astype(F32)
            blocks += [jnp.where(low, own, got), jnp.where(low, got, own)]
        out_ref[:, span] = (short * jnp.concatenate(blocks, axis=0).T).astype(BF16)


def project_kernel(x_ref, rows_ref, weight_ref, own_ref, other_ref):
    half = own_ref.shape[0]
    n_z, n_tp, channels, wide = weight_ref.shape
    part = rows_ref.shape[1]
    whole = rows_ref[...].reshape(2 * half, n_tp * wide)
    out = jnp.zeros((2 * half, n_z * channels), F32)
    for at in range(n_tp):
        block = weight_ref[:, at].reshape(n_z * channels, wide)
        out = out + dot(whole[:, at * wide : (at + 1) * wide], block, ((1,), (1,)))
    low = x_ref[0] == 0
    own_ref[...] = jnp.where(low, out[:half], out[half:]).astype(BF16)
    other_ref[...] = jnp.where(low, out[half:], out[:half]).astype(BF16)


def unite_kernel(channels, x_ref, own_ref, got_ref, out_ref):
    rows, lanes = own_ref.shape[0], 128
    low = x_ref[0] == 0
    lane = lax.broadcasted_iota(jnp.int32, (rows, lanes), 1)
    for group in range(out_ref.shape[1] // lanes):
        span = slice(group // 2 * lanes, (group // 2 + 1) * lanes)
        start = group % 2 * 2 * channels
        own, got = own_ref[:, span].astype(F32), got_ref[:, span].astype(F32)
        even, odd = jnp.where(low, own, got), jnp.where(low, got, own)

        def moved(x, by):
            by = by % lanes
            return pltpu.roll(x, by, 1) if by else x

        left = jnp.where(lane < channels, moved(even, -start), moved(odd, channels - start))
        right = jnp.where(
            lane < 3 * channels, moved(even, channels - start), moved(odd, 2 * channels - start)
        )
        out_ref[:, group * lanes : (group + 1) * lanes] = jnp.where(
            lane < 2 * channels, left, right
        ).astype(BF16)


def body(
    first_stream,
    gate_stream,
    value_stream,
    short_taps,
    long_filter,
    skip_gain,
    queries,
    attn_keys,
    attn_values,
    out_weight,
):
    seq = ("z", "xh")
    n_z, n_x, n_tp = lax.axis_size("z"), lax.axis_size("xh"), lax.axis_size("tp")
    n_seq, n_plane = n_z * n_x, n_x * n_tp
    seq_at = lax.axis_index(seq)
    x_at = lax.axis_index("xh")
    x_scalar = x_at.astype(jnp.int32).reshape(1)
    rows = queries.shape[1]
    wide = queries.shape[2]
    channels = long_filter.shape[3]
    part = rows // n_tp
    own_rows = n_z * part
    taps = short_taps[0]
    swap = [(0, 1), (1, 0)]
    shape = jax.ShapeDtypeStruct

    sent_rows, own, other = kernel_call(
        pack_kernel,
        (
            shape((n_tp, 3 * part + channels, wide), BF16),
            shape((n_z, channels + 8, rows), BF16),
            shape((n_z, channels + 8, rows), BF16),
        ),
        (x_scalar,),
        (
            first_stream[0],
            value_stream[0],
            short_taps.reshape(9, 1, -1),
            queries[0],
            attn_keys[0],
            attn_values[0],
            out_weight[0].transpose(1, 2, 0),
        ),
        grant=56,
    )
    got = lax.ppermute(other, "xh", swap)
    got_rows = lax.all_to_all(sent_rows, "tp", 0, 0)
    packed, weight = kernel_call(
        repack_kernel,
        (
            shape((n_z, 3 * part + 2 * channels + 16, HD), BF16),
            shape((n_tp, channels, wide), BF16),
        ),
        (x_scalar,),
        (got_rows, own, got),
        (
            pltpu.VMEM((n_z, channels + 8, rows), BF16),
            pltpu.VMEM((n_z, 3 * part + 2 * channels + 16, HD), BF16),
            pltpu.SemaphoreType.DMA((3,)),
        ),
        hbm_in=(1,),
        hbm_out=(0, 1),
    )
    mixed = lax.all_to_all(packed, "z", 0, 0)
    weight = lax.all_gather(weight, "z")

    n_sec = lax.axis_size("section")
    onward = [(i, (i + 1) % n_sec) for i in range(n_sec)]
    gate = lax.ppermute(gate_stream[0], "section", onward)
    gate_taps = lax.ppermute(taps[1], "section", onward)
    tail = lax.ppermute(
        gate_stream[0, -2:],
        ("section",) + seq,
        [(s * n_seq + i, t * n_seq + i + 1) for s, t in onward for i in range(n_seq - 1)],
    )
    local_taps = lax.dynamic_slice_in_dim(taps, seq_at * channels, channels, 2)
    local_taps = local_taps.reshape(9, channels).T
    tables = transform_tables(n_seq, rows)
    half = tables["mid"].shape[1]
    kernel_spec = kernel_call(
        spectrum_kernel,
        shape((channels * half, 2 * rows), F32),
        (),
        (
            long_filter[0, 0, 0].reshape(channels, n_seq, rows),
            tables["first_three"],
            tables["mid"],
            tables["forward"],
        ),
        (pltpu.VMEM((channels * half, 2 * rows), F32),),
        from_hbm=(1, 2, 3),
    )
    mixed, gate, gate_taps, tail, local_taps, kernel_spec = lax.optimization_barrier(
        (mixed, gate, gate_taps, tail, local_taps, kernel_spec)
    )

    sent_pairs, query = kernel_call(
        functools.partial(split_kernel, part),
        (shape((n_tp, 2, own_rows, HD), BF16), shape((own_rows, HD), BF16)),
        (),
        (mixed,),
        (pltpu.VMEM((2, own_rows, HD), BF16), pltpu.SemaphoreType.DMA((n_tp,))),
        hbm_out=(0,),
    )
    other_query = lax.ppermute(query, "xh", swap)
    pairs = lax.all_to_all(sent_pairs, "tp", 0, 0)

    gain = lax.dynamic_slice_in_dim(skip_gain[0], seq_at * channels, channels, 0)
    joined, signal, done = kernel_call(
        functools.partial(signal_kernel, 3 * part),
        (
            shape((channels * half, 2 * rows), F32),
            shape((n_seq * channels, rows), F32),
            shape((8, rows), F32),
        ),
        (),
        (
            mixed,
            local_taps,
            kernel_spec,
            tables["first_two"],
            tables["mid"],
            tables["forward"],
        ),
        (pltpu.VMEM((channels * half, 2 * rows), F32),),
        from_hbm=(3, 4, 5),
    )
    work = 2 * own_rows * n_tp * own_rows * HD
    own_delta = -lax.axis_index("tp") * part
    other_delta = (2 * x_at - 1) * rows + own_delta
    sent = kernel_call(
        functools.partial(other_kernel, n_x * rows, part),
        shape((own_rows + 32, HD), BF16),
        (other_delta.astype(jnp.int32).reshape(1),),
        (other_query, pairs, done),
        (pltpu.VMEM((32, HD), F32),),
        work,
    )
    got = lax.ppermute(sent, "xh", swap)
    query, sent = lax.optimization_barrier((query, sent))
    own_out, own_log = kernel_call(
        functools.partial(own_kernel, n_x * rows, part),
        (shape((own_rows, HD), F32),) * 2,
        (own_delta.astype(jnp.int32).reshape(1),),
        (query, pairs),
        (),
        work,
    )
    long_out = kernel_call(
        convolve_kernel,
        shape((n_seq, channels, rows), BF16),
        (gain,),
        (joined, signal, tables["mid"], tables["backward"], tables["last"]),
        (pltpu.VMEM((n_seq * channels, rows), F32),),
        from_hbm=(2, 3, 4),
    )
    returned = kernel_call(
        merge_kernel,
        shape((n_z, part + n_x * channels, HD), BF16),
        (),
        (own_out, own_log, got, long_out.reshape(n_z, n_x * channels, rows)),
    )
    back = lax.all_to_all(returned, "z", 0, 0)
    back, weight = lax.optimization_barrier((back, weight))

    plane_rows, own_long, other_long = kernel_call(
        rows_kernel,
        (
            shape((n_plane, part, n_z * HD), BF16),
            shape((n_z, channels, rows), BF16),
            shape((n_z, channels, rows), BF16),
        ),
        (x_scalar,),
        (back,),
        (
            pltpu.VMEM((part, n_z * HD), BF16),
            pltpu.VMEM((n_z, channels, rows), BF16),
            pltpu.VMEM((n_z, channels, rows), BF16),
            pltpu.SemaphoreType.DMA((n_plane + 2,)),
        ),
        hbm_out=(0, 1, 2),
    )
    plane_rows = lax.all_to_all(plane_rows, ("xh", "tp"), 0, 0)
    own_long = lax.ppermute(own_long, "section", onward)
    got_long = lax.ppermute(
        other_long, ("section", "xh"), [(2 * s + x, 2 * t + 1 - x) for s, t in onward for x in range(2)]
    )
    handed = kernel_call(
        gate_kernel,
        shape(gate_stream.shape[1:], BF16),
        (x_scalar,),
        (own_long, got_long, gate, tail, gate_taps),
    )
    own_out, other_out = kernel_call(
        project_kernel,
        (shape((rows, n_z * channels), BF16),) * 2,
        (x_scalar,),
        (plane_rows, weight),
        (),
        4 * rows * n_tp * wide * n_z * channels,
    )
    got_out = lax.ppermute(other_out, "xh", swap)
    attended = kernel_call(
        functools.partial(unite_kernel, channels),
        shape(handed.shape, BF16),
        (x_scalar,),
        (own_out, got_out),
    )
    return (handed[None], attended[None])


def solution(mesh):
    n_sec, n_seq, n_tp = (mesh.shape[name] for name in ("section", "seq", "tp"))
    finer = Mesh(mesh.devices.reshape(n_sec, n_seq // 2, 2, n_tp), ("section", "z", "xh", "tp"))
    seq = ("z", "xh")
    placed = (
        P("section", seq, "tp"),
        P("section", seq, "tp"),
        P("section", seq, "tp"),
        P("section", None, None, "tp"),
        P("section", "tp", seq, None, None),
        P("section", "tp"),
        P("section", seq, "tp"),
        P("section", seq, "tp"),
        P("section", seq, "tp"),
        P("section", "tp", None, seq),
    )
    return jax.shard_map(
        body,
        mesh=finer,
        in_specs=placed,
        out_specs=(P("section", seq, "tp"), P("section", seq, "tp")),
        check_vma=False,
    )
```

```python
import functools
import math

import jax
import jax.numpy as jnp
import numpy as np
from jax import lax
from jax.experimental import pallas as pl
from jax.experimental.pallas import tpu as pltpu
from jax.sharding import Mesh, PartitionSpec as P

HD = 128
BF16 = jnp.bfloat16
F32 = jnp.float32


def dot(left, right, contract):
    return lax.dot_general(left, right, (contract, ((), ())), preferred_element_type=F32)


def transform_tables(depth, breadth):
    full = 2 * depth
    half = -(-(depth + 1) // 8) * 8
    k = np.arange(depth + 1)
    b = np.arange(breadth)
    one = -2.0 * np.pi * np.outer(k, np.arange(depth)) / full
    first = np.zeros((2 * half, depth))
    first[: depth + 1], first[half : half + depth + 1] = np.cos(one), np.sin(one)
    angle = -2.0 * np.pi * np.outer(k, b) / (full * breadth)
    mid = np.zeros((2, half, breadth))
    mid[0, : depth + 1], mid[1, : depth + 1] = np.cos(angle), np.sin(angle)
    two = -2.0 * np.pi * (np.outer(b, b) % breadth) / breadth
    cos_two, sin_two = np.cos(two), np.sin(two)
    weight = np.where((k == 0) | (k == depth), 1.0, 2.0) / (full * breadth)
    last = np.zeros((depth, 2 * half))
    last[:, : depth + 1] = np.cos(one).T * weight
    last[:, half : half + depth + 1] = np.sin(one).T * weight

    def halves(x):
        high = x.astype(BF16)
        return high, (x - high.astype(np.float64)).astype(BF16)

    first_high, first_low = halves(first)
    last_high, last_low = halves(last)
    return {
        "first_two": np.concatenate([first_high, first_low], axis=1),
        "first_three": np.concatenate([first_high, first_high, first_low], axis=1),
        "mid": mid.astype(np.float32),
        "forward": np.stack(halves(np.block([[cos_two, sin_two], [-sin_two, cos_two]]))),
        "backward": np.stack(halves(np.block([[cos_two, -sin_two], [sin_two, cos_two]]))),
        "last": np.concatenate([last_high, last_high, last_low], axis=1),
    }


def kernel_call(
    kernel,
    out_shape,
    scalars,
    arrays,
    scratch=(),
    flops=0,
    grant=16,
    hbm_in=(),
    hbm_out=(),
    from_hbm=(),
):
    single = not isinstance(out_shape, tuple)
    outs = (out_shape,) if single else out_shape

    def spec(at, hbm):
        return pl.BlockSpec(memory_space=pltpu.HBM if at in hbm else pltpu.VMEM)

    arrays = [
        pltpu.with_memory_space_constraint(jnp.asarray(x), pltpu.HBM) if at in hbm_in + from_hbm else x
        for at, x in enumerate(arrays)
    ]
    in_specs = [pl.BlockSpec(memory_space=pltpu.SMEM)] * len(scalars)
    in_specs += [spec(at, hbm_in) for at in range(len(arrays))]
    out_specs = tuple(spec(at, hbm_out) for at in range(len(outs)))
    moved = sum(x.size * x.dtype.itemsize for x in (*arrays, *outs))
    placed = tuple(
        pltpu.HBM(x.shape, x.dtype) if at in hbm_out else x for at, x in enumerate(outs)
    )
    return pl.pallas_call(
        kernel,
        out_shape=placed[0] if single else placed,
        in_specs=in_specs,
        out_specs=out_specs[0] if single else out_specs,
        scratch_shapes=list(scratch),
        compiler_params=pltpu.CompilerParams(vmem_limit_bytes=grant * 1024 * 1024),
        cost_estimate=pl.CostEstimate(flops=flops, bytes_accessed=moved, transcendentals=0),
    )(*scalars, *arrays)


def pack_kernel(x_ref, first_ref, value_ref, taps_ref, query_ref, key_ref, value_head_ref, weight_ref, rows_ref, own_ref, other_ref):
    n_tp = rows_ref.shape[0]
    rows = query_ref.shape[0]
    part = rows // n_tp
    for at, ref in enumerate((query_ref, key_ref, value_head_ref)):
        rows_ref[:, at * part : (at + 1) * part, :] = ref[...].reshape(n_tp, part, -1)
    rows_ref[:, 3 * part :, :] = weight_ref[...]
    n_z, _, lanes = own_ref.shape
    per = 2 * n_z * lanes // first_ref.shape[1]
    channels = lanes // per
    low = x_ref[0] == 0
    lane = lax.broadcasted_iota(jnp.int32, (1, lanes), 1)
    for group in range(2 * n_z // per):
        span = slice(group * lanes, (group + 1) * lanes)
        shorts, edges = [], []
        for ref, which in ((first_ref, 0), (value_ref, 2)):
            x = ref[:, span].astype(F32)
            shorts.append(
                taps_ref[3 * which, :, span] * x
                + taps_ref[3 * which + 1, :, span] * pltpu.roll(x, 1, 0)
                + taps_ref[3 * which + 2, :, span] * pltpu.roll(x, 2, 0)
            )
            edges += [x[:2], x[rows - 2 :]]
        turned = (shorts[0] * shorts[1]).T
        edges = jnp.concatenate(edges, axis=0)
        moved = [pltpu.roll(edges, d * channels, 1) if d else edges for d in range(per)]
        for at in range(per // 2):
            z_at = group * per // 2 + at
            blocks = []
            for x_at in range(2):
                j = 2 * at + x_at
                lines = [turned[j * channels : (j + 1) * channels]]
                for row in range(2):
                    line = moved[(per - 1 - j) % per][row * per + per - 1 : (row + 1) * per]
                    for kind in reversed(range(per - 1)):
                        piece = moved[(kind - j) % per][row * per + kind : row * per + kind + 1]
                        line = jnp.where(lane < (kind + 1) * channels, piece, line)
                    lines.append(line)
                lines.append(jnp.zeros((6, lanes), F32))
                blocks.append(jnp.concatenate(lines, axis=0))
            own_ref[z_at] = jnp.where(low, blocks[0], blocks[1]).astype(BF16)
            other_ref[z_at] = jnp.where(low, blocks[1], blocks[0]).astype(BF16)


def repack_kernel(
    x_ref, rows_ref, own_hbm, got_ref, out_hbm, weight_hbm, own_ref, out_ref, sems
):
    n_tp, height, wide = rows_ref.shape
    channels = weight_hbm.shape[1]
    size = height - channels
    heads = wide // HD
    fetch = pltpu.make_async_copy(own_hbm, own_ref, sems.at[0])
    fetch.start()
    pass_on = pltpu.make_async_copy(rows_ref.at[:, size:, :], weight_hbm, sems.at[1])
    pass_on.start()
    for at in range(n_tp):
        for head in range(heads):
            block = rows_ref[at, :size, head * HD : (head + 1) * HD]
            out_ref[at * heads + head, :size, :] = block
    low = x_ref[0] == 0
    fetch.wait()
    own, got = own_ref[...].astype(F32), got_ref[...].astype(F32)
    even, odd = jnp.where(low, own, got), jnp.where(low, got, own)
    out_ref[:, size : size + channels, :] = even[:, :channels].astype(BF16)
    out_ref[:, size + channels : size + 2 * channels, :] = odd[:, :channels].astype(BF16)
    row = lax.broadcasted_iota(jnp.int32, (1, 8, HD), 1)
    lines = jnp.where(row < 2, even[:, channels:], pltpu.roll(odd[:, channels:], 2, 1))
    out_ref[:, size + 2 * channels :, :] = lines.astype(BF16)
    store = pltpu.make_async_copy(out_ref, out_hbm, sems.at[2])
    store.start()
    store.wait()
    pass_on.wait()


def split_kernel(part, mixed_ref, pairs_hbm, query_ref, block_ref, sems):
    n_z = mixed_ref.shape[0]
    for at in range(2):
        block = mixed_ref[:, (at + 1) * part : (at + 2) * part, :]
        block_ref[at] = block.reshape(n_z * part, HD)
    stores = [
        pltpu.make_async_copy(block_ref, pairs_hbm.at[to], sems.at[to])
        for to in range(pairs_hbm.shape[0])
    ]
    for store in stores:
        store.start()
    query_ref[...] = mixed_ref[:, :part, :].reshape(n_z * part, HD)
    for store in stores:
        store.wait()


def split_two(x):
    high = x.astype(BF16)
    return high, (x - high.astype(F32)).astype(BF16)


def dot_three(x, high, low):
    x_high, x_low = split_two(x)
    rows = ((1,), (0,))
    return dot(x_high, high, rows) + (dot(x_low, high, rows) + dot(x_high, low, rows))


def turn(real, imag, cos_mid, sin_mid, turned_ref, span):
    breadth = cos_mid.shape[1]
    turned_ref[span, :breadth] = real * cos_mid - imag * sin_mid
    turned_ref[span, breadth:] = real * sin_mid + imag * cos_mid


def spectrum_kernel(filter_ref, first_ref, mid_ref, forward_ref, out_ref, turned_ref):
    channels = filter_ref.shape[0]
    half = mid_ref.shape[1]
    cos_mid, sin_mid = mid_ref[0], mid_ref[1]
    for at in range(channels):
        high, low = split_two(filter_ref[at])
        both = dot(first_ref[...], jnp.concatenate([high, low, high], axis=0), ((1,), (0,)))
        turn(both[:half], both[half:], cos_mid, sin_mid, turned_ref, slice(at * half, (at + 1) * half))
    step = 4 * half
    for at in range(channels // 4):
        span = slice(at * step, (at + 1) * step)
        out_ref[span, :] = dot_three(turned_ref[span, :], forward_ref[0], forward_ref[1])


def signal_kernel(
    start,
    mixed_ref,
    taps_ref,
    spectrum_ref,
    first_ref,
    mid_ref,
    forward_ref,
    out_ref,
    signal_ref,
    done_ref,
    turned_ref,
):
    done_ref[...] = jnp.zeros_like(done_ref)
    rows, half = mid_ref.shape[2], mid_ref.shape[1]
    channels = out_ref.shape[0] // half
    n_seq = signal_ref.shape[0] // channels
    count = n_seq * 4
    edges = mixed_ref[:, start + 2 * channels :, :].astype(F32).reshape(count, rows).T
    zeroth, first, last_but_one, last = (
        edges[kind * channels : (kind + 1) * channels] for kind in range(4)
    )
    lane = lax.broadcasted_iota(jnp.int32, (channels, count), 1)

    def before(x):
        moved = jnp.where(lane % 8 < 2, pltpu.roll(x, 6, 1), pltpu.roll(x, 2, 1))
        return jnp.where(lane < 2, 0.0, moved)

    is_first = lane % 2 == 0
    tap = [jnp.where(is_first, taps_ref[:, i : i + 1], taps_ref[:, 6 + i : 7 + i]) for i in range(3)]
    zero = tap[0] * zeroth + tap[1] * before(last) + tap[2] * before(last_but_one)
    one = tap[0] * first + tap[1] * zeroth + tap[2] * before(last)
    zero = zero * pltpu.roll(zero, count - 1, 1)
    one = one * pltpu.roll(one, count - 1, 1)
    made = jnp.where(is_first, zero, pltpu.roll(one, 1, 1)).astype(BF16).astype(F32)
    column = lax.broadcasted_iota(jnp.int32, (channels, rows), 1)
    for at in range(n_seq):
        lane_at = at // 2 * 8 + at % 2 * 2
        turned = pltpu.roll(made, count - lane_at, 1) if at else made
        begin = start + at % 2 * channels
        block = mixed_ref[at // 2, begin : begin + channels, :].astype(F32)
        signal_ref[at * channels : (at + 1) * channels, :] = jnp.where(
            column < 2, turned[:, :rows], block
        )
    cos_mid, sin_mid = mid_ref[0], mid_ref[1]
    for at in range(channels):
        signal = signal_ref[pl.ds(at, n_seq, stride=channels), :].astype(BF16)
        both = dot(first_ref[...], jnp.concatenate([signal, signal], axis=0), ((1,), (0,)))
        turn(both[:half], both[half:], cos_mid, sin_mid, turned_ref, slice(at * half, (at + 1) * half))
    step = 4 * half
    for group in range(channels // 4):
        span = slice(group * step, (group + 1) * step)
        mine = dot_three(turned_ref[span, :], forward_ref[0], forward_ref[1])
        real, imag = mine[:, :rows], mine[:, rows:]
        other_real, other_imag = spectrum_ref[span, :rows], spectrum_ref[span, rows:]
        out_ref[span, :rows] = real * other_real - imag * other_imag
        out_ref[span, rows:] = real * other_imag + imag * other_real


def convolve_kernel(
    gain_ref, joined_ref, signal_ref, mid_ref, backward_ref, last_ref, out_ref, long_ref
):
    n_seq, channels, rows = out_ref.shape
    half = mid_ref.shape[1]
    cos_mid, sin_mid = mid_ref[0], mid_ref[1]
    step = 4 * half
    for group in range(channels // 4):
        span = slice(group * step, (group + 1) * step)
        mid = dot_three(joined_ref[span, :], backward_ref[0], backward_ref[1])
        for at in range(4):
            real, imag = (mid[at * half : (at + 1) * half, c * rows : (c + 1) * rows] for c in (0, 1))
            back = jnp.concatenate(
                [real * cos_mid + imag * sin_mid, imag * cos_mid - real * sin_mid], axis=0
            )
            high, low = split_two(back)
            out = dot(last_ref[...], jnp.concatenate([high, low, high], axis=0), ((1,), (0,)))
            channel = group * 4 + at
            strided = pl.ds(channel, n_seq, stride=channels)
            long_ref[strided, :] = out + gain_ref[channel] * signal_ref[strided, :]
    out_ref[...] = long_ref[...].astype(BF16).reshape(n_seq, channels, rows)


def attend(delta, query_ref, pairs_ref, tile, few, rows):
    size = 128
    query = query_ref[tile * size : (tile + 1) * size, :]
    row = lax.broadcasted_iota(jnp.int32, (size, size), 0)
    column = lax.broadcasted_iota(jnp.int32, (size, size), 1)
    q_pos = row // few * rows + row % few
    k_pos = column // few * rows + column % few
    parts = []
    for at in range(pairs_ref.shape[0]):
        allowed = k_pos + (at * few + delta) <= q_pos
        for start, stop in ((0, tile * size), (tile * size, (tile + 1) * size)):
            if start == stop:
                continue
            keys = pairs_ref[at, 0, start:stop, :]
            scores = dot(query, keys, ((1,), (1,))) * (1.0 / math.sqrt(HD))
            if start == tile * size:
                parts.append((jnp.where(allowed, scores, -1e30), allowed, at, start, stop))
            else:
                parts.append((scores, None, at, start, stop))
    highest = parts[0][0].max(axis=1, keepdims=True)
    for part in parts[1:]:
        highest = jnp.maximum(highest, part[0].max(axis=1, keepdims=True))
    totals = jnp.zeros((size, 1), F32)
    weighted = jnp.zeros((size, HD), F32)
    for scores, allowed, at, start, stop in parts:
        probs = jnp.exp(scores - highest)
        if allowed is not None:
            probs = jnp.where(allowed, probs, 0.0)
        totals = totals + probs.sum(axis=1, keepdims=True)
        values = pairs_ref[at, 1, start:stop, :]
        weighted = weighted + dot(probs.astype(BF16), values, ((1,), (0,)))
    some = totals > 0.0
    totals = jnp.maximum(totals, 1e-30)
    return weighted / totals, jnp.where(some, highest + jnp.log(totals), -1e30)


def other_kernel(rows, few, delta_ref, query_ref, pairs_ref, done_ref, out_ref, log_ref):
    own_rows = query_ref.shape[0]
    log_ref[...] = jnp.zeros_like(log_ref)
    for tile in range(own_rows // 128):
        out, log = attend(delta_ref[0], query_ref, pairs_ref, tile, few, rows)
        out_ref[tile * 128 : (tile + 1) * 128, :] = out.astype(BF16)
        line = jnp.broadcast_to(log, (128, 128)).T[:8]
        first = line.astype(BF16).astype(F32)
        second = (line - first).astype(BF16).astype(F32)
        third = line - first - second
        for at, term in enumerate((first, second, third)):
            log_ref[at * 8 + tile : at * 8 + tile + 1, :] = term[:1]
    out_ref[own_rows:, :] = log_ref[...].astype(BF16)


def own_kernel(rows, few, delta_ref, query_ref, pairs_ref, out_ref, log_ref):
    for tile in range(query_ref.shape[0] // 128):
        span = slice(tile * 128, (tile + 1) * 128)
        out, log = attend(delta_ref[0], query_ref, pairs_ref, tile, few, rows)
        out_ref[span, :] = out
        log_ref[span, :] = jnp.broadcast_to(log, (128, 128))


def merge_kernel(own_ref, log_ref, got_ref, long_ref, out_ref):
    own_rows = own_ref.shape[0]
    few = own_rows // out_ref.shape[0]
    per = 128 // few
    logs = got_ref[own_rows:, :].astype(F32)
    for tile in range(own_rows // 128):
        span = slice(tile * 128, (tile + 1) * 128)
        log = log_ref[span, :]
        line = logs[tile : tile + 1] + logs[8 + tile : 9 + tile] + logs[16 + tile : 17 + tile]
        got_log = jnp.broadcast_to(line, (128, 128)).T
        highest = jnp.maximum(log, got_log)
        own_share, got_share = jnp.exp(log - highest), jnp.exp(got_log - highest)
        merged = own_ref[span, :] * own_share + got_ref[span, :].astype(F32) * got_share
        merged = (merged / (own_share + got_share)).astype(BF16).reshape(per, few, HD)
        out_ref[tile * per : (tile + 1) * per, :few, :] = merged
    out_ref[:, few:, :] = long_ref[...]


def rows_kernel(
    x_ref, back_ref, rows_hbm, own_hbm, other_hbm, rows_ref, own_ref, other_ref, sems
):
    part = rows_ref.shape[0]
    channels = own_ref.shape[1]
    count = rows_hbm.shape[0]
    for head in range(back_ref.shape[0]):
        rows_ref[:, head * HD : (head + 1) * HD] = back_ref[head, :part, :]
    stores = [pltpu.make_async_copy(rows_ref, rows_hbm.at[to], sems.at[to]) for to in range(count)]
    for store in stores:
        store.start()
    low = x_ref[0] == 0
    even = back_ref[:, part : part + channels, :].astype(F32)
    odd = back_ref[:, part + channels :, :].astype(F32)
    own_ref[...] = jnp.where(low, even, odd).astype(BF16)
    other_ref[...] = jnp.where(low, odd, even).astype(BF16)
    stores += [
        pltpu.make_async_copy(own_ref, own_hbm, sems.at[count]),
        pltpu.make_async_copy(other_ref, other_hbm, sems.at[count + 1]),
    ]
    for store in stores[count:]:
        store.start()
    for store in stores:
        store.wait()


def gate_kernel(x_ref, own_ref, got_ref, gate_ref, tail_ref, taps_ref, out_ref):
    rows = gate_ref.shape[0]
    lanes = 128
    channels = own_ref.shape[1]
    per = lanes // channels
    row = lax.broadcasted_iota(jnp.int32, (rows, lanes), 0)
    low = x_ref[0] == 0
    for group in range(gate_ref.shape[1] // lanes):
        span = slice(group * lanes, (group + 1) * lanes)
        x = gate_ref[:, span].astype(F32)
        tail = tail_ref[:, span].astype(F32)
        one = jnp.where(row == 0, tail[1:2], pltpu.roll(x, 1, 0))
        two = jnp.where(row == 0, tail[0:1], jnp.where(row == 1, tail[1:2], pltpu.roll(x, 2, 0)))
        short = taps_ref[0:1, span] * x + taps_ref[1:2, span] * one + taps_ref[2:3, span] * two
        blocks = []
        for at in range(per // 2):
            own = own_ref[group * per // 2 + at].astype(F32)
            got = got_ref[group * per // 2 + at].astype(F32)
            blocks += [jnp.where(low, own, got), jnp.where(low, got, own)]
        out_ref[:, span] = (short * jnp.concatenate(blocks, axis=0).T).astype(BF16)


def project_kernel(x_ref, rows_ref, weight_ref, own_ref, other_ref):
    half = own_ref.shape[0]
    n_z, n_tp, channels, wide = weight_ref.shape
    part = rows_ref.shape[1]
    whole = rows_ref[...].reshape(2 * half, n_tp * wide)
    out = jnp.zeros((2 * half, n_z * channels), F32)
    for at in range(n_tp):
        block = weight_ref[:, at].reshape(n_z * channels, wide)
        out = out + dot(whole[:, at * wide : (at + 1) * wide], block, ((1,), (1,)))
    low = x_ref[0] == 0
    own_ref[...] = jnp.where(low, out[:half], out[half:]).astype(BF16)
    other_ref[...] = jnp.where(low, out[half:], out[:half]).astype(BF16)


def unite_kernel(channels, x_ref, own_ref, got_ref, out_ref):
    rows, lanes = own_ref.shape[0], 128
    low = x_ref[0] == 0
    lane = lax.broadcasted_iota(jnp.int32, (rows, lanes), 1)
    for group in range(out_ref.shape[1] // lanes):
        span = slice(group // 2 * lanes, (group // 2 + 1) * lanes)
        start = group % 2 * 2 * channels
        own, got = own_ref[:, span].astype(F32), got_ref[:, span].astype(F32)
        even, odd = jnp.where(low, own, got), jnp.where(low, got, own)

        def moved(x, by):
            by = by % lanes
            return pltpu.roll(x, by, 1) if by else x

        left = jnp.where(lane < channels, moved(even, -start), moved(odd, channels - start))
        right = jnp.where(
            lane < 3 * channels, moved(even, channels - start), moved(odd, 2 * channels - start)
        )
        out_ref[:, group * lanes : (group + 1) * lanes] = jnp.where(
            lane < 2 * channels, left, right
        ).astype(BF16)


def body(
    first_stream,
    gate_stream,
    value_stream,
    short_taps,
    long_filter,
    skip_gain,
    queries,
    attn_keys,
    attn_values,
    out_weight,
):
    seq = ("z", "xh")
    n_z, n_x, n_tp = lax.axis_size("z"), lax.axis_size("xh"), lax.axis_size("tp")
    n_seq, n_plane = n_z * n_x, n_x * n_tp
    seq_at = lax.axis_index(seq)
    x_at = lax.axis_index("xh")
    x_scalar = x_at.astype(jnp.int32).reshape(1)
    rows = queries.shape[1]
    wide = queries.shape[2]
    channels = long_filter.shape[3]
    part = rows // n_tp
    own_rows = n_z * part
    taps = short_taps[0]
    swap = [(0, 1), (1, 0)]
    shape = jax.ShapeDtypeStruct

    sent_rows, own, other = kernel_call(
        pack_kernel,
        (
            shape((n_tp, 3 * part + channels, wide), BF16),
            shape((n_z, channels + 8, rows), BF16),
            shape((n_z, channels + 8, rows), BF16),
        ),
        (x_scalar,),
        (
            first_stream[0],
            value_stream[0],
            short_taps.reshape(9, 1, -1),
            queries[0],
            attn_keys[0],
            attn_values[0],
            out_weight[0].transpose(1, 2, 0),
        ),
        grant=56,
    )
    got = lax.ppermute(other, "xh", swap)
    got_rows = lax.all_to_all(sent_rows, "tp", 0, 0)
    packed, weight = kernel_call(
        repack_kernel,
        (
            shape((n_z, 3 * part + 2 * channels + 8, HD), BF16),
            shape((n_tp, channels, wide), BF16),
        ),
        (x_scalar,),
        (got_rows, own, got),
        (
            pltpu.VMEM((n_z, channels + 8, rows), BF16),
            pltpu.VMEM((n_z, 3 * part + 2 * channels + 8, HD), BF16),
            pltpu.SemaphoreType.DMA((3,)),
        ),
        hbm_in=(1,),
        hbm_out=(0, 1),
    )
    mixed = lax.all_to_all(packed, "z", 0, 0)
    weight = lax.all_gather(weight, "z")

    n_sec = lax.axis_size("section")
    onward = [(i, (i + 1) % n_sec) for i in range(n_sec)]
    gate = lax.ppermute(gate_stream[0], "section", onward)
    gate_taps = lax.ppermute(taps[1], "section", onward)
    tail = lax.ppermute(
        gate_stream[0, -2:],
        ("section",) + seq,
        [(s * n_seq + i, t * n_seq + i + 1) for s, t in onward for i in range(n_seq - 1)],
    )
    local_taps = lax.dynamic_slice_in_dim(taps, seq_at * channels, channels, 2)
    local_taps = local_taps.reshape(9, channels).T
    tables = transform_tables(n_seq, rows)
    half = tables["mid"].shape[1]
    kernel_spec = kernel_call(
        spectrum_kernel,
        shape((channels * half, 2 * rows), F32),
        (),
        (
            long_filter[0, 0, 0].reshape(channels, n_seq, rows),
            tables["first_three"],
            tables["mid"],
            tables["forward"],
        ),
        (pltpu.VMEM((channels * half, 2 * rows), F32),),
        from_hbm=(1, 2, 3),
    )
    mixed, gate, gate_taps, tail, local_taps, kernel_spec = lax.optimization_barrier(
        (mixed, gate, gate_taps, tail, local_taps, kernel_spec)
    )

    sent_pairs, query = kernel_call(
        functools.partial(split_kernel, part),
        (shape((n_tp, 2, own_rows, HD), BF16), shape((own_rows, HD), BF16)),
        (),
        (mixed,),
        (pltpu.VMEM((2, own_rows, HD), BF16), pltpu.SemaphoreType.DMA((n_tp,))),
        hbm_out=(0,),
    )
    other_query = lax.ppermute(query, "xh", swap)
    pairs = lax.all_to_all(sent_pairs, "tp", 0, 0)

    gain = lax.dynamic_slice_in_dim(skip_gain[0], seq_at * channels, channels, 0)
    joined, signal, done = kernel_call(
        functools.partial(signal_kernel, 3 * part),
        (
            shape((channels * half, 2 * rows), F32),
            shape((n_seq * channels, rows), F32),
            shape((8, rows), F32),
        ),
        (),
        (
            mixed,
            local_taps,
            kernel_spec,
            tables["first_two"],
            tables["mid"],
            tables["forward"],
        ),
        (pltpu.VMEM((channels * half, 2 * rows), F32),),
        from_hbm=(3, 4, 5),
    )
    work = 2 * own_rows * n_tp * own_rows * HD
    own_delta = -lax.axis_index("tp") * part
    other_delta = (2 * x_at - 1) * rows + own_delta
    sent = kernel_call(
        functools.partial(other_kernel, n_x * rows, part),
        shape((own_rows + 32, HD), BF16),
        (other_delta.astype(jnp.int32).reshape(1),),
        (other_query, pairs, done),
        (pltpu.VMEM((32, HD), F32),),
        work,
    )
    got = lax.ppermute(sent, "xh", swap)
    query, sent = lax.optimization_barrier((query, sent))
    own_out, own_log = kernel_call(
        functools.partial(own_kernel, n_x * rows, part),
        (shape((own_rows, HD), F32),) * 2,
        (own_delta.astype(jnp.int32).reshape(1),),
        (query, pairs),
        (),
        work,
    )
    long_out = kernel_call(
        convolve_kernel,
        shape((n_seq, channels, rows), BF16),
        (gain,),
        (joined, signal, tables["mid"], tables["backward"], tables["last"]),
        (pltpu.VMEM((n_seq * channels, rows), F32),),
        from_hbm=(2, 3, 4),
    )
    returned = kernel_call(
        merge_kernel,
        shape((n_z, part + n_x * channels, HD), BF16),
        (),
        (own_out, own_log, got, long_out.reshape(n_z, n_x * channels, rows)),
    )
    back = lax.all_to_all(returned, "z", 0, 0)
    back, weight = lax.optimization_barrier((back, weight))

    plane_rows, own_long, other_long = kernel_call(
        rows_kernel,
        (
            shape((n_plane, part, n_z * HD), BF16),
            shape((n_z, channels, rows), BF16),
            shape((n_z, channels, rows), BF16),
        ),
        (x_scalar,),
        (back,),
        (
            pltpu.VMEM((part, n_z * HD), BF16),
            pltpu.VMEM((n_z, channels, rows), BF16),
            pltpu.VMEM((n_z, channels, rows), BF16),
            pltpu.SemaphoreType.DMA((n_plane + 2,)),
        ),
        hbm_out=(0, 1, 2),
    )
    plane_rows = lax.all_to_all(plane_rows, ("xh", "tp"), 0, 0)
    own_long = lax.ppermute(own_long, "section", onward)
    got_long = lax.ppermute(
        other_long, ("section", "xh"), [(2 * s + x, 2 * t + 1 - x) for s, t in onward for x in range(2)]
    )
    handed = kernel_call(
        gate_kernel,
        shape(gate_stream.shape[1:], BF16),
        (x_scalar,),
        (own_long, got_long, gate, tail, gate_taps),
    )
    own_out, other_out = kernel_call(
        project_kernel,
        (shape((rows, n_z * channels), BF16),) * 2,
        (x_scalar,),
        (plane_rows, weight),
        (),
        4 * rows * n_tp * wide * n_z * channels,
    )
    got_out = lax.ppermute(other_out, "xh", swap)
    attended = kernel_call(
        functools.partial(unite_kernel, channels),
        shape(handed.shape, BF16),
        (x_scalar,),
        (own_out, got_out),
    )
    return (handed[None], attended[None])


def solution(mesh):
    n_sec, n_seq, n_tp = (mesh.shape[name] for name in ("section", "seq", "tp"))
    finer = Mesh(mesh.devices.reshape(n_sec, n_seq // 2, 2, n_tp), ("section", "z", "xh", "tp"))
    seq = ("z", "xh")
    placed = (
        P("section", seq, "tp"),
        P("section", seq, "tp"),
        P("section", seq, "tp"),
        P("section", None, None, "tp"),
        P("section", "tp", seq, None, None),
        P("section", "tp"),
        P("section", seq, "tp"),
        P("section", seq, "tp"),
        P("section", seq, "tp"),
        P("section", "tp", None, seq),
    )
    return jax.shard_map(
        body,
        mesh=finer,
        in_specs=placed,
        out_specs=(P("section", seq, "tp"), P("section", seq, "tp")),
        check_vma=False,
    )
```

```python
import functools
import math

import jax
import jax.numpy as jnp
import numpy as np
from jax import lax
from jax.experimental import pallas as pl
from jax.experimental.pallas import tpu as pltpu
from jax.sharding import Mesh, PartitionSpec as P

HD = 128
BF16 = jnp.bfloat16
F32 = jnp.float32


def dot(left, right, contract):
    return lax.dot_general(left, right, (contract, ((), ())), preferred_element_type=F32)


def transform_tables(depth, breadth):
    full = 2 * depth
    half = -(-(depth + 1) // 8) * 8
    k = np.arange(depth + 1)
    b = np.arange(breadth)
    one = -2.0 * np.pi * np.outer(k, np.arange(depth)) / full
    first = np.zeros((2 * half, depth))
    first[: depth + 1], first[half : half + depth + 1] = np.cos(one), np.sin(one)
    angle = -2.0 * np.pi * np.outer(k, b) / (full * breadth)
    mid = np.zeros((2, half, breadth))
    mid[0, : depth + 1], mid[1, : depth + 1] = np.cos(angle), np.sin(angle)
    two = -2.0 * np.pi * (np.outer(b, b) % breadth) / breadth
    cos_two, sin_two = np.cos(two), np.sin(two)
    weight = np.where((k == 0) | (k == depth), 1.0, 2.0) / (full * breadth)
    last = np.zeros((depth, 2 * half))
    last[:, : depth + 1] = np.cos(one).T * weight
    last[:, half : half + depth + 1] = np.sin(one).T * weight

    def halves(x):
        high = x.astype(BF16)
        return high, (x - high.astype(np.float64)).astype(BF16)

    first_high, first_low = halves(first)
    last_high, last_low = halves(last)
    return {
        "first_two": np.concatenate([first_high, first_low], axis=1),
        "first_three": np.concatenate([first_high, first_high, first_low], axis=1),
        "mid": mid.astype(np.float32),
        "forward": np.stack(halves(np.block([[cos_two, sin_two], [-sin_two, cos_two]]))),
        "backward": np.stack(halves(np.block([[cos_two, -sin_two], [sin_two, cos_two]]))),
        "last": np.concatenate([last_high, last_high, last_low], axis=1),
    }


def kernel_call(
    kernel,
    out_shape,
    scalars,
    arrays,
    scratch=(),
    flops=0,
    grant=16,
    hbm_in=(),
    hbm_out=(),
    from_hbm=(),
):
    single = not isinstance(out_shape, tuple)
    outs = (out_shape,) if single else out_shape

    def spec(at, hbm):
        return pl.BlockSpec(memory_space=pltpu.HBM if at in hbm else pltpu.VMEM)

    arrays = [
        pltpu.with_memory_space_constraint(jnp.asarray(x), pltpu.HBM) if at in hbm_in + from_hbm else x
        for at, x in enumerate(arrays)
    ]
    in_specs = [pl.BlockSpec(memory_space=pltpu.SMEM)] * len(scalars)
    in_specs += [spec(at, hbm_in) for at in range(len(arrays))]
    out_specs = tuple(spec(at, hbm_out) for at in range(len(outs)))
    moved = sum(x.size * x.dtype.itemsize for x in (*arrays, *outs))
    placed = tuple(
        pltpu.HBM(x.shape, x.dtype) if at in hbm_out else x for at, x in enumerate(outs)
    )
    return pl.pallas_call(
        kernel,
        out_shape=placed[0] if single else placed,
        in_specs=in_specs,
        out_specs=out_specs[0] if single else out_specs,
        scratch_shapes=list(scratch),
        compiler_params=pltpu.CompilerParams(vmem_limit_bytes=grant * 1024 * 1024),
        cost_estimate=pl.CostEstimate(flops=flops, bytes_accessed=moved, transcendentals=0),
    )(*scalars, *arrays)


def pack_kernel(x_ref, first_ref, value_ref, taps_ref, query_ref, key_ref, value_head_ref, weight_ref, rows_ref, own_ref, other_ref):
    n_tp = rows_ref.shape[0]
    rows = query_ref.shape[0]
    part = rows // n_tp
    for at, ref in enumerate((query_ref, key_ref, value_head_ref)):
        rows_ref[:, at * part : (at + 1) * part, :] = ref[...].reshape(n_tp, part, -1)
    rows_ref[:, 3 * part :, :] = weight_ref[...]
    n_z, _, lanes = own_ref.shape
    per = 2 * n_z * lanes // first_ref.shape[1]
    channels = lanes // per
    low = x_ref[0] == 0
    lane = lax.broadcasted_iota(jnp.int32, (1, lanes), 1)
    for group in range(2 * n_z // per):
        span = slice(group * lanes, (group + 1) * lanes)
        shorts, edges = [], []
        for ref, which in ((first_ref, 0), (value_ref, 2)):
            x = ref[:, span].astype(F32)
            shorts.append(
                taps_ref[3 * which, :, span] * x
                + taps_ref[3 * which + 1, :, span] * pltpu.roll(x, 1, 0)
                + taps_ref[3 * which + 2, :, span] * pltpu.roll(x, 2, 0)
            )
            edges += [x[:2], x[rows - 2 :]]
        turned = (shorts[0] * shorts[1]).T
        edges = jnp.concatenate(edges, axis=0)
        moved = [pltpu.roll(edges, d * channels, 1) if d else edges for d in range(per)]
        for at in range(per // 2):
            z_at = group * per // 2 + at
            blocks = []
            for x_at in range(2):
                j = 2 * at + x_at
                lines = [turned[j * channels : (j + 1) * channels]]
                for row in range(2):
                    line = moved[(per - 1 - j) % per][row * per + per - 1 : (row + 1) * per]
                    for kind in reversed(range(per - 1)):
                        piece = moved[(kind - j) % per][row * per + kind : row * per + kind + 1]
                        line = jnp.where(lane < (kind + 1) * channels, piece, line)
                    lines.append(line)
                lines.append(jnp.zeros((6, lanes), F32))
                blocks.append(jnp.concatenate(lines, axis=0))
            own_ref[z_at] = jnp.where(low, blocks[0], blocks[1]).astype(BF16)
            other_ref[z_at] = jnp.where(low, blocks[1], blocks[0]).astype(BF16)


def repack_kernel(
    x_ref, rows_ref, own_hbm, got_ref, out_hbm, weight_hbm, own_ref, out_ref, sems
):
    n_tp, height, wide = rows_ref.shape
    channels = weight_hbm.shape[1]
    size = height - channels
    heads = wide // HD
    fetch = pltpu.make_async_copy(own_hbm, own_ref, sems.at[0])
    fetch.start()
    pass_on = pltpu.make_async_copy(rows_ref.at[:, size:, :], weight_hbm, sems.at[1])
    pass_on.start()
    for at in range(n_tp):
        for head in range(heads):
            block = rows_ref[at, :size, head * HD : (head + 1) * HD]
            out_ref[at * heads + head, :size, :] = block
    low = x_ref[0] == 0
    fetch.wait()
    own, got = own_ref[...].astype(F32), got_ref[...].astype(F32)
    even, odd = jnp.where(low, own, got), jnp.where(low, got, own)
    out_ref[:, size : size + channels, :] = even[:, :channels].astype(BF16)
    out_ref[:, size + channels : size + 2 * channels, :] = odd[:, :channels].astype(BF16)
    row = lax.broadcasted_iota(jnp.int32, (1, 8, HD), 1)
    lines = jnp.where(row < 2, even[:, channels:], pltpu.roll(odd[:, channels:], 2, 1))
    out_ref[:, size + 2 * channels :, :] = lines.astype(BF16)
    store = pltpu.make_async_copy(out_ref, out_hbm, sems.at[2])
    store.start()
    store.wait()
    pass_on.wait()


def split_kernel(part, mixed_ref, pairs_hbm, query_ref, block_ref, sems):
    n_z = mixed_ref.shape[0]
    for at in range(2):
        block = mixed_ref[:, (at + 1) * part : (at + 2) * part, :]
        block_ref[at] = block.reshape(n_z * part, HD)
    stores = [
        pltpu.make_async_copy(block_ref, pairs_hbm.at[to], sems.at[to])
        for to in range(pairs_hbm.shape[0])
    ]
    for store in stores:
        store.start()
    query_ref[...] = mixed_ref[:, :part, :].reshape(n_z * part, HD)
    for store in stores:
        store.wait()


def split_two(x):
    high = x.astype(BF16)
    return high, (x - high.astype(F32)).astype(BF16)


def dot_three(x, high, low):
    x_high, x_low = split_two(x)
    rows = ((1,), (0,))
    return dot(x_high, high, rows) + (dot(x_low, high, rows) + dot(x_high, low, rows))


def turn(real, imag, cos_mid, sin_mid, turned_ref, span):
    breadth = cos_mid.shape[1]
    turned_ref[span, :breadth] = real * cos_mid - imag * sin_mid
    turned_ref[span, breadth:] = real * sin_mid + imag * cos_mid


def spectrum_kernel(filter_ref, first_ref, mid_ref, forward_ref, out_ref, turned_ref):
    channels = filter_ref.shape[0]
    half = mid_ref.shape[1]
    cos_mid, sin_mid = mid_ref[0], mid_ref[1]
    for at in range(channels):
        high, low = split_two(filter_ref[at])
        both = dot(first_ref[...], jnp.concatenate([high, low, high], axis=0), ((1,), (0,)))
        turn(both[:half], both[half:], cos_mid, sin_mid, turned_ref, slice(at * half, (at + 1) * half))
    step = 4 * half
    for at in range(channels // 4):
        span = slice(at * step, (at + 1) * step)
        out_ref[span, :] = dot_three(turned_ref[span, :], forward_ref[0], forward_ref[1])


def signal_kernel(
    start,
    mixed_ref,
    taps_ref,
    spectrum_ref,
    first_ref,
    mid_ref,
    forward_ref,
    out_hbm,
    signal_hbm,
    done_ref,
    turned_ref,
    out_ref,
    signal_ref,
    sems,
):
    done_ref[...] = jnp.zeros_like(done_ref)
    rows, half = mid_ref.shape[2], mid_ref.shape[1]
    channels = out_ref.shape[0] // half
    n_seq = signal_ref.shape[0] // channels
    count = n_seq * 4
    edges = mixed_ref[:, start + 2 * channels :, :].astype(F32).reshape(count, rows).T
    zeroth, first, last_but_one, last = (
        edges[kind * channels : (kind + 1) * channels] for kind in range(4)
    )
    lane = lax.broadcasted_iota(jnp.int32, (channels, count), 1)

    def before(x):
        moved = jnp.where(lane % 8 < 2, pltpu.roll(x, 6, 1), pltpu.roll(x, 2, 1))
        return jnp.where(lane < 2, 0.0, moved)

    is_first = lane % 2 == 0
    tap = [jnp.where(is_first, taps_ref[:, i : i + 1], taps_ref[:, 6 + i : 7 + i]) for i in range(3)]
    zero = tap[0] * zeroth + tap[1] * before(last) + tap[2] * before(last_but_one)
    one = tap[0] * first + tap[1] * zeroth + tap[2] * before(last)
    zero = zero * pltpu.roll(zero, count - 1, 1)
    one = one * pltpu.roll(one, count - 1, 1)
    made = jnp.where(is_first, zero, pltpu.roll(one, 1, 1)).astype(BF16).astype(F32)
    column = lax.broadcasted_iota(jnp.int32, (channels, rows), 1)
    for at in range(n_seq):
        lane_at = at // 2 * 8 + at % 2 * 2
        turned = pltpu.roll(made, count - lane_at, 1) if at else made
        begin = start + at % 2 * channels
        block = mixed_ref[at // 2, begin : begin + channels, :].astype(F32)
        signal_ref[at * channels : (at + 1) * channels, :] = jnp.where(
            column < 2, turned[:, :rows], block
        )
    stores = [pltpu.make_async_copy(signal_ref, signal_hbm, sems.at[0])]
    stores[0].start()
    cos_mid, sin_mid = mid_ref[0], mid_ref[1]
    for at in range(channels):
        signal = signal_ref[pl.ds(at, n_seq, stride=channels), :].astype(BF16)
        both = dot(first_ref[...], jnp.concatenate([signal, signal], axis=0), ((1,), (0,)))
        turn(both[:half], both[half:], cos_mid, sin_mid, turned_ref, slice(at * half, (at + 1) * half))
    step = 4 * half
    for group in range(channels // 4):
        span = slice(group * step, (group + 1) * step)
        mine = dot_three(turned_ref[span, :], forward_ref[0], forward_ref[1])
        real, imag = mine[:, :rows], mine[:, rows:]
        other_real, other_imag = spectrum_ref[span, :rows], spectrum_ref[span, rows:]
        out_ref[span, :rows] = real * other_real - imag * other_imag
        out_ref[span, rows:] = real * other_imag + imag * other_real
        begin = pl.ds(group * step, step)
        store = pltpu.make_async_copy(out_ref.at[begin], out_hbm.at[begin], sems.at[group + 1])
        store.start()
        stores.append(store)
    for store in stores:
        store.wait()


def convolve_kernel(
    gain_ref, joined_ref, signal_ref, mid_ref, backward_ref, last_ref, out_ref, long_ref
):
    n_seq, channels, rows = out_ref.shape
    half = mid_ref.shape[1]
    cos_mid, sin_mid = mid_ref[0], mid_ref[1]
    step = 4 * half
    for group in range(channels // 4):
        span = slice(group * step, (group + 1) * step)
        mid = dot_three(joined_ref[span, :], backward_ref[0], backward_ref[1])
        for at in range(4):
            real, imag = (mid[at * half : (at + 1) * half, c * rows : (c + 1) * rows] for c in (0, 1))
            back = jnp.concatenate(
                [real * cos_mid + imag * sin_mid, imag * cos_mid - real * sin_mid], axis=0
            )
            high, low = split_two(back)
            out = dot(last_ref[...], jnp.concatenate([high, low, high], axis=0), ((1,), (0,)))
            channel = group * 4 + at
            strided = pl.ds(channel, n_seq, stride=channels)
            long_ref[strided, :] = out + gain_ref[channel] * signal_ref[strided, :]
    out_ref[...] = long_ref[...].astype(BF16).reshape(n_seq, channels, rows)


def attend(delta, query_ref, pairs_ref, tile, few, rows):
    size = 128
    query = query_ref[tile * size : (tile + 1) * size, :]
    row = lax.broadcasted_iota(jnp.int32, (size, size), 0)
    column = lax.broadcasted_iota(jnp.int32, (size, size), 1)
    q_pos = row // few * rows + row % few
    k_pos = column // few * rows + column % few
    parts = []
    for at in range(pairs_ref.shape[0]):
        allowed = k_pos + (at * few + delta) <= q_pos
        for start, stop in ((0, tile * size), (tile * size, (tile + 1) * size)):
            if start == stop:
                continue
            keys = pairs_ref[at, 0, start:stop, :]
            scores = dot(query, keys, ((1,), (1,))) * (1.0 / math.sqrt(HD))
            if start == tile * size:
                parts.append((jnp.where(allowed, scores, -1e30), allowed, at, start, stop))
            else:
                parts.append((scores, None, at, start, stop))
    highest = parts[0][0].max(axis=1, keepdims=True)
    for part in parts[1:]:
        highest = jnp.maximum(highest, part[0].max(axis=1, keepdims=True))
    totals = jnp.zeros((size, 1), F32)
    weighted = jnp.zeros((size, HD), F32)
    for scores, allowed, at, start, stop in parts:
        probs = jnp.exp(scores - highest)
        if allowed is not None:
            probs = jnp.where(allowed, probs, 0.0)
        totals = totals + probs.sum(axis=1, keepdims=True)
        values = pairs_ref[at, 1, start:stop, :]
        weighted = weighted + dot(probs.astype(BF16), values, ((1,), (0,)))
    some = totals > 0.0
    totals = jnp.maximum(totals, 1e-30)
    return weighted / totals, jnp.where(some, highest + jnp.log(totals), -1e30)


def other_kernel(rows, few, delta_ref, query_ref, pairs_ref, done_ref, out_ref, log_ref):
    own_rows = query_ref.shape[0]
    log_ref[...] = jnp.zeros_like(log_ref)
    for tile in range(own_rows // 128):
        out, log = attend(delta_ref[0], query_ref, pairs_ref, tile, few, rows)
        out_ref[tile * 128 : (tile + 1) * 128, :] = out.astype(BF16)
        line = jnp.broadcast_to(log, (128, 128)).T[:8]
        first = line.astype(BF16).astype(F32)
        second = (line - first).astype(BF16).astype(F32)
        third = line - first - second
        for at, term in enumerate((first, second, third)):
            log_ref[at * 8 + tile : at * 8 + tile + 1, :] = term[:1]
    out_ref[own_rows:, :] = log_ref[...].astype(BF16)


def own_kernel(rows, few, delta_ref, query_ref, pairs_ref, out_ref, log_ref):
    for tile in range(query_ref.shape[0] // 128):
        span = slice(tile * 128, (tile + 1) * 128)
        out, log = attend(delta_ref[0], query_ref, pairs_ref, tile, few, rows)
        out_ref[span, :] = out
        log_ref[span, :] = jnp.broadcast_to(log, (128, 128))


def merge_kernel(own_ref, log_ref, got_ref, long_ref, out_ref):
    own_rows = own_ref.shape[0]
    few = own_rows // out_ref.shape[0]
    per = 128 // few
    logs = got_ref[own_rows:, :].astype(F32)
    for tile in range(own_rows // 128):
        span = slice(tile * 128, (tile + 1) * 128)
        log = log_ref[span, :]
        line = logs[tile : tile + 1] + logs[8 + tile : 9 + tile] + logs[16 + tile : 17 + tile]
        got_log = jnp.broadcast_to(line, (128, 128)).T
        highest = jnp.maximum(log, got_log)
        own_share, got_share = jnp.exp(log - highest), jnp.exp(got_log - highest)
        merged = own_ref[span, :] * own_share + got_ref[span, :].astype(F32) * got_share
        merged = (merged / (own_share + got_share)).astype(BF16).reshape(per, few, HD)
        out_ref[tile * per : (tile + 1) * per, :few, :] = merged
    out_ref[:, few:, :] = long_ref[...]


def rows_kernel(
    x_ref, back_ref, rows_hbm, own_hbm, other_hbm, rows_ref, own_ref, other_ref, sems
):
    part = rows_ref.shape[0]
    channels = own_ref.shape[1]
    count = rows_hbm.shape[0]
    for head in range(back_ref.shape[0]):
        rows_ref[:, head * HD : (head + 1) * HD] = back_ref[head, :part, :]
    stores = [pltpu.make_async_copy(rows_ref, rows_hbm.at[to], sems.at[to]) for to in range(count)]
    for store in stores:
        store.start()
    low = x_ref[0] == 0
    even = back_ref[:, part : part + channels, :].astype(F32)
    odd = back_ref[:, part + channels :, :].astype(F32)
    own_ref[...] = jnp.where(low, even, odd).astype(BF16)
    other_ref[...] = jnp.where(low, odd, even).astype(BF16)
    stores += [
        pltpu.make_async_copy(own_ref, own_hbm, sems.at[count]),
        pltpu.make_async_copy(other_ref, other_hbm, sems.at[count + 1]),
    ]
    for store in stores[count:]:
        store.start()
    for store in stores:
        store.wait()


def gate_kernel(x_ref, own_ref, got_ref, gate_ref, tail_ref, taps_ref, out_ref):
    rows = gate_ref.shape[0]
    lanes = 128
    channels = own_ref.shape[1]
    per = lanes // channels
    row = lax.broadcasted_iota(jnp.int32, (rows, lanes), 0)
    low = x_ref[0] == 0
    for group in range(gate_ref.shape[1] // lanes):
        span = slice(group * lanes, (group + 1) * lanes)
        x = gate_ref[:, span].astype(F32)
        tail = tail_ref[:, span].astype(F32)
        one = jnp.where(row == 0, tail[1:2], pltpu.roll(x, 1, 0))
        two = jnp.where(row == 0, tail[0:1], jnp.where(row == 1, tail[1:2], pltpu.roll(x, 2, 0)))
        short = taps_ref[0:1, span] * x + taps_ref[1:2, span] * one + taps_ref[2:3, span] * two
        blocks = []
        for at in range(per // 2):
            own = own_ref[group * per // 2 + at].astype(F32)
            got = got_ref[group * per // 2 + at].astype(F32)
            blocks += [jnp.where(low, own, got), jnp.where(low, got, own)]
        out_ref[:, span] = (short * jnp.concatenate(blocks, axis=0).T).astype(BF16)


def project_kernel(x_ref, rows_ref, weight_ref, own_ref, other_ref):
    half = own_ref.shape[0]
    n_z, n_tp, channels, wide = weight_ref.shape
    part = rows_ref.shape[1]
    whole = rows_ref[...].reshape(2 * half, n_tp * wide)
    out = jnp.zeros((2 * half, n_z * channels), F32)
    for at in range(n_tp):
        block = weight_ref[:, at].reshape(n_z * channels, wide)
        out = out + dot(whole[:, at * wide : (at + 1) * wide], block, ((1,), (1,)))
    low = x_ref[0] == 0
    own_ref[...] = jnp.where(low, out[:half], out[half:]).astype(BF16)
    other_ref[...] = jnp.where(low, out[half:], out[:half]).astype(BF16)


def unite_kernel(channels, x_ref, own_ref, got_ref, out_ref):
    rows, lanes = own_ref.shape[0], 128
    low = x_ref[0] == 0
    lane = lax.broadcasted_iota(jnp.int32, (rows, lanes), 1)
    for group in range(out_ref.shape[1] // lanes):
        span = slice(group // 2 * lanes, (group // 2 + 1) * lanes)
        start = group % 2 * 2 * channels
        own, got = own_ref[:, span].astype(F32), got_ref[:, span].astype(F32)
        even, odd = jnp.where(low, own, got), jnp.where(low, got, own)

        def moved(x, by):
            by = by % lanes
            return pltpu.roll(x, by, 1) if by else x

        left = jnp.where(lane < channels, moved(even, -start), moved(odd, channels - start))
        right = jnp.where(
            lane < 3 * channels, moved(even, channels - start), moved(odd, 2 * channels - start)
        )
        out_ref[:, group * lanes : (group + 1) * lanes] = jnp.where(
            lane < 2 * channels, left, right
        ).astype(BF16)


def body(
    first_stream,
    gate_stream,
    value_stream,
    short_taps,
    long_filter,
    skip_gain,
    queries,
    attn_keys,
    attn_values,
    out_weight,
):
    seq = ("z", "xh")
    n_z, n_x, n_tp = lax.axis_size("z"), lax.axis_size("xh"), lax.axis_size("tp")
    n_seq, n_plane = n_z * n_x, n_x * n_tp
    seq_at = lax.axis_index(seq)
    x_at = lax.axis_index("xh")
    x_scalar = x_at.astype(jnp.int32).reshape(1)
    rows = queries.shape[1]
    wide = queries.shape[2]
    channels = long_filter.shape[3]
    part = rows // n_tp
    own_rows = n_z * part
    taps = short_taps[0]
    swap = [(0, 1), (1, 0)]
    shape = jax.ShapeDtypeStruct

    sent_rows, own, other = kernel_call(
        pack_kernel,
        (
            shape((n_tp, 3 * part + channels, wide), BF16),
            shape((n_z, channels + 8, rows), BF16),
            shape((n_z, channels + 8, rows), BF16),
        ),
        (x_scalar,),
        (
            first_stream[0],
            value_stream[0],
            short_taps.reshape(9, 1, -1),
            queries[0],
            attn_keys[0],
            attn_values[0],
            out_weight[0].transpose(1, 2, 0),
        ),
        grant=56,
    )
    got = lax.ppermute(other, "xh", swap)
    got_rows = lax.all_to_all(sent_rows, "tp", 0, 0)
    packed, weight = kernel_call(
        repack_kernel,
        (
            shape((n_z, 3 * part + 2 * channels + 8, HD), BF16),
            shape((n_tp, channels, wide), BF16),
        ),
        (x_scalar,),
        (got_rows, own, got),
        (
            pltpu.VMEM((n_z, channels + 8, rows), BF16),
            pltpu.VMEM((n_z, 3 * part + 2 * channels + 8, HD), BF16),
            pltpu.SemaphoreType.DMA((3,)),
        ),
        hbm_in=(1,),
        hbm_out=(0, 1),
    )
    mixed = lax.all_to_all(packed, "z", 0, 0)
    weight = lax.all_gather(weight, "z")

    n_sec = lax.axis_size("section")
    onward = [(i, (i + 1) % n_sec) for i in range(n_sec)]
    gate = lax.ppermute(gate_stream[0], "section", onward)
    gate_taps = lax.ppermute(taps[1], "section", onward)
    tail = lax.ppermute(
        gate_stream[0, -2:],
        ("section",) + seq,
        [(s * n_seq + i, t * n_seq + i + 1) for s, t in onward for i in range(n_seq - 1)],
    )
    local_taps = lax.dynamic_slice_in_dim(taps, seq_at * channels, channels, 2)
    local_taps = local_taps.reshape(9, channels).T
    tables = transform_tables(n_seq, rows)
    half = tables["mid"].shape[1]
    kernel_spec = kernel_call(
        spectrum_kernel,
        shape((channels * half, 2 * rows), F32),
        (),
        (
            long_filter[0, 0, 0].reshape(channels, n_seq, rows),
            tables["first_three"],
            tables["mid"],
            tables["forward"],
        ),
        (pltpu.VMEM((channels * half, 2 * rows), F32),),
        from_hbm=(1, 2, 3),
    )
    mixed, gate, gate_taps, tail, local_taps, kernel_spec = lax.optimization_barrier(
        (mixed, gate, gate_taps, tail, local_taps, kernel_spec)
    )

    sent_pairs, query = kernel_call(
        functools.partial(split_kernel, part),
        (shape((n_tp, 2, own_rows, HD), BF16), shape((own_rows, HD), BF16)),
        (),
        (mixed,),
        (pltpu.VMEM((2, own_rows, HD), BF16), pltpu.SemaphoreType.DMA((n_tp,))),
        hbm_out=(0,),
    )
    other_query = lax.ppermute(query, "xh", swap)
    pairs = lax.all_to_all(sent_pairs, "tp", 0, 0)

    gain = lax.dynamic_slice_in_dim(skip_gain[0], seq_at * channels, channels, 0)
    joined, signal, done = kernel_call(
        functools.partial(signal_kernel, 3 * part),
        (
            shape((channels * half, 2 * rows), F32),
            shape((n_seq * channels, rows), F32),
            shape((8, rows), F32),
        ),
        (),
        (
            mixed,
            local_taps,
            kernel_spec,
            tables["first_two"],
            tables["mid"],
            tables["forward"],
        ),
        (
            pltpu.VMEM((channels * half, 2 * rows), F32),
            pltpu.VMEM((channels * half, 2 * rows), F32),
            pltpu.VMEM((n_seq * channels, rows), F32),
            pltpu.SemaphoreType.DMA((channels // 4 + 1,)),
        ),
        hbm_out=(0, 1),
        from_hbm=(3, 4, 5),
    )
    work = 2 * own_rows * n_tp * own_rows * HD
    own_delta = -lax.axis_index("tp") * part
    other_delta = (2 * x_at - 1) * rows + own_delta
    sent = kernel_call(
        functools.partial(other_kernel, n_x * rows, part),
        shape((own_rows + 32, HD), BF16),
        (other_delta.astype(jnp.int32).reshape(1),),
        (other_query, pairs, done),
        (pltpu.VMEM((32, HD), F32),),
        work,
    )
    got = lax.ppermute(sent, "xh", swap)
    query, sent = lax.optimization_barrier((query, sent))
    own_out, own_log = kernel_call(
        functools.partial(own_kernel, n_x * rows, part),
        (shape((own_rows, HD), F32),) * 2,
        (own_delta.astype(jnp.int32).reshape(1),),
        (query, pairs),
        (),
        work,
    )
    long_out = kernel_call(
        convolve_kernel,
        shape((n_seq, channels, rows), BF16),
        (gain,),
        (joined, signal, tables["mid"], tables["backward"], tables["last"]),
        (pltpu.VMEM((n_seq * channels, rows), F32),),
        from_hbm=(2, 3, 4),
    )
    returned = kernel_call(
        merge_kernel,
        shape((n_z, part + n_x * channels, HD), BF16),
        (),
        (own_out, own_log, got, long_out.reshape(n_z, n_x * channels, rows)),
    )
    back = lax.all_to_all(returned, "z", 0, 0)
    back, weight = lax.optimization_barrier((back, weight))

    plane_rows, own_long, other_long = kernel_call(
        rows_kernel,
        (
            shape((n_plane, part, n_z * HD), BF16),
            shape((n_z, channels, rows), BF16),
            shape((n_z, channels, rows), BF16),
        ),
        (x_scalar,),
        (back,),
        (
            pltpu.VMEM((part, n_z * HD), BF16),
            pltpu.VMEM((n_z, channels, rows), BF16),
            pltpu.VMEM((n_z, channels, rows), BF16),
            pltpu.SemaphoreType.DMA((n_plane + 2,)),
        ),
        hbm_out=(0, 1, 2),
    )
    plane_rows = lax.all_to_all(plane_rows, ("xh", "tp"), 0, 0)
    own_long = lax.ppermute(own_long, "section", onward)
    got_long = lax.ppermute(
        other_long, ("section", "xh"), [(2 * s + x, 2 * t + 1 - x) for s, t in onward for x in range(2)]
    )
    handed = kernel_call(
        gate_kernel,
        shape(gate_stream.shape[1:], BF16),
        (x_scalar,),
        (own_long, got_long, gate, tail, gate_taps),
    )
    own_out, other_out = kernel_call(
        project_kernel,
        (shape((rows, n_z * channels), BF16),) * 2,
        (x_scalar,),
        (plane_rows, weight),
        (),
        4 * rows * n_tp * wide * n_z * channels,
    )
    got_out = lax.ppermute(other_out, "xh", swap)
    attended = kernel_call(
        functools.partial(unite_kernel, channels),
        shape(handed.shape, BF16),
        (x_scalar,),
        (own_out, got_out),
    )
    return (handed[None], attended[None])


def solution(mesh):
    n_sec, n_seq, n_tp = (mesh.shape[name] for name in ("section", "seq", "tp"))
    finer = Mesh(mesh.devices.reshape(n_sec, n_seq // 2, 2, n_tp), ("section", "z", "xh", "tp"))
    seq = ("z", "xh")
    placed = (
        P("section", seq, "tp"),
        P("section", seq, "tp"),
        P("section", seq, "tp"),
        P("section", None, None, "tp"),
        P("section", "tp", seq, None, None),
        P("section", "tp"),
        P("section", seq, "tp"),
        P("section", seq, "tp"),
        P("section", seq, "tp"),
        P("section", "tp", None, seq),
    )
    return jax.shard_map(
        body,
        mesh=finer,
        in_specs=placed,
        out_specs=(P("section", seq, "tp"), P("section", seq, "tp")),
        check_vma=False,
    )
```

```python
import functools
import math

import jax
import jax.numpy as jnp
import numpy as np
from jax import lax
from jax.experimental import pallas as pl
from jax.experimental.pallas import tpu as pltpu
from jax.sharding import Mesh, PartitionSpec as P

HD = 128
BF16 = jnp.bfloat16
F32 = jnp.float32


def dot(left, right, contract):
    return lax.dot_general(left, right, (contract, ((), ())), preferred_element_type=F32)


def transform_tables(depth, breadth):
    full = 2 * depth
    half = -(-(depth + 1) // 8) * 8
    k = np.arange(depth + 1)
    b = np.arange(breadth)
    one = -2.0 * np.pi * np.outer(k, np.arange(depth)) / full
    first = np.zeros((2 * half, depth))
    first[: depth + 1], first[half : half + depth + 1] = np.cos(one), np.sin(one)
    angle = -2.0 * np.pi * np.outer(k, b) / (full * breadth)
    mid = np.zeros((2, half, breadth))
    mid[0, : depth + 1], mid[1, : depth + 1] = np.cos(angle), np.sin(angle)
    two = -2.0 * np.pi * (np.outer(b, b) % breadth) / breadth
    cos_two, sin_two = np.cos(two), np.sin(two)
    weight = np.where((k == 0) | (k == depth), 1.0, 2.0) / (full * breadth)
    last = np.zeros((depth, 2 * half))
    last[:, : depth + 1] = np.cos(one).T * weight
    last[:, half : half + depth + 1] = np.sin(one).T * weight

    def halves(x):
        high = x.astype(BF16)
        return high, (x - high.astype(np.float64)).astype(BF16)

    first_high, first_low = halves(first)
    last_high, last_low = halves(last)
    return {
        "first_two": np.concatenate([first_high, first_low], axis=1),
        "first_three": np.concatenate([first_high, first_high, first_low], axis=1),
        "mid": mid.astype(np.float32),
        "forward": np.stack(halves(np.block([[cos_two, sin_two], [-sin_two, cos_two]]))),
        "backward": np.stack(halves(np.block([[cos_two, -sin_two], [sin_two, cos_two]]))),
        "last": np.concatenate([last_high, last_high, last_low], axis=1),
    }


def kernel_call(
    kernel,
    out_shape,
    scalars,
    arrays,
    scratch=(),
    flops=0,
    grant=16,
    hbm_in=(),
    hbm_out=(),
    from_hbm=(),
):
    single = not isinstance(out_shape, tuple)
    outs = (out_shape,) if single else out_shape

    def spec(at, hbm):
        return pl.BlockSpec(memory_space=pltpu.HBM if at in hbm else pltpu.VMEM)

    arrays = [
        pltpu.with_memory_space_constraint(jnp.asarray(x), pltpu.HBM) if at in hbm_in + from_hbm else x
        for at, x in enumerate(arrays)
    ]
    in_specs = [pl.BlockSpec(memory_space=pltpu.SMEM)] * len(scalars)
    in_specs += [spec(at, hbm_in) for at in range(len(arrays))]
    out_specs = tuple(spec(at, hbm_out) for at in range(len(outs)))
    moved = sum(x.size * x.dtype.itemsize for x in (*arrays, *outs))
    placed = tuple(
        pltpu.HBM(x.shape, x.dtype) if at in hbm_out else x for at, x in enumerate(outs)
    )
    return pl.pallas_call(
        kernel,
        out_shape=placed[0] if single else placed,
        in_specs=in_specs,
        out_specs=out_specs[0] if single else out_specs,
        scratch_shapes=list(scratch),
        compiler_params=pltpu.CompilerParams(vmem_limit_bytes=grant * 1024 * 1024),
        cost_estimate=pl.CostEstimate(flops=flops, bytes_accessed=moved, transcendentals=0),
    )(*scalars, *arrays)


def pack_kernel(x_ref, first_ref, value_ref, taps_ref, query_ref, key_ref, value_head_ref, weight_ref, rows_ref, own_ref, other_ref):
    n_tp = rows_ref.shape[0]
    rows = query_ref.shape[0]
    part = rows // n_tp
    for at, ref in enumerate((query_ref, key_ref, value_head_ref)):
        rows_ref[:, at * part : (at + 1) * part, :] = ref[...].reshape(n_tp, part, -1)
    rows_ref[:, 3 * part :, :] = weight_ref[...]
    n_z, _, lanes = own_ref.shape
    per = 2 * n_z * lanes // first_ref.shape[1]
    channels = lanes // per
    low = x_ref[0] == 0
    lane = lax.broadcasted_iota(jnp.int32, (1, lanes), 1)
    for group in range(2 * n_z // per):
        span = slice(group * lanes, (group + 1) * lanes)
        shorts, edges = [], []
        for ref, which in ((first_ref, 0), (value_ref, 2)):
            x = ref[:, span].astype(F32)
            shorts.append(
                taps_ref[3 * which, :, span] * x
                + taps_ref[3 * which + 1, :, span] * pltpu.roll(x, 1, 0)
                + taps_ref[3 * which + 2, :, span] * pltpu.roll(x, 2, 0)
            )
            edges += [x[:2], x[rows - 2 :]]
        turned = (shorts[0] * shorts[1]).T
        edges = jnp.concatenate(edges, axis=0)
        moved = [pltpu.roll(edges, d * channels, 1) if d else edges for d in range(per)]
        for at in range(per // 2):
            z_at = group * per // 2 + at
            blocks = []
            for x_at in range(2):
                j = 2 * at + x_at
                lines = [turned[j * channels : (j + 1) * channels]]
                for row in range(2):
                    line = moved[(per - 1 - j) % per][row * per + per - 1 : (row + 1) * per]
                    for kind in reversed(range(per - 1)):
                        piece = moved[(kind - j) % per][row * per + kind : row * per + kind + 1]
                        line = jnp.where(lane < (kind + 1) * channels, piece, line)
                    lines.append(line)
                lines.append(jnp.zeros((6, lanes), F32))
                blocks.append(jnp.concatenate(lines, axis=0))
            own_ref[z_at] = jnp.where(low, blocks[0], blocks[1]).astype(BF16)
            other_ref[z_at] = jnp.where(low, blocks[1], blocks[0]).astype(BF16)


def repack_kernel(
    x_ref, rows_ref, own_hbm, got_ref, out_hbm, weight_hbm, own_ref, out_ref, sems
):
    n_tp, height, wide = rows_ref.shape
    channels = weight_hbm.shape[1]
    size = height - channels
    heads = wide // HD
    fetch = pltpu.make_async_copy(own_hbm, own_ref, sems.at[0])
    fetch.start()
    pass_on = pltpu.make_async_copy(rows_ref.at[:, size:, :], weight_hbm, sems.at[1])
    pass_on.start()
    for at in range(n_tp):
        for head in range(heads):
            block = rows_ref[at, :size, head * HD : (head + 1) * HD]
            out_ref[at * heads + head, :size, :] = block
    low = x_ref[0] == 0
    fetch.wait()
    row = lax.broadcasted_iota(jnp.int32, (1, 8, HD), 1)
    middle = out_ref.shape[0] // 2
    stores = []
    for at in range(2):
        span = pl.ds(at * middle, middle)
        own, got = own_ref[span].astype(F32), got_ref[span].astype(F32)
        even, odd = jnp.where(low, own, got), jnp.where(low, got, own)
        out_ref[span, size : size + channels, :] = even[:, :channels].astype(BF16)
        out_ref[span, size + channels : size + 2 * channels, :] = odd[:, :channels].astype(BF16)
        lines = jnp.where(row < 2, even[:, channels:], pltpu.roll(odd[:, channels:], 2, 1))
        out_ref[span, size + 2 * channels :, :] = lines.astype(BF16)
        stores.append(pltpu.make_async_copy(out_ref.at[span], out_hbm.at[span], sems.at[2 + at]))
        stores[at].start()
    for store in stores:
        store.wait()
    pass_on.wait()


def split_kernel(part, mixed_ref, pairs_hbm, query_ref, block_ref, sems):
    n_z = mixed_ref.shape[0]
    for at in range(2):
        block = mixed_ref[:, (at + 1) * part : (at + 2) * part, :]
        block_ref[at] = block.reshape(n_z * part, HD)
    stores = [
        pltpu.make_async_copy(block_ref, pairs_hbm.at[to], sems.at[to])
        for to in range(pairs_hbm.shape[0])
    ]
    for store in stores:
        store.start()
    query_ref[...] = mixed_ref[:, :part, :].reshape(n_z * part, HD)
    for store in stores:
        store.wait()


def split_two(x):
    high = x.astype(BF16)
    return high, (x - high.astype(F32)).astype(BF16)


def dot_three(x, high, low):
    x_high, x_low = split_two(x)
    rows = ((1,), (0,))
    return dot(x_high, high, rows) + (dot(x_low, high, rows) + dot(x_high, low, rows))


def turn(real, imag, cos_mid, sin_mid, turned_ref, span):
    breadth = cos_mid.shape[1]
    turned_ref[span, :breadth] = real * cos_mid - imag * sin_mid
    turned_ref[span, breadth:] = real * sin_mid + imag * cos_mid


def spectrum_kernel(filter_ref, first_ref, mid_ref, forward_ref, out_ref, turned_ref):
    channels = filter_ref.shape[0]
    half = mid_ref.shape[1]
    cos_mid, sin_mid = mid_ref[0], mid_ref[1]
    for at in range(channels):
        high, low = split_two(filter_ref[at])
        both = dot(first_ref[...], jnp.concatenate([high, low, high], axis=0), ((1,), (0,)))
        turn(both[:half], both[half:], cos_mid, sin_mid, turned_ref, slice(at * half, (at + 1) * half))
    step = 4 * half
    for at in range(channels // 4):
        span = slice(at * step, (at + 1) * step)
        out_ref[span, :] = dot_three(turned_ref[span, :], forward_ref[0], forward_ref[1])


def signal_kernel(
    start,
    mixed_ref,
    taps_ref,
    spectrum_ref,
    first_ref,
    mid_ref,
    forward_ref,
    out_ref,
    signal_ref,
    done_ref,
    turned_ref,
):
    done_ref[...] = jnp.zeros_like(done_ref)
    rows, half = mid_ref.shape[2], mid_ref.shape[1]
    channels = out_ref.shape[0] // half
    n_seq = signal_ref.shape[0] // channels
    count = n_seq * 4
    edges = mixed_ref[:, start + 2 * channels :, :].astype(F32).reshape(count, rows).T
    zeroth, first, last_but_one, last = (
        edges[kind * channels : (kind + 1) * channels] for kind in range(4)
    )
    lane = lax.broadcasted_iota(jnp.int32, (channels, count), 1)

    def before(x):
        moved = jnp.where(lane % 8 < 2, pltpu.roll(x, 6, 1), pltpu.roll(x, 2, 1))
        return jnp.where(lane < 2, 0.0, moved)

    is_first = lane % 2 == 0
    tap = [jnp.where(is_first, taps_ref[:, i : i + 1], taps_ref[:, 6 + i : 7 + i]) for i in range(3)]
    zero = tap[0] * zeroth + tap[1] * before(last) + tap[2] * before(last_but_one)
    one = tap[0] * first + tap[1] * zeroth + tap[2] * before(last)
    zero = zero * pltpu.roll(zero, count - 1, 1)
    one = one * pltpu.roll(one, count - 1, 1)
    made = jnp.where(is_first, zero, pltpu.roll(one, 1, 1)).astype(BF16).astype(F32)
    column = lax.broadcasted_iota(jnp.int32, (channels, rows), 1)
    for at in range(n_seq):
        lane_at = at // 2 * 8 + at % 2 * 2
        turned = pltpu.roll(made, count - lane_at, 1) if at else made
        begin = start + at % 2 * channels
        block = mixed_ref[at // 2, begin : begin + channels, :].astype(F32)
        signal_ref[at * channels : (at + 1) * channels, :] = jnp.where(
            column < 2, turned[:, :rows], block
        )
    cos_mid, sin_mid = mid_ref[0], mid_ref[1]
    for at in range(channels):
        signal = signal_ref[pl.ds(at, n_seq, stride=channels), :].astype(BF16)
        both = dot(first_ref[...], jnp.concatenate([signal, signal], axis=0), ((1,), (0,)))
        turn(both[:half], both[half:], cos_mid, sin_mid, turned_ref, slice(at * half, (at + 1) * half))
    step = 4 * half
    for group in range(channels // 4):
        span = slice(group * step, (group + 1) * step)
        mine = dot_three(turned_ref[span, :], forward_ref[0], forward_ref[1])
        real, imag = mine[:, :rows], mine[:, rows:]
        other_real, other_imag = spectrum_ref[span, :rows], spectrum_ref[span, rows:]
        out_ref[span, :rows] = real * other_real - imag * other_imag
        out_ref[span, rows:] = real * other_imag + imag * other_real


def convolve_kernel(
    gain_ref, joined_ref, signal_ref, mid_ref, backward_ref, last_ref, out_ref, long_ref
):
    n_seq, channels, rows = out_ref.shape
    half = mid_ref.shape[1]
    cos_mid, sin_mid = mid_ref[0], mid_ref[1]
    step = 4 * half
    for group in range(channels // 4):
        span = slice(group * step, (group + 1) * step)
        mid = dot_three(joined_ref[span, :], backward_ref[0], backward_ref[1])
        for at in range(4):
            real, imag = (mid[at * half : (at + 1) * half, c * rows : (c + 1) * rows] for c in (0, 1))
            back = jnp.concatenate(
                [real * cos_mid + imag * sin_mid, imag * cos_mid - real * sin_mid], axis=0
            )
            high, low = split_two(back)
            out = dot(last_ref[...], jnp.concatenate([high, low, high], axis=0), ((1,), (0,)))
            channel = group * 4 + at
            strided = pl.ds(channel, n_seq, stride=channels)
            long_ref[strided, :] = out + gain_ref[channel] * signal_ref[strided, :]
    out_ref[...] = long_ref[...].astype(BF16).reshape(n_seq, channels, rows)


def attend(delta, query_ref, pairs_ref, tile, few, rows):
    size = 128
    query = query_ref[tile * size : (tile + 1) * size, :]
    row = lax.broadcasted_iota(jnp.int32, (size, size), 0)
    column = lax.broadcasted_iota(jnp.int32, (size, size), 1)
    q_pos = row // few * rows + row % few
    k_pos = column // few * rows + column % few
    parts = []
    for at in range(pairs_ref.shape[0]):
        allowed = k_pos + (at * few + delta) <= q_pos
        for start, stop in ((0, tile * size), (tile * size, (tile + 1) * size)):
            if start == stop:
                continue
            keys = pairs_ref[at, 0, start:stop, :]
            scores = dot(query, keys, ((1,), (1,))) * (1.0 / math.sqrt(HD))
            if start == tile * size:
                parts.append((jnp.where(allowed, scores, -1e30), allowed, at, start, stop))
            else:
                parts.append((scores, None, at, start, stop))
    highest = parts[0][0].max(axis=1, keepdims=True)
    for part in parts[1:]:
        highest = jnp.maximum(highest, part[0].max(axis=1, keepdims=True))
    totals = jnp.zeros((size, 1), F32)
    weighted = jnp.zeros((size, HD), F32)
    for scores, allowed, at, start, stop in parts:
        probs = jnp.exp(scores - highest)
        if allowed is not None:
            probs = jnp.where(allowed, probs, 0.0)
        totals = totals + probs.sum(axis=1, keepdims=True)
        values = pairs_ref[at, 1, start:stop, :]
        weighted = weighted + dot(probs.astype(BF16), values, ((1,), (0,)))
    some = totals > 0.0
    totals = jnp.maximum(totals, 1e-30)
    return weighted / totals, jnp.where(some, highest + jnp.log(totals), -1e30)


def other_kernel(rows, few, delta_ref, query_ref, pairs_ref, done_ref, out_ref, log_ref):
    own_rows = query_ref.shape[0]
    log_ref[...] = jnp.zeros_like(log_ref)
    for tile in range(own_rows // 128):
        out, log = attend(delta_ref[0], query_ref, pairs_ref, tile, few, rows)
        out_ref[tile * 128 : (tile + 1) * 128, :] = out.astype(BF16)
        line = jnp.broadcast_to(log, (128, 128)).T[:8]
        first = line.astype(BF16).astype(F32)
        second = (line - first).astype(BF16).astype(F32)
        third = line - first - second
        for at, term in enumerate((first, second, third)):
            log_ref[at * 8 + tile : at * 8 + tile + 1, :] = term[:1]
    out_ref[own_rows:, :] = log_ref[...].astype(BF16)


def own_kernel(rows, few, delta_ref, query_ref, pairs_ref, out_ref, log_ref):
    for tile in range(query_ref.shape[0] // 128):
        span = slice(tile * 128, (tile + 1) * 128)
        out, log = attend(delta_ref[0], query_ref, pairs_ref, tile, few, rows)
        out_ref[span, :] = out
        log_ref[span, :] = jnp.broadcast_to(log, (128, 128))


def merge_kernel(own_ref, log_ref, got_ref, long_ref, out_ref):
    own_rows = own_ref.shape[0]
    few = own_rows // out_ref.shape[0]
    per = 128 // few
    logs = got_ref[own_rows:, :].astype(F32)
    for tile in range(own_rows // 128):
        span = slice(tile * 128, (tile + 1) * 128)
        log = log_ref[span, :]
        line = logs[tile : tile + 1] + logs[8 + tile : 9 + tile] + logs[16 + tile : 17 + tile]
        got_log = jnp.broadcast_to(line, (128, 128)).T
        highest = jnp.maximum(log, got_log)
        own_share, got_share = jnp.exp(log - highest), jnp.exp(got_log - highest)
        merged = own_ref[span, :] * own_share + got_ref[span, :].astype(F32) * got_share
        merged = (merged / (own_share + got_share)).astype(BF16).reshape(per, few, HD)
        out_ref[tile * per : (tile + 1) * per, :few, :] = merged
    out_ref[:, few:, :] = long_ref[...]


def rows_kernel(
    x_ref, back_ref, rows_hbm, own_hbm, other_hbm, rows_ref, own_ref, other_ref, sems
):
    part = rows_ref.shape[0]
    channels = own_ref.shape[1]
    count = rows_hbm.shape[0]
    for head in range(back_ref.shape[0]):
        rows_ref[:, head * HD : (head + 1) * HD] = back_ref[head, :part, :]
    stores = [pltpu.make_async_copy(rows_ref, rows_hbm.at[to], sems.at[to]) for to in range(count)]
    for store in stores:
        store.start()
    low = x_ref[0] == 0
    even = back_ref[:, part : part + channels, :].astype(F32)
    odd = back_ref[:, part + channels :, :].astype(F32)
    own_ref[...] = jnp.where(low, even, odd).astype(BF16)
    other_ref[...] = jnp.where(low, odd, even).astype(BF16)
    stores += [
        pltpu.make_async_copy(own_ref, own_hbm, sems.at[count]),
        pltpu.make_async_copy(other_ref, other_hbm, sems.at[count + 1]),
    ]
    for store in stores[count:]:
        store.start()
    for store in stores:
        store.wait()


def gate_kernel(x_ref, own_ref, got_ref, gate_ref, tail_ref, taps_ref, out_ref):
    rows = gate_ref.shape[0]
    lanes = 128
    channels = own_ref.shape[1]
    per = lanes // channels
    row = lax.broadcasted_iota(jnp.int32, (rows, lanes), 0)
    low = x_ref[0] == 0
    for group in range(gate_ref.shape[1] // lanes):
        span = slice(group * lanes, (group + 1) * lanes)
        x = gate_ref[:, span].astype(F32)
        tail = tail_ref[:, span].astype(F32)
        one = jnp.where(row == 0, tail[1:2], pltpu.roll(x, 1, 0))
        two = jnp.where(row == 0, tail[0:1], jnp.where(row == 1, tail[1:2], pltpu.roll(x, 2, 0)))
        short = taps_ref[0:1, span] * x + taps_ref[1:2, span] * one + taps_ref[2:3, span] * two
        blocks = []
        for at in range(per // 2):
            own = own_ref[group * per // 2 + at].astype(F32)
            got = got_ref[group * per // 2 + at].astype(F32)
            blocks += [jnp.where(low, own, got), jnp.where(low, got, own)]
        out_ref[:, span] = (short * jnp.concatenate(blocks, axis=0).T).astype(BF16)


def project_kernel(x_ref, rows_ref, weight_ref, own_ref, other_ref):
    half = own_ref.shape[0]
    n_z, n_tp, channels, wide = weight_ref.shape
    part = rows_ref.shape[1]
    whole = rows_ref[...].reshape(2 * half, n_tp * wide)
    out = jnp.zeros((2 * half, n_z * channels), F32)
    for at in range(n_tp):
        block = weight_ref[:, at].reshape(n_z * channels, wide)
        out = out + dot(whole[:, at * wide : (at + 1) * wide], block, ((1,), (1,)))
    low = x_ref[0] == 0
    own_ref[...] = jnp.where(low, out[:half], out[half:]).astype(BF16)
    other_ref[...] = jnp.where(low, out[half:], out[:half]).astype(BF16)


def unite_kernel(channels, x_ref, own_ref, got_ref, out_ref):
    rows, lanes = own_ref.shape[0], 128
    low = x_ref[0] == 0
    lane = lax.broadcasted_iota(jnp.int32, (rows, lanes), 1)
    for group in range(out_ref.shape[1] // lanes):
        span = slice(group // 2 * lanes, (group // 2 + 1) * lanes)
        start = group % 2 * 2 * channels
        own, got = own_ref[:, span].astype(F32), got_ref[:, span].astype(F32)
        even, odd = jnp.where(low, own, got), jnp.where(low, got, own)

        def moved(x, by):
            by = by % lanes
            return pltpu.roll(x, by, 1) if by else x

        left = jnp.where(lane < channels, moved(even, -start), moved(odd, channels - start))
        right = jnp.where(
            lane < 3 * channels, moved(even, channels - start), moved(odd, 2 * channels - start)
        )
        out_ref[:, group * lanes : (group + 1) * lanes] = jnp.where(
            lane < 2 * channels, left, right
        ).astype(BF16)


def body(
    first_stream,
    gate_stream,
    value_stream,
    short_taps,
    long_filter,
    skip_gain,
    queries,
    attn_keys,
    attn_values,
    out_weight,
):
    seq = ("z", "xh")
    n_z, n_x, n_tp = lax.axis_size("z"), lax.axis_size("xh"), lax.axis_size("tp")
    n_seq, n_plane = n_z * n_x, n_x * n_tp
    seq_at = lax.axis_index(seq)
    x_at = lax.axis_index("xh")
    x_scalar = x_at.astype(jnp.int32).reshape(1)
    rows = queries.shape[1]
    wide = queries.shape[2]
    channels = long_filter.shape[3]
    part = rows // n_tp
    own_rows = n_z * part
    taps = short_taps[0]
    swap = [(0, 1), (1, 0)]
    shape = jax.ShapeDtypeStruct

    sent_rows, own, other = kernel_call(
        pack_kernel,
        (
            shape((n_tp, 3 * part + channels, wide), BF16),
            shape((n_z, channels + 8, rows), BF16),
            shape((n_z, channels + 8, rows), BF16),
        ),
        (x_scalar,),
        (
            first_stream[0],
            value_stream[0],
            short_taps.reshape(9, 1, -1),
            queries[0],
            attn_keys[0],
            attn_values[0],
            out_weight[0].transpose(1, 2, 0),
        ),
        grant=56,
    )
    got = lax.ppermute(other, "xh", swap)
    got_rows = lax.all_to_all(sent_rows, "tp", 0, 0)
    packed, weight = kernel_call(
        repack_kernel,
        (
            shape((n_z, 3 * part + 2 * channels + 8, HD), BF16),
            shape((n_tp, channels, wide), BF16),
        ),
        (x_scalar,),
        (got_rows, own, got),
        (
            pltpu.VMEM((n_z, channels + 8, rows), BF16),
            pltpu.VMEM((n_z, 3 * part + 2 * channels + 8, HD), BF16),
            pltpu.SemaphoreType.DMA((4,)),
        ),
        hbm_in=(1,),
        hbm_out=(0, 1),
    )
    mixed = lax.all_to_all(packed, "z", 0, 0)
    weight = lax.all_gather(weight, "z")

    n_sec = lax.axis_size("section")
    onward = [(i, (i + 1) % n_sec) for i in range(n_sec)]
    gate = lax.ppermute(gate_stream[0], "section", onward)
    gate_taps = lax.ppermute(taps[1], "section", onward)
    tail = lax.ppermute(
        gate_stream[0, -2:],
        ("section",) + seq,
        [(s * n_seq + i, t * n_seq + i + 1) for s, t in onward for i in range(n_seq - 1)],
    )
    local_taps = lax.dynamic_slice_in_dim(taps, seq_at * channels, channels, 2)
    local_taps = local_taps.reshape(9, channels).T
    tables = transform_tables(n_seq, rows)
    half = tables["mid"].shape[1]
    kernel_spec = kernel_call(
        spectrum_kernel,
        shape((channels * half, 2 * rows), F32),
        (),
        (
            long_filter[0, 0, 0].reshape(channels, n_seq, rows),
            tables["first_three"],
            tables["mid"],
            tables["forward"],
        ),
        (pltpu.VMEM((channels * half, 2 * rows), F32),),
        from_hbm=(1, 2, 3),
    )
    mixed, gate, gate_taps, tail, local_taps, kernel_spec = lax.optimization_barrier(
        (mixed, gate, gate_taps, tail, local_taps, kernel_spec)
    )

    sent_pairs, query = kernel_call(
        functools.partial(split_kernel, part),
        (shape((n_tp, 2, own_rows, HD), BF16), shape((own_rows, HD), BF16)),
        (),
        (mixed,),
        (pltpu.VMEM((2, own_rows, HD), BF16), pltpu.SemaphoreType.DMA((n_tp,))),
        hbm_out=(0,),
    )
    other_query = lax.ppermute(query, "xh", swap)
    pairs = lax.all_to_all(sent_pairs, "tp", 0, 0)

    gain = lax.dynamic_slice_in_dim(skip_gain[0], seq_at * channels, channels, 0)
    joined, signal, done = kernel_call(
        functools.partial(signal_kernel, 3 * part),
        (
            shape((channels * half, 2 * rows), F32),
            shape((n_seq * channels, rows), F32),
            shape((8, rows), F32),
        ),
        (),
        (
            mixed,
            local_taps,
            kernel_spec,
            tables["first_two"],
            tables["mid"],
            tables["forward"],
        ),
        (pltpu.VMEM((channels * half, 2 * rows), F32),),
        from_hbm=(3, 4, 5),
    )
    work = 2 * own_rows * n_tp * own_rows * HD
    own_delta = -lax.axis_index("tp") * part
    other_delta = (2 * x_at - 1) * rows + own_delta
    sent = kernel_call(
        functools.partial(other_kernel, n_x * rows, part),
        shape((own_rows + 32, HD), BF16),
        (other_delta.astype(jnp.int32).reshape(1),),
        (other_query, pairs, done),
        (pltpu.VMEM((32, HD), F32),),
        work,
    )
    got = lax.ppermute(sent, "xh", swap)
    query, sent = lax.optimization_barrier((query, sent))
    own_out, own_log = kernel_call(
        functools.partial(own_kernel, n_x * rows, part),
        (shape((own_rows, HD), F32),) * 2,
        (own_delta.astype(jnp.int32).reshape(1),),
        (query, pairs),
        (),
        work,
    )
    long_out = kernel_call(
        convolve_kernel,
        shape((n_seq, channels, rows), BF16),
        (gain,),
        (joined, signal, tables["mid"], tables["backward"], tables["last"]),
        (pltpu.VMEM((n_seq * channels, rows), F32),),
        from_hbm=(2, 3, 4),
    )
    returned = kernel_call(
        merge_kernel,
        shape((n_z, part + n_x * channels, HD), BF16),
        (),
        (own_out, own_log, got, long_out.reshape(n_z, n_x * channels, rows)),
    )
    back = lax.all_to_all(returned, "z", 0, 0)
    back, weight = lax.optimization_barrier((back, weight))

    plane_rows, own_long, other_long = kernel_call(
        rows_kernel,
        (
            shape((n_plane, part, n_z * HD), BF16),
            shape((n_z, channels, rows), BF16),
            shape((n_z, channels, rows), BF16),
        ),
        (x_scalar,),
        (back,),
        (
            pltpu.VMEM((part, n_z * HD), BF16),
            pltpu.VMEM((n_z, channels, rows), BF16),
            pltpu.VMEM((n_z, channels, rows), BF16),
            pltpu.SemaphoreType.DMA((n_plane + 2,)),
        ),
        hbm_out=(0, 1, 2),
    )
    plane_rows = lax.all_to_all(plane_rows, ("xh", "tp"), 0, 0)
    own_long = lax.ppermute(own_long, "section", onward)
    got_long = lax.ppermute(
        other_long, ("section", "xh"), [(2 * s + x, 2 * t + 1 - x) for s, t in onward for x in range(2)]
    )
    handed = kernel_call(
        gate_kernel,
        shape(gate_stream.shape[1:], BF16),
        (x_scalar,),
        (own_long, got_long, gate, tail, gate_taps),
    )
    own_out, other_out = kernel_call(
        project_kernel,
        (shape((rows, n_z * channels), BF16),) * 2,
        (x_scalar,),
        (plane_rows, weight),
        (),
        4 * rows * n_tp * wide * n_z * channels,
    )
    got_out = lax.ppermute(other_out, "xh", swap)
    attended = kernel_call(
        functools.partial(unite_kernel, channels),
        shape(handed.shape, BF16),
        (x_scalar,),
        (own_out, got_out),
    )
    return (handed[None], attended[None])


def solution(mesh):
    n_sec, n_seq, n_tp = (mesh.shape[name] for name in ("section", "seq", "tp"))
    finer = Mesh(mesh.devices.reshape(n_sec, n_seq // 2, 2, n_tp), ("section", "z", "xh", "tp"))
    seq = ("z", "xh")
    placed = (
        P("section", seq, "tp"),
        P("section", seq, "tp"),
        P("section", seq, "tp"),
        P("section", None, None, "tp"),
        P("section", "tp", seq, None, None),
        P("section", "tp"),
        P("section", seq, "tp"),
        P("section", seq, "tp"),
        P("section", seq, "tp"),
        P("section", "tp", None, seq),
    )
    return jax.shard_map(
        body,
        mesh=finer,
        in_specs=placed,
        out_specs=(P("section", seq, "tp"), P("section", seq, "tp")),
        check_vma=False,
    )
```
